32 devices in a mesh: segment: 2 (over y), dp: 16 (over z, x, core).
Axes of the slice: x: 2, y: 2, z: 4, core: 2. Of those that a mesh axis runs over, the one named last changes fastest.
Arguments:
- segment_input: bfloat16 [2, 32, 384, 768], P('segment', 'dp'), may hold values from -16 to 16
- image_extent: int32 [32, 3], P('dp'), may hold values from 0 to 24, as said below
- norm1_gain: bfloat16 [2, 768], P('segment', 'dp'), may hold values from 0.5 to 1.5
- norm1_bias: bfloat16 [2, 768], P('segment', 'dp'), may hold values from -3 to 3
- norm2_gain: bfloat16 [2, 768], P('segment', 'dp'), may hold values from 0.5 to 1.5
- norm2_bias: bfloat16 [2, 768], P('segment', 'dp'), may hold values from -3 to 3
- qkv_weight: bfloat16 [2, 768, 2304], P('segment', 'dp'), may hold values from -0.21875 to 0.21875
- out_weight: bfloat16 [2, 768, 768], P('segment', 'dp'), may hold values from -1.75 to 1.75
- up_weight: bfloat16 [2, 768, 3072], P('segment', 'dp'), may hold values from -0.21875 to 0.21875
- down_weight: bfloat16 [2, 3072, 768], P('segment', 'dp'), may hold values from -0.109375 to 0.109375
- code_maps: bfloat16 [2, 768, 18], P('segment', 'dp'), may hold values from -1.5 to 1.5
Outputs:
- segment_output: float32 [2, 32, 384, 768], P('segment', 'dp')
- rms_stats: float32 [2, 3], P('segment')
- norm1_gain_grad: float32 [2, 768], P('segment', 'dp')
- norm1_bias_grad: float32 [2, 768], P('segment', 'dp')
- norm2_gain_grad: float32 [2, 768], P('segment', 'dp')
- norm2_bias_grad: float32 [2, 768], P('segment', 'dp')
- qkv_weight_grad: float32 [2, 768, 2304], P('segment', 'dp')
- out_weight_grad: float32 [2, 768, 768], P('segment', 'dp')
- up_weight_grad: float32 [2, 768, 3072], P('segment', 'dp')
- down_weight_grad: float32 [2, 3072, 768], P('segment', 'dp')
- code_maps_grad: float32 [2, 768, 18], P('segment', 'dp')
The draws below stay inside these ranges and needn't reach their ends.
Inputs may be any that keep to these rules, and one draw needn't show every extreme that they name: `image_extent`: column 0 is the bucket: 0 for a grid of 16 rows of 24 patches, 1 for 24 rows of 16; patch p lies in row p // (row length) and column p % (row length). Columns 1 and 2 count the valid rows and columns, from a quarter of the bucket's (at least 1) up to all of them.
All inputs are finite; a program needn't handle non-finite values.
Results may differ from the reference program's by a relative error of at most 0.025.
Values may be sent and summed in bfloat16 or wider, within the bound.
A program may use at most 256 MiB of HBM per device.

```python
import math
import jax
import jax.numpy as jnp
from jax import lax

D = 768
HEADS = 12
FF = 3072
CODE_BITS = 18
GH = 16
GW = 24
IMAGES = 32


def draw_segment_input(key, part):
    key = jax.random.fold_in(key, 11)
    position = jnp.arange(IMAGES, dtype=jnp.float32) / max(IMAGES - 1, 1)
    shape_all = (2, IMAGES, GH * GW, D)
    base_draw = jnp.clip(jax.random.normal(key, shape_all, jnp.float32), -5.0, 5.0)
    image_scale = 3.0 ** position
    return (base_draw * image_scale[None, :, None, None]).astype(jnp.bfloat16)


def draw_image_extent(key, part):
    key = jax.random.fold_in(key, 23)
    keys_all = jax.random.split(key, 3)
    bucket = jax.random.randint(keys_all[0], (IMAGES,), 0, 2)
    heights = jnp.where(bucket == 0, GH, GW)
    widths = jnp.where(bucket == 0, GW, GH)
    row_count = jax.random.randint(keys_all[1], (IMAGES,), jnp.maximum(heights // 4, 1), heights + 1)
    col_count = jax.random.randint(keys_all[2], (IMAGES,), jnp.maximum(widths // 4, 1), widths + 1)
    return jnp.stack([bucket, row_count, col_count], 1).astype(jnp.int32)


def levels(own_key, shape, cuts, smallest, high):
    def one(dim, blocks):
        steps = jax.random.uniform(jax.random.fold_in(jax.random.fold_in(own_key, 6), dim), (blocks,), jnp.float32, smallest / len(cuts), high / len(cuts))
        return jnp.repeat(jnp.exp(steps), shape[dim] // blocks).reshape((-1,) + (1,) * (len(shape) - dim - 1))

    level = one(*cuts[0])
    for cut in cuts[1:]:
        level = level * one(*cut)
    return level


def noise(key, shape, deviation, reach, cuts=(), held_as=jnp.bfloat16):
    array = deviation * jax.random.normal(key, shape, jnp.float32)
    if cuts:
        array = array * levels(key, shape, cuts, -0.22, 0.18)
    return jnp.clip(array, -reach, reach).astype(held_as)


def setup_inputs(seed: int = 0) -> dict:
    arg_keys = jax.random.split(jax.random.key(seed), 12)
    segment_input = draw_segment_input(jax.random.fold_in(arg_keys[11], 71), 0)
    image_extent = draw_image_extent(jax.random.fold_in(arg_keys[11], 71), 0)
    norm1_gain = jnp.clip(1.0 + 0.1 * jax.random.normal(arg_keys[2], (2, D), jnp.float32), 0.5, 1.5).astype(jnp.bfloat16)
    norm1_bias = noise(arg_keys[3], (2, D), 0.3, 3.0, ((0, 2), (1, 16)))
    norm2_gain = jnp.clip(1.0 + 0.1 * jax.random.normal(arg_keys[4], (2, D), jnp.float32), 0.5, 1.5).astype(jnp.bfloat16)
    norm2_bias = noise(arg_keys[5], (2, D), 0.3, 3.0, ((0, 2), (1, 16)))
    qkv_weight = noise(arg_keys[6], (2, D, 3 * D), D ** -0.5, 0.21875, ((0, 2), (1, 16)))
    out_weight = noise(arg_keys[7], (2, D, D), (D // 64) ** -0.5, 1.75, ((0, 2), (1, 16)))
    up_weight = noise(arg_keys[8], (2, D, FF), D ** -0.5, 0.21875, ((0, 2), (1, 16)))
    down_weight = noise(arg_keys[9], (2, FF, D), FF ** -0.5, 0.109375, ((0, 2), (1, 16)))
    code_maps = noise(arg_keys[10], (2, D, CODE_BITS), CODE_BITS ** -0.5, 1.5, ((0, 2), (1, 16)))
    return dict(segment_input=segment_input, image_extent=image_extent, norm1_gain=norm1_gain, norm1_bias=norm1_bias, norm2_gain=norm2_gain, norm2_bias=norm2_bias, qkv_weight=qkv_weight, out_weight=out_weight, up_weight=up_weight, down_weight=down_weight, code_maps=code_maps)


@jax.custom_vjp
def low(v):
    return lax.optimization_barrier(v.astype(jnp.bfloat16)).astype(jnp.float32)

@jax.custom_vjp
def low_back(v):
    return v

def low_keep(v):
    return (low(v), None)

def low_pass(kept, grad):
    return (grad,)

def back_keep(v):
    return (v, None)

def back_low(kept, grad):
    return (low(grad),)
low.defvjp(low_keep, low_pass)
low_back.defvjp(back_keep, back_low)
norm_eps = 1e-06

def matmul_hi(left, right):
    return jnp.dot(left, right, precision=lax.Precision.HIGHEST)

def layer_norm(values_in, norm_gain, norm_bias):
    centered = values_in - lax.optimization_barrier(jnp.mean(values_in, -1, keepdims=True))
    return centered * lax.rsqrt(lax.optimization_barrier(jnp.mean(centered * centered, -1, keepdims=True)) + norm_eps) * norm_gain + norm_bias

def extent_mask(extent, patches):
    bucket = extent[:, 0:1]
    line_len = jnp.where(bucket == 0, GW, GH)
    position = jnp.arange(patches, dtype=jnp.int32)[None, :]
    inside = (position // line_len < extent[:, 1:2]) & (position % line_len < extent[:, 2:3])
    return inside.astype(jnp.float32)

def vit_block(block_in, patch_keep_mask, weights):
    gain_one, bias_one, gain_two, bias_two, w_qkv, w_out, w_up, w_down = weights
    image_count, patches = patch_keep_mask.shape
    features = block_in.shape[1]
    head_dim = features // HEADS
    normed = low(layer_norm(block_in, gain_one, bias_one))
    qkv_full = matmul_hi(normed, w_qkv)

    def split_part(section):
        return low_back(low(section)).reshape(image_count, patches, HEADS, head_dim)
    queries = split_part(qkv_full[:, :features])
    key_rows = split_part(qkv_full[:, features:2 * features])
    values = split_part(qkv_full[:, 2 * features:])
    scores = jnp.einsum('iqhe,ikhe->ihqk', queries, key_rows, precision=lax.Precision.HIGHEST) * (1.0 / math.sqrt(head_dim))
    scores = low_back(scores)
    scores = jnp.where(patch_keep_mask[:, None, None, :] > 0, scores, -1e+30)
    row_max = lax.optimization_barrier(jnp.max(scores, -1, keepdims=True))
    exponent = jnp.exp(scores - row_max)
    probs_low = low(exponent / lax.optimization_barrier(jnp.sum(exponent, -1, keepdims=True)))
    mixed_heads = jnp.einsum('ihqk,ikhe->iqhe', probs_low, values, precision=lax.Precision.HIGHEST)
    mixed_heads = low_back(low(mixed_heads.reshape(image_count * patches, features)))
    attn_out = low_back(matmul_hi(mixed_heads, w_out))
    middle = block_in + attn_out
    normed_two = low(layer_norm(middle, gain_two, bias_two))
    pre_act = low_back(matmul_hi(normed_two, w_up))
    activation = low(jax.nn.gelu(pre_act, approximate=False))
    mlp_out = low_back(matmul_hi(activation, w_down))
    return (middle + mlp_out, attn_out, mlp_out)

def soft_code(code_pre):
    direction = code_pre * lax.rsqrt(lax.optimization_barrier(jnp.sum(code_pre * code_pre, -1, keepdims=True)) + 1.0)
    return jnp.tanh(2.0 * math.sqrt(code_pre.shape[-1]) * direction)

def reference(segment_input, image_extent, norm1_gain, norm1_bias, norm2_gain, norm2_bias, qkv_weight, out_weight, up_weight, down_weight, code_maps):
    images = segment_input.shape[1]
    patches = segment_input.shape[2]
    features = segment_input.shape[3]
    group_size = 8
    group_count = images // group_size
    validity = extent_mask(image_extent, patches)
    inputs = segment_input[0].astype(jnp.float32).reshape(group_count, group_size, patches, features)
    masks_all = validity.reshape(group_count, group_size, patches)
    cotangent = segment_input[1].astype(jnp.float32)
    params = tuple((member.astype(jnp.float32) for member in (norm1_gain, norm1_bias, norm2_gain, norm2_bias, qkv_weight, out_weight, up_weight, down_weight, code_maps)))

    def forward(inputs, params):
        gain_one, bias_one, gain_two, bias_two, w_qkv, w_out, w_up, w_down, maps_all = params

        def segment_weights(slot_index):
            return (gain_one[slot_index], bias_one[slot_index], gain_two[slot_index], bias_two[slot_index], w_qkv[slot_index], w_out[slot_index], w_up[slot_index], w_down[slot_index])

        def group_step(energies, pair_item):
            image_rows, patch_keep_mask = pair_item
            flat_rows = image_rows.reshape(-1, features)
            enc_out, enc_attn, enc_mlp = vit_block(flat_rows, patch_keep_mask, segment_weights(0))
            code_pre = low_back(matmul_hi(low(enc_out), maps_all[0]))
            codes_low = low_back(low(soft_code(code_pre)))
            lifted = low_back(matmul_hi(codes_low, maps_all[1].T))
            dec_out, dec_attn, dec_mlp = vit_block(lifted, patch_keep_mask, segment_weights(1))
            row_mask = patch_keep_mask.reshape(-1)

            def energy(tensor):
                return jnp.sum(row_mask * lax.optimization_barrier(jnp.sum(tensor * tensor, -1)))
            fresh = jnp.stack([energy(enc_out), energy(enc_attn), energy(enc_mlp), energy(dec_out), energy(dec_attn), energy(dec_mlp)])
            return (energies + fresh, dec_out.reshape(image_rows.shape))
        energies, decoded = lax.scan(jax.checkpoint(group_step), jnp.zeros((6,), jnp.float32), (inputs, masks_all))
        return (decoded.reshape(images, patches, features), energies)
    (decoded, energies), pullback = jax.vjp(forward, inputs, params)
    grad_in, grads = pullback((cotangent, jnp.zeros_like(energies)))
    valid_count = jnp.sum(validity)
    rms_stats = jnp.sqrt(energies / (valid_count * features)).reshape(2, 3)
    segment_output = jnp.stack([grad_in.reshape(images, patches, features), decoded])
    return (segment_output, rms_stats, grads[0], grads[1], grads[2], grads[3], grads[4], grads[5], grads[6], grads[7], grads[8])
```

```python
from functools import partial
import math

import jax
import jax.numpy as jnp
from jax import lax
from jax.experimental import pallas as pl
from jax.experimental.pallas import tpu as pltpu
from jax.sharding import PartitionSpec as P

HEADS = 12
CODE_BITS = 18
GH = 16
GW = 24
MB = 2


norm_eps = 1e-06


def passed_along(array, axis, by):
    length = lax.axis_size(axis)
    pairs = [(i, i + by) for i in range(length) if 0 <= i + by < length]
    return lax.ppermute(array, axis, pairs)


def layer_norm(values_in, norm_gain, norm_bias):
    centered = values_in - jnp.mean(values_in, -1, keepdims=True)
    return (
        centered
        * lax.rsqrt(jnp.mean(centered * centered, -1, keepdims=True) + norm_eps)
        * norm_gain
        + norm_bias
    )


def extent_mask(extent, patches):
    bucket = extent[:, 0:1]
    line_len = jnp.where(bucket == 0, GW, GH)
    position = jnp.arange(patches, dtype=jnp.int32)[None, :]
    inside = (position // line_len < extent[:, 1:2]) & (position % line_len < extent[:, 2:3])
    return inside.astype(jnp.float32)


def soft_code(code_pre):
    direction = code_pre * lax.rsqrt(jnp.sum(code_pre * code_pre, 0, keepdims=True) + 1.0)
    return jnp.tanh(2.0 * math.sqrt(code_pre.shape[0]) * direction)


def energy(tensor, row_mask):
    return jnp.sum(row_mask * jnp.sum(tensor * tensor, -1))


def split_heads(qkv_low, image_count, patches):
    head_dim = qkv_low.shape[1] // (3 * HEADS)
    joined = qkv_low.reshape(image_count, patches, 3, HEADS, head_dim)
    return (joined[:, :, 0], joined[:, :, 1], joined[:, :, 2])


def masked_scores(queries, key_rows, patch_keep_mask):
    head_dim = queries.shape[-1]
    scores = jnp.einsum(
        "iqhe,ikhe->ihqk", queries, key_rows, preferred_element_type=jnp.float32
    ) * (1.0 / math.sqrt(head_dim))
    return jnp.where(patch_keep_mask[:, None, None, :] > 0, scores, -1e30)


def attention_forward(block_in, patch_keep_mask, weights):
    norm_gain, norm_bias, w_qkv, w_out = weights
    image_count, patches = patch_keep_mask.shape
    features = block_in.shape[1]
    normed = layer_norm(block_in, norm_gain, norm_bias).astype(jnp.bfloat16)
    qkv_low = jnp.dot(normed, w_qkv, preferred_element_type=jnp.float32).astype(jnp.bfloat16)
    queries, key_rows, values = split_heads(qkv_low, image_count, patches)
    scores = masked_scores(queries, key_rows, patch_keep_mask)
    row_max = jnp.max(scores, -1, keepdims=True)
    exponent = jnp.exp(scores - row_max)
    row_sum = jnp.sum(exponent, -1, keepdims=True)
    probs_low = (exponent / row_sum).astype(jnp.bfloat16)
    log_total = (row_max + jnp.log(row_sum))[..., 0]
    mixed_heads = jnp.einsum(
        "ihqk,ikhe->iqhe", probs_low, values, preferred_element_type=jnp.float32
    )
    mixed_heads = mixed_heads.reshape(image_count * patches, features).astype(jnp.bfloat16)
    attn_out = jnp.dot(mixed_heads, w_out, preferred_element_type=jnp.float32)
    return (attn_out, qkv_low, log_total, mixed_heads)


def mlp_forward(middle, weights):
    norm_gain, norm_bias, w_up, w_down = weights
    normed = layer_norm(middle, norm_gain, norm_bias).astype(jnp.bfloat16)
    pre_act = jnp.dot(normed, w_up, preferred_element_type=jnp.float32)
    activation = jax.nn.gelu(pre_act, approximate=False).astype(jnp.bfloat16)
    return (jnp.dot(activation, w_down, preferred_element_type=jnp.float32), pre_act)


def block_forward(block_in, patch_keep_mask, attn_weights, mlp_weights):
    attn_out, qkv_low, log_total, mixed_heads = attention_forward(
        block_in, patch_keep_mask, attn_weights
    )
    middle = block_in + attn_out
    mlp_out, pre_act = mlp_forward(middle, mlp_weights)
    block_result = middle + mlp_out
    row_mask = patch_keep_mask.reshape(-1)
    energies = jnp.stack(
        [energy(block_result, row_mask), energy(attn_out, row_mask), energy(mlp_out, row_mask)]
    )
    return (block_result, (block_in, qkv_low, log_total, mixed_heads, middle, pre_act), energies)


def blank_forward(block_in, patch_keep_mask, attn_weights, mlp_weights):
    row_total, features = block_in.shape
    image_count, patches = patch_keep_mask.shape
    hidden = mlp_weights[2].shape[1]
    zero_rows = jnp.zeros((row_total, features), jnp.float32)
    saved_tensor = (
        zero_rows,
        jnp.zeros((row_total, 3 * features), jnp.bfloat16),
        jnp.zeros((image_count, HEADS, patches), jnp.float32),
        jnp.zeros((row_total, features), jnp.bfloat16),
        zero_rows,
        jnp.zeros((row_total, hidden), jnp.float32),
    )
    return (zero_rows, saved_tensor, jnp.zeros((3,), jnp.float32))


def mlp_backward(grad_out, middle, pre_act, weights):
    norm_gain, norm_bias, w_up, w_down = weights
    grad_low = grad_out.astype(jnp.bfloat16)
    activation, gelu_back = jax.vjp(partial(jax.nn.gelu, approximate=False), pre_act)
    grad_act = jnp.einsum("rd,fd->rf", grad_low, w_down, preferred_element_type=jnp.float32)
    grad_pre = gelu_back(grad_act)[0].astype(jnp.bfloat16)
    normed, norm_back = jax.vjp(
        layer_norm, middle, norm_gain.astype(jnp.float32), norm_bias.astype(jnp.float32)
    )
    grad_normed = jnp.einsum("rf,df->rd", grad_pre, w_up, preferred_element_type=jnp.float32)
    grad_part, gain_grad, bias_grad = norm_back(grad_normed)
    operands = (activation.astype(jnp.bfloat16), grad_low, normed.astype(jnp.bfloat16), grad_pre)
    return (grad_out + grad_part, (gain_grad, bias_grad), operands)


def blank_mlp(grad_out, middle, pre_act, weights):
    row_total, features = grad_out.shape
    hidden = weights[2].shape[1]
    operands = (
        jnp.zeros((row_total, hidden), jnp.bfloat16),
        jnp.zeros((row_total, features), jnp.bfloat16),
        jnp.zeros((row_total, features), jnp.bfloat16),
        jnp.zeros((row_total, hidden), jnp.bfloat16),
    )
    return (
        jnp.zeros_like(grad_out),
        (jnp.zeros((features,), jnp.float32), jnp.zeros((features,), jnp.float32)),
        operands,
    )


def mlp_weight_grads(operands):
    activation_low, grad_low, normed_low, grad_pre = operands
    up_grad = jnp.einsum("rd,rf->df", normed_low, grad_pre, preferred_element_type=jnp.float32)
    down_grad = jnp.einsum(
        "rf,rd->fd", activation_low, grad_low, preferred_element_type=jnp.float32
    )
    return (up_grad, down_grad)


def attention_backward(
    grad_mid, block_in, qkv_low, log_total, mixed_heads, patch_keep_mask, weights
):
    norm_gain, norm_bias, w_qkv, w_out = weights
    image_count, patches = patch_keep_mask.shape
    features = block_in.shape[1]
    head_dim = features // HEADS
    grad_low = grad_mid.astype(jnp.bfloat16)
    grad_mixed = jnp.einsum(
        "re,de->rd", grad_low, w_out, preferred_element_type=jnp.float32
    ).astype(jnp.bfloat16)
    grad_mixed = grad_mixed.reshape(image_count, patches, HEADS, head_dim)
    queries, key_rows, values = split_heads(qkv_low, image_count, patches)
    scores = masked_scores(queries, key_rows, patch_keep_mask)
    probs = jnp.exp(scores - log_total[..., None])
    grad_probs = jnp.einsum(
        "iqhe,ikhe->ihqk", grad_mixed, values, preferred_element_type=jnp.float32
    )
    grad_values = jnp.einsum(
        "ihqk,iqhe->ikhe",
        probs.astype(jnp.bfloat16),
        grad_mixed,
        preferred_element_type=jnp.float32,
    )
    inner = jnp.sum(probs * grad_probs, -1, keepdims=True)
    grad_scores = (probs * (grad_probs - inner)).astype(jnp.bfloat16)
    score_scale = 1.0 / math.sqrt(head_dim)
    grad_queries = (
        jnp.einsum("ihqk,ikhe->iqhe", grad_scores, key_rows, preferred_element_type=jnp.float32)
        * score_scale
    )
    grad_keys = (
        jnp.einsum("ihqk,iqhe->ikhe", grad_scores, queries, preferred_element_type=jnp.float32)
        * score_scale
    )
    grad_qkv = (
        jnp.stack([grad_queries, grad_keys, grad_values], 2)
        .astype(jnp.bfloat16)
        .reshape(image_count * patches, 3 * features)
    )
    normed, norm_back = jax.vjp(
        layer_norm, block_in, norm_gain.astype(jnp.float32), norm_bias.astype(jnp.float32)
    )
    grad_normed = jnp.einsum("re,de->rd", grad_qkv, w_qkv, preferred_element_type=jnp.float32)
    grad_part, gain_grad, bias_grad = norm_back(grad_normed)
    operands = (mixed_heads, grad_low, normed.astype(jnp.bfloat16), grad_qkv)
    return (grad_mid + grad_part, (gain_grad, bias_grad), operands)


def blank_attention(grad_mid, block_in, qkv_low, log_total, mixed_heads, patch_keep_mask, weights):
    row_total, features = grad_mid.shape
    operands = (
        jnp.zeros((row_total, features), jnp.bfloat16),
        jnp.zeros((row_total, features), jnp.bfloat16),
        jnp.zeros((row_total, features), jnp.bfloat16),
        jnp.zeros((row_total, 3 * features), jnp.bfloat16),
    )
    return (
        jnp.zeros_like(grad_mid),
        (jnp.zeros((features,), jnp.float32), jnp.zeros((features,), jnp.float32)),
        operands,
    )


def attention_weight_grads(operands):
    mixed_heads, grad_low, normed_low, grad_qkv = operands
    qkv_grad = jnp.einsum("rd,re->de", normed_low, grad_qkv, preferred_element_type=jnp.float32)
    out_grad = jnp.einsum("rd,re->de", mixed_heads, grad_low, preferred_element_type=jnp.float32)
    return (qkv_grad, out_grad)


def join_rows(pieces):
    return jax.tree.map(lambda *members: jnp.concatenate(members, 0), *pieces)


MESH_ID = pl.DeviceIdType.MESH


def ring_place():
    seg = lax.axis_index("segment")
    here = lax.axis_index("dp")
    core = lax.rem(here, 2)
    col = lax.rem(here // 2, 2)
    row = here // 4
    return seg, here, core, col, row


def meet_neighbours(seg, here, core, col, row, rows):
    barrier = pltpu.get_barrier_semaphore()

    def greet(other):
        pl.semaphore_signal(barrier, inc=1, device_id=(seg, other), device_id_type=MESH_ID)

    greet(here + 1 - 2 * core)
    greet(here + 2 - 4 * col)

    @pl.when(row > 0)
    def _():
        greet(here - 4)

    @pl.when(row < rows - 1)
    def _():
        greet(here + 4)

    has_two = jnp.logical_and(row > 0, row < rows - 1)
    pl.semaphore_wait(barrier, jnp.where(has_two, 4, 3))


def gather_body(rows, *refs):
    n_arr = 3
    shards = refs[:n_arr]
    fulls = refs[n_arr : 2 * n_arr]
    own_sem, send_sem, recv_sem = refs[2 * n_arr :]
    seg, here, core, col, row = ring_place()
    sib = here + 1 - 2 * core
    xn = here + 2 - 4 * col

    def block(arr, src):
        height = shards[arr].shape[0]
        return fulls[arr].at[pl.ds(pl.multiple_of(src * height, height), height)]

    def copy(arr, src, first, slot, to):
        return pltpu.make_async_remote_copy(
            src_ref=shards[arr] if first else block(arr, src),
            dst_ref=block(arr, src),
            send_sem=send_sem.at[arr, slot],
            recv_sem=recv_sem.at[arr, src],
            device_id=(seg, to),
            device_id_type=MESH_ID,
        )

    def arrive(arr, src):
        copy(arr, src, False, 0, sib).wait_recv()

    def index(src_row, src_col):
        return (src_row * 2 + src_col) * 2 + core

    def to_sib(arr, src_row, src_col, first=False):
        return copy(arr, index(src_row, src_col), first, 3 * rows + src_row * 2 + src_col, sib)

    def to_x(arr, src_row, first=False):
        return copy(arr, index(src_row, col), first, 2 * rows + src_row, xn)

    def to_up(arr, src_row, first=False):
        return copy(arr, index(src_row, col), first, src_row, here + 4)

    def to_down(arr, src_row, first=False):
        return copy(arr, index(src_row, col), first, rows + src_row, here - 4)

    def own_copy(arr):
        return pltpu.make_async_copy(shards[arr], block(arr, here), own_sem.at[arr])

    def own(arr):
        @pl.when(row < rows - 1)
        def _():
            to_up(arr, row, True).start()

        @pl.when(row > 0)
        def _():
            to_down(arr, row, True).start()

        to_x(arr, row, True).start()
        to_sib(arr, row, col, True).start()
        own_copy(arr).start()

    def away(arr, dist):
        @pl.when(row - dist >= 0)
        def _():
            src_row = row - dist
            arrive(arr, index(src_row, col))

            @pl.when(row < rows - 1)
            def _():
                to_up(arr, src_row).start()

            to_x(arr, src_row).start()
            to_sib(arr, src_row, col).start()

        @pl.when(row + dist < rows)
        def _():
            src_row = row + dist
            arrive(arr, index(src_row, col))

            @pl.when(row > 0)
            def _():
                to_down(arr, src_row).start()

            to_x(arr, src_row).start()
            to_sib(arr, src_row, col).start()

    def across(arr):
        def at(src_row):
            arrive(arr, index(src_row, 1 - col))
            to_sib(arr, src_row, 1 - col).start()

        at(row)
        for dist in range(1, rows):
            pl.when(row - dist >= 0)(lambda: at(row - dist))
            pl.when(row + dist < rows)(lambda: at(row + dist))

    meet_neighbours(seg, here, core, col, row, rows)
    for arr in range(n_arr):
        own(arr)
        if arr > 0:
            away(arr - 1, rows - 1)
        away(arr, 1)
        if arr > 0:
            across(arr - 1)
        for dist in range(2, rows - 1):
            away(arr, dist)
    away(n_arr - 1, rows - 1)
    across(n_arr - 1)
    for arr in range(n_arr):
        own_copy(arr).wait()

        @pl.loop(0, 2 * rows)
        def _(i):
            copy(arr, 2 * i + 1 - core, False, 0, sib).wait_recv()
            copy(arr, 2 * i + core, False, 3 * rows + i, sib).wait_send()

        @pl.loop(0, rows)
        def _(i):
            to_x(arr, i).wait_send()

            @pl.when(jnp.logical_and(i <= row, row < rows - 1))
            def _():
                to_up(arr, i).wait_send()

            @pl.when(jnp.logical_and(i >= row, row > 0))
            def _():
                to_down(arr, i).wait_send()


def gather_blocks(shards):
    count = lax.axis_size("dp")
    rows = count // 4
    any_spec = pl.BlockSpec(memory_space=pl.ANY)
    return pl.pallas_call(
        partial(gather_body, rows),
        out_shape=tuple(
            jax.ShapeDtypeStruct((count * s.shape[0], s.shape[1]), s.dtype) for s in shards
        ),
        in_specs=[any_spec] * 3,
        out_specs=(any_spec,) * 3,
        scratch_shapes=[
            pltpu.SemaphoreType.DMA((3,)),
            pltpu.SemaphoreType.DMA((3, 5 * rows)),
            pltpu.SemaphoreType.DMA((3, 4 * rows)),
        ],
        compiler_params=pltpu.CompilerParams(collective_id=1, has_side_effects=True),
        name="gather_weights",
    )(*shards)


def scatter_body(rows, *refs):
    n_arr = 3
    parts = refs[:n_arr]
    outs = refs[n_arr : 2 * n_arr]
    own, sibs, xsend, xrecv, zsend, zrecv = [
        refs[(2 + i) * n_arr : (3 + i) * n_arr] for i in range(6)
    ]
    own_sem, sib_ssem, sib_rsem, x_ssem, x_rsem, z_ssem, z_rsem = refs[8 * n_arr :]
    seg, here, core, col, row = ring_place()
    sib = here + 1 - 2 * core
    xn = here + 2 - 4 * col

    def block(arr, dst):
        height = outs[arr].shape[0]
        return parts[arr].at[pl.ds(pl.multiple_of(dst * height, height), height)]

    def remote(src, dst, ssem, rsem, to):
        return pltpu.make_async_remote_copy(
            src_ref=src,
            dst_ref=dst,
            send_sem=ssem,
            recv_sem=rsem,
            device_id=(seg, to),
            device_id_type=MESH_ID,
        )

    def own_copy(arr, place):
        return pltpu.make_async_copy(
            block(arr, 2 * place + core), own[arr].at[place], own_sem.at[arr, place]
        )

    def sib_copy(arr, place):
        return remote(
            block(arr, 2 * place + 1 - core),
            sibs[arr].at[place],
            sib_ssem.at[arr, place],
            sib_rsem.at[arr, place],
            sib,
        )

    def x_copy(arr, dst_row):
        return remote(
            xsend[arr].at[dst_row],
            xrecv[arr].at[dst_row],
            x_ssem.at[arr, dst_row],
            x_rsem.at[arr, dst_row],
            xn,
        )

    def z_copy(arr, way, dst_row):
        return remote(
            zsend[arr].at[dst_row],
            zrecv[arr].at[way, dst_row],
            z_ssem.at[arr, dst_row],
            z_rsem.at[arr, way, dst_row],
            here + 4 - 8 * way,
        )

    def each_far(body):
        @pl.loop(0, 2 * (rows - 1))
        def _(i):
            way = lax.rem(i, 2)
            dst_row = row + (1 - 2 * way) * (rows - 1 - i // 2)
            pl.when(jnp.logical_and(dst_row >= 0, dst_row < rows))(lambda: body(way, dst_row))

    def start_pairs(arr):
        def go(dst_row, at_col):
            sib_copy(arr, 2 * dst_row + at_col).start()
            own_copy(arr, 2 * dst_row + at_col).start()

        each_far(lambda way, dst_row: go(dst_row, 1 - col))
        go(row, 1 - col)
        each_far(lambda way, dst_row: go(dst_row, col))
        go(row, col)

    def pair_sum(arr, place):
        sib_copy(arr, place).wait_recv()
        own_copy(arr, place).wait()
        return own[arr][place].astype(jnp.float32) + sibs[arr][place].astype(jnp.float32)

    def x_stage(arr):
        def go(dst_row):
            xsend[arr][dst_row] = pair_sum(arr, 2 * dst_row + 1 - col).astype(jnp.bfloat16)
            x_copy(arr, dst_row).start()

        each_far(lambda way, dst_row: go(dst_row))
        go(row)

    def column_sum(arr, dst_row):
        x_copy(arr, dst_row).wait_recv()
        return pair_sum(arr, 2 * dst_row + col) + xrecv[arr][dst_row].astype(jnp.float32)

    def z_stage(arr):
        def go(way, dst_row):
            behind = row - 1 + 2 * way

            @pl.when(jnp.logical_and(behind >= 0, behind < rows))
            def _():
                z_copy(arr, way, dst_row).wait_recv()

            total = column_sum(arr, dst_row) + zrecv[arr][way, dst_row].astype(jnp.float32)
            zsend[arr][dst_row] = total.astype(jnp.bfloat16)
            z_copy(arr, way, dst_row).start()

        each_far(go)

        @pl.when(row > 0)
        def _():
            z_copy(arr, 0, row).wait_recv()

        @pl.when(row < rows - 1)
        def _():
            z_copy(arr, 1, row).wait_recv()

        outs[arr][...] = (
            column_sum(arr, row)
            + zrecv[arr][0, row].astype(jnp.float32)
            + zrecv[arr][1, row].astype(jnp.float32)
        )

    meet_neighbours(seg, here, core, col, row, rows)
    for arr in range(n_arr):
        start_pairs(arr)

    def clear(way):
        for arr in range(n_arr):
            zrecv[arr][way] = jnp.zeros(zrecv[arr].shape[1:], jnp.bfloat16)

    pl.when(row == 0)(lambda: clear(0))
    pl.when(row == rows - 1)(lambda: clear(1))
    x_stage(0)
    for arr in range(n_arr):
        if arr + 1 < n_arr:
            x_stage(arr + 1)
        z_stage(arr)
    for arr in range(n_arr):

        @pl.loop(0, 2 * rows)
        def _(i):
            sib_copy(arr, i).wait_send()

        @pl.loop(0, rows)
        def _(i):
            x_copy(arr, i).wait_send()

        each_far(lambda way, dst_row: z_copy(arr, way, dst_row).wait_send())


def scatter_sums(parts):
    count = lax.axis_size("dp")
    rows = count // 4
    any_spec = pl.BlockSpec(memory_space=pl.ANY)
    vmem_spec = pl.BlockSpec(memory_space=pltpu.VMEM)
    shapes = [(p.shape[0] // count, p.shape[1]) for p in parts]

    def buffers(*lead):
        return [pltpu.VMEM(lead + s, jnp.bfloat16) for s in shapes]

    dma = pltpu.SemaphoreType.DMA
    return pl.pallas_call(
        partial(scatter_body, rows),
        out_shape=tuple(jax.ShapeDtypeStruct(s, jnp.float32) for s in shapes),
        in_specs=[any_spec] * 3,
        out_specs=(vmem_spec,) * 3,
        scratch_shapes=buffers(2 * rows)
        + buffers(2 * rows)
        + buffers(rows)
        + buffers(rows)
        + buffers(rows)
        + buffers(2, rows)
        + [
            dma((3, 2 * rows)),
            dma((3, 2 * rows)),
            dma((3, 2 * rows)),
            dma((3, rows)),
            dma((3, rows)),
            dma((3, rows)),
            dma((3, 2, rows)),
        ],
        compiler_params=pltpu.CompilerParams(
            collective_id=2, has_side_effects=True, vmem_limit_bytes=56 << 20
        ),
        name="scatter_sums",
    )(*parts)


def on_device(
    segment_input,
    image_extent,
    norm1_gain,
    norm1_bias,
    norm2_gain,
    norm2_bias,
    qkv_weight,
    out_weight,
    up_weight,
    down_weight,
    code_maps,
):
    segment_no = lax.axis_index("segment")
    is_first = segment_no == 0
    images = segment_input.shape[1]
    patches = segment_input.shape[2]
    features = segment_input.shape[3]
    microbatch_count = MB
    per_micro = images // microbatch_count
    row_total = per_micro * patches
    validity = extent_mask(image_extent, patches)
    own_input = segment_input[0]
    qkv_width = qkv_weight.shape[2]
    small = jnp.concatenate(
        [code_maps[0]]
        + [v[0][:, None] for v in (norm1_gain, norm1_bias, norm2_gain, norm2_bias)],
        axis=1,
    )
    small = jnp.pad(small, ((0, 0), (0, 128 - small.shape[1])))
    shards = (
        jnp.concatenate([qkv_weight[0], out_weight[0], small], axis=1),
        up_weight[0],
        down_weight[0],
    )
    by_kernel = shards[0].shape[0] % 16 == 0
    if by_kernel:
        attn_all, up_all, down_all = gather_blocks(shards)
    else:
        attn_all, up_all, down_all = [lax.all_gather(s, "dp", axis=0, tiled=True) for s in shards]
    small_all = attn_all[:, qkv_width + features :]
    norms = small_all[:, CODE_BITS : CODE_BITS + 4].T
    attn_weights = (
        norms[0],
        norms[1],
        attn_all[:, :qkv_width],
        attn_all[:, qkv_width : qkv_width + features],
        small_all[:, :CODE_BITS],
    )
    mlp_weights = (norms[2], norms[3], up_all, down_all)
    code_in = jnp.zeros((CODE_BITS, row_total), jnp.bfloat16)
    code_grad = jnp.zeros((CODE_BITS, row_total), jnp.bfloat16)
    energies = jnp.zeros((3,), jnp.float32)
    saved_tensors = []
    decoded = []
    pieces = []
    for step_index in range(microbatch_count + 1):
        run_send = step_index < microbatch_count
        run_position = step_index - segment_no
        run_active = (run_position >= 0) & (run_position < microbatch_count)
        run_start_at = jnp.clip(run_position, 0, microbatch_count - 1) * per_micro
        inputs = (
            lax.dynamic_slice_in_dim(own_input, run_start_at, per_micro, 0)
            .reshape(row_total, features)
            .astype(jnp.float32)
        )
        run_patch_keep_mask = lax.dynamic_slice_in_dim(validity, run_start_at, per_micro, 0)
        lifted = jnp.einsum(
            "lr,dl->rd", code_in, attn_weights[4], preferred_element_type=jnp.float32
        )
        block_in = jnp.where(is_first, inputs, lifted)
        run_block_result, run_saved_tensor, part_energy = lax.cond(
            run_active,
            block_forward,
            blank_forward,
            block_in,
            run_patch_keep_mask,
            attn_weights[:4],
            mlp_weights,
        )
        run_code_pre = jnp.einsum(
            "rd,dl->lr",
            run_block_result.astype(jnp.bfloat16),
            attn_weights[4],
            preferred_element_type=jnp.float32,
        )
        codes_out = soft_code(run_code_pre).astype(jnp.bfloat16)
        run_record_item = (run_saved_tensor, code_in, run_patch_keep_mask, run_block_result)
        run_code_next = code_in
        if run_send:
            run_code_next = passed_along(codes_out, "segment", 1)
        record_item, part_energy, code_in = (run_record_item, part_energy, run_code_next)
        energies = energies + part_energy
        saved_tensors.append(record_item)
        decoded.append(record_item[3])
    weight_pair = (attn_weights, mlp_weights)
    attn_use, mlp_use = weight_pair
    small_total = (
        jnp.zeros((features,), jnp.float32),
        jnp.zeros((features,), jnp.float32),
        jnp.zeros((features,), jnp.float32),
        jnp.zeros((features,), jnp.float32),
        jnp.zeros(attn_use[4].shape, jnp.float32),
    )
    sums = (small_total, [], [])
    results = []
    for step_index in range(microbatch_count + 1):
        position = microbatch_count - step_index - segment_no
        run_attn_use, run_mlp_use = weight_pair
        run_small_total, mlp_pieces, attn_pieces = sums
        code_maps_all = run_attn_use[4]
        saved_tensor, applied_code, patch_keep_mask, block_result = saved_tensors[
            microbatch_count - step_index
        ]
        active = (position >= 0) & (position < microbatch_count)
        start_at = jnp.clip(position, 0, microbatch_count - 1) * per_micro
        target = (
            lax.dynamic_slice_in_dim(own_input, start_at, per_micro, 0)
            .reshape(row_total, features)
            .astype(jnp.float32)
        )
        out_low = block_result.astype(jnp.bfloat16)
        code_pre = jnp.einsum(
            "rd,dl->lr", out_low, code_maps_all, preferred_element_type=jnp.float32
        )
        code_value, code_back = jax.vjp(soft_code, code_pre)
        grad_code = code_back(code_grad.astype(jnp.float32))[0].astype(jnp.bfloat16)
        enc_grad = jnp.einsum(
            "lr,dl->rd", grad_code, code_maps_all, preferred_element_type=jnp.float32
        )
        grad_out = jnp.where(is_first, enc_grad, target)
        enc_map = jnp.einsum("rd,lr->dl", out_low, grad_code, preferred_element_type=jnp.float32)
        map_part = jnp.where(is_first & active, enc_map, 0.0)
        grad_mid, mlp_small, mlp_operands = lax.cond(
            active, mlp_backward, blank_mlp, grad_out, saved_tensor[4], saved_tensor[5], run_mlp_use
        )
        mlp_pieces = mlp_pieces + [mlp_operands]
        grad_in, attn_small, attn_operands = lax.cond(
            active,
            attention_backward,
            blank_attention,
            grad_mid,
            saved_tensor[0],
            saved_tensor[1],
            saved_tensor[2],
            saved_tensor[3],
            patch_keep_mask,
            run_attn_use[:4],
        )
        grad_in_low = grad_in.astype(jnp.bfloat16)
        dec_map = jnp.einsum(
            "rd,lr->dl", grad_in_low, applied_code, preferred_element_type=jnp.float32
        )
        map_part = map_part + jnp.where(jnp.logical_not(is_first) & active, dec_map, 0.0)
        code_grad_new = jnp.einsum(
            "rd,dl->lr", grad_in_low, code_maps_all, preferred_element_type=jnp.float32
        ).astype(jnp.bfloat16)
        code_next = code_grad
        if step_index < microbatch_count:
            code_next = passed_along(code_grad_new, "segment", -1)
        attn_pieces = attn_pieces + [attn_operands]
        run_small_total = jax.tree.map(
            jnp.add,
            run_small_total,
            (mlp_small[0], mlp_small[1], attn_small[0], attn_small[1], map_part),
        )
        grad_in, code_grad, sums = (
            grad_in,
            code_next,
            (run_small_total, mlp_pieces, attn_pieces),
        )
        results.append(grad_in)
    for micro_index in range(microbatch_count):
        chosen = jnp.where(
            is_first, results[microbatch_count - micro_index], decoded[micro_index + 1]
        )
        pieces.append(chosen.reshape(per_micro, patches, features))
    small_total, mlp_pieces, attn_pieces = sums
    up_grad, down_grad = mlp_weight_grads(join_rows(mlp_pieces))
    qkv_grad, out_grad = attention_weight_grads(join_rows(attn_pieces))
    small_grad = jnp.concatenate(
        [small_total[4]]
        + [small_total[i][:, None] for i in (2, 3, 0, 1)],
        axis=1,
    )
    small_grad = jnp.pad(small_grad, ((0, 0), (0, 128 - small_grad.shape[1])))
    attn_grad = jnp.concatenate([qkv_grad, out_grad, small_grad], axis=1)
    if by_kernel:
        low_parts = tuple(v.astype(jnp.bfloat16) for v in (down_grad, up_grad, attn_grad))
        down_shard, up_shard, attn_shard = scatter_sums(low_parts)
    else:
        down_shard, up_shard, attn_shard = [
            lax.psum_scatter(v, "dp", scatter_dimension=0, tiled=True)
            for v in (down_grad, up_grad, attn_grad)
        ]
    small_shard = attn_shard[:, qkv_width + features :]
    norm_shards = [small_shard[:, CODE_BITS + i][None] for i in range(4)]
    segment_output = jnp.concatenate(pieces, 0)[None]
    energy_all, valid_all = lax.psum((energies, jnp.sum(validity)), "dp")
    rms_stats = jnp.sqrt(energy_all / (valid_all * features))[None]
    return (
        segment_output,
        rms_stats,
        norm_shards[0],
        norm_shards[1],
        norm_shards[2],
        norm_shards[3],
        attn_shard[:, :qkv_width][None],
        attn_shard[:, qkv_width : qkv_width + features][None],
        up_shard[None],
        down_shard[None],
        small_shard[:, :CODE_BITS][None],
    )


def solution(mesh):
    return jax.shard_map(
        on_device,
        mesh=mesh,
        in_specs=(
            P("segment", "dp", None, None),
            P("dp", None),
            P("segment", "dp"),
            P("segment", "dp"),
            P("segment", "dp"),
            P("segment", "dp"),
            P("segment", "dp", None),
            P("segment", "dp", None),
            P("segment", "dp", None),
            P("segment", "dp", None),
            P("segment", "dp", None),
        ),
        out_specs=(
            P("segment", "dp", None, None),
            P("segment", None),
            P("segment", "dp"),
            P("segment", "dp"),
            P("segment", "dp"),
            P("segment", "dp"),
            P("segment", "dp", None),
            P("segment", "dp", None),
            P("segment", "dp", None),
            P("segment", "dp", None),
            P("segment", "dp", None),
        ),
        check_vma=False,
    )
```

```python
from functools import partial
import math

import jax
import jax.numpy as jnp
from jax import lax
from jax.experimental import pallas as pl
from jax.experimental.pallas import tpu as pltpu
from jax.sharding import PartitionSpec as P

HEADS = 12
CODE_BITS = 18
GH = 16
GW = 24
LOG2E = math.log2(math.e)


norm_eps = 1e-06


def extent_mask(extent, patches):
    bucket = extent[:, 0:1]
    line_len = jnp.where(bucket == 0, GW, GH)
    position = jnp.arange(patches, dtype=jnp.int32)[None, :]
    inside = (position // line_len < extent[:, 1:2]) & (position % line_len < extent[:, 2:3])
    return inside.astype(jnp.float32)


MESH_ID = pl.DeviceIdType.MESH


def ring_place():
    seg = lax.axis_index("segment")
    here = lax.axis_index("dp")
    core = lax.rem(here, 2)
    col = lax.rem(here // 2, 2)
    row = here // 4
    return seg, here, core, col, row


def meet_neighbours(seg, here, core, col, row, rows):
    barrier = pltpu.get_barrier_semaphore()

    def greet(other):
        pl.semaphore_signal(barrier, inc=1, device_id=(seg, other), device_id_type=MESH_ID)

    greet(here + 1 - 2 * core)
    greet(here + 2 - 4 * col)

    @pl.when(row > 0)
    def _():
        greet(here - 4)

    @pl.when(row < rows - 1)
    def _():
        greet(here + 4)

    has_two = jnp.logical_and(row > 0, row < rows - 1)
    pl.semaphore_wait(barrier, jnp.where(has_two, 4, 3))


def gather_body(rows, *refs):
    n_arr = 3
    shards = refs[:n_arr]
    fulls = refs[n_arr : 2 * n_arr]
    own_sem, send_sem, recv_sem = refs[2 * n_arr :]
    seg, here, core, col, row = ring_place()
    sib = here + 1 - 2 * core
    xn = here + 2 - 4 * col

    def block(arr, src):
        height = shards[arr].shape[0]
        return fulls[arr].at[pl.ds(pl.multiple_of(src * height, height), height)]

    def copy(arr, src, first, slot, to):
        return pltpu.make_async_remote_copy(
            src_ref=shards[arr] if first else block(arr, src),
            dst_ref=block(arr, src),
            send_sem=send_sem.at[arr, slot],
            recv_sem=recv_sem.at[arr, src],
            device_id=(seg, to),
            device_id_type=MESH_ID,
        )

    def arrive(arr, src):
        copy(arr, src, False, 0, sib).wait_recv()

    def index(src_row, src_col):
        return (src_row * 2 + src_col) * 2 + core

    def to_sib(arr, src_row, src_col, first=False):
        return copy(arr, index(src_row, src_col), first, 3 * rows + src_row * 2 + src_col, sib)

    def to_x(arr, src_row, first=False):
        return copy(arr, index(src_row, col), first, 2 * rows + src_row, xn)

    def to_up(arr, src_row, first=False):
        return copy(arr, index(src_row, col), first, src_row, here + 4)

    def to_down(arr, src_row, first=False):
        return copy(arr, index(src_row, col), first, rows + src_row, here - 4)

    def own_copy(arr):
        return pltpu.make_async_copy(shards[arr], block(arr, here), own_sem.at[arr])

    def own(arr):
        @pl.when(row < rows - 1)
        def _():
            to_up(arr, row, True).start()

        @pl.when(row > 0)
        def _():
            to_down(arr, row, True).start()

        to_x(arr, row, True).start()
        to_sib(arr, row, col, True).start()
        own_copy(arr).start()

    def away(arr, dist):
        @pl.when(row - dist >= 0)
        def _():
            src_row = row - dist
            arrive(arr, index(src_row, col))

            @pl.when(row < rows - 1)
            def _():
                to_up(arr, src_row).start()

            to_x(arr, src_row).start()
            to_sib(arr, src_row, col).start()

        @pl.when(row + dist < rows)
        def _():
            src_row = row + dist
            arrive(arr, index(src_row, col))

            @pl.when(row > 0)
            def _():
                to_down(arr, src_row).start()

            to_x(arr, src_row).start()
            to_sib(arr, src_row, col).start()

    def across(arr):
        def at(src_row):
            arrive(arr, index(src_row, 1 - col))
            to_sib(arr, src_row, 1 - col).start()

        at(row)
        for dist in range(1, rows):
            pl.when(row - dist >= 0)(lambda: at(row - dist))
            pl.when(row + dist < rows)(lambda: at(row + dist))

    meet_neighbours(seg, here, core, col, row, rows)
    for arr in range(n_arr):
        own(arr)
        if arr > 0:
            away(arr - 1, rows - 1)
        away(arr, 1)
        if arr > 0:
            across(arr - 1)
        for dist in range(2, rows - 1):
            away(arr, dist)
    away(n_arr - 1, rows - 1)
    across(n_arr - 1)
    for arr in range(n_arr):
        own_copy(arr).wait()

        @pl.loop(0, 2 * rows)
        def _(i):
            copy(arr, 2 * i + 1 - core, False, 0, sib).wait_recv()
            copy(arr, 2 * i + core, False, 3 * rows + i, sib).wait_send()

        @pl.loop(0, rows)
        def _(i):
            to_x(arr, i).wait_send()

            @pl.when(jnp.logical_and(i <= row, row < rows - 1))
            def _():
                to_up(arr, i).wait_send()

            @pl.when(jnp.logical_and(i >= row, row > 0))
            def _():
                to_down(arr, i).wait_send()


def gather_blocks(shards):
    count = lax.axis_size("dp")
    rows = count // 4
    any_spec = pl.BlockSpec(memory_space=pl.ANY)
    return pl.pallas_call(
        partial(gather_body, rows),
        out_shape=tuple(
            jax.ShapeDtypeStruct((count * s.shape[0], s.shape[1]), s.dtype) for s in shards
        ),
        in_specs=[any_spec] * 3,
        out_specs=(any_spec,) * 3,
        scratch_shapes=[
            pltpu.SemaphoreType.DMA((3,)),
            pltpu.SemaphoreType.DMA((3, 5 * rows)),
            pltpu.SemaphoreType.DMA((3, 4 * rows)),
        ],
        compiler_params=pltpu.CompilerParams(collective_id=1, has_side_effects=True),
        name="gather_weights",
    )(*shards)


def scatter_body(rows, *refs):
    n_arr = 3
    parts = refs[:n_arr]
    outs = refs[n_arr : 2 * n_arr]
    own, sibs, xsend, xrecv, zsend, zrecv = [
        refs[(2 + i) * n_arr : (3 + i) * n_arr] for i in range(6)
    ]
    own_sem, sib_ssem, sib_rsem, x_ssem, x_rsem, z_ssem, z_rsem = refs[8 * n_arr :]
    seg, here, core, col, row = ring_place()
    sib = here + 1 - 2 * core
    xn = here + 2 - 4 * col

    def block(arr, dst):
        height = outs[arr].shape[0]
        return parts[arr].at[pl.ds(pl.multiple_of(dst * height, height), height)]

    def remote(src, dst, ssem, rsem, to):
        return pltpu.make_async_remote_copy(
            src_ref=src,
            dst_ref=dst,
            send_sem=ssem,
            recv_sem=rsem,
            device_id=(seg, to),
            device_id_type=MESH_ID,
        )

    def own_copy(arr, place):
        return pltpu.make_async_copy(
            block(arr, 2 * place + core), own[arr].at[place], own_sem.at[arr, place]
        )

    def sib_copy(arr, place):
        return remote(
            block(arr, 2 * place + 1 - core),
            sibs[arr].at[place],
            sib_ssem.at[arr, place],
            sib_rsem.at[arr, place],
            sib,
        )

    def x_copy(arr, dst_row):
        return remote(
            xsend[arr].at[dst_row],
            xrecv[arr].at[dst_row],
            x_ssem.at[arr, dst_row],
            x_rsem.at[arr, dst_row],
            xn,
        )

    def z_copy(arr, way, dst_row):
        return remote(
            zsend[arr].at[dst_row],
            zrecv[arr].at[way, dst_row],
            z_ssem.at[arr, dst_row],
            z_rsem.at[arr, way, dst_row],
            here + 4 - 8 * way,
        )

    def each_far(body):
        @pl.loop(0, 2 * (rows - 1))
        def _(i):
            way = lax.rem(i, 2)
            dst_row = row + (1 - 2 * way) * (rows - 1 - i // 2)
            pl.when(jnp.logical_and(dst_row >= 0, dst_row < rows))(lambda: body(way, dst_row))

    def start_pairs(arr):
        def go(dst_row, at_col):
            sib_copy(arr, 2 * dst_row + at_col).start()
            own_copy(arr, 2 * dst_row + at_col).start()

        each_far(lambda way, dst_row: go(dst_row, 1 - col))
        go(row, 1 - col)
        each_far(lambda way, dst_row: go(dst_row, col))
        go(row, col)

    def pair_sum(arr, place):
        sib_copy(arr, place).wait_recv()
        own_copy(arr, place).wait()
        return own[arr][place].astype(jnp.float32) + sibs[arr][place].astype(jnp.float32)

    def x_stage(arr):
        def go(dst_row):
            xsend[arr][dst_row] = pair_sum(arr, 2 * dst_row + 1 - col).astype(jnp.bfloat16)
            x_copy(arr, dst_row).start()

        each_far(lambda way, dst_row: go(dst_row))
        go(row)

    def column_sum(arr, dst_row):
        x_copy(arr, dst_row).wait_recv()
        return pair_sum(arr, 2 * dst_row + col) + xrecv[arr][dst_row].astype(jnp.float32)

    def z_stage(arr):
        def go(way, dst_row):
            behind = row - 1 + 2 * way

            @pl.when(jnp.logical_and(behind >= 0, behind < rows))
            def _():
                z_copy(arr, way, dst_row).wait_recv()

            total = column_sum(arr, dst_row) + zrecv[arr][way, dst_row].astype(jnp.float32)
            zsend[arr][dst_row] = total.astype(jnp.bfloat16)
            z_copy(arr, way, dst_row).start()

        each_far(go)

        @pl.when(row > 0)
        def _():
            z_copy(arr, 0, row).wait_recv()

        @pl.when(row < rows - 1)
        def _():
            z_copy(arr, 1, row).wait_recv()

        outs[arr][...] = (
            column_sum(arr, row)
            + zrecv[arr][0, row].astype(jnp.float32)
            + zrecv[arr][1, row].astype(jnp.float32)
        )

    meet_neighbours(seg, here, core, col, row, rows)
    for arr in range(n_arr):
        start_pairs(arr)

    def clear(way):
        for arr in range(n_arr):
            zrecv[arr][way] = jnp.zeros(zrecv[arr].shape[1:], jnp.bfloat16)

    pl.when(row == 0)(lambda: clear(0))
    pl.when(row == rows - 1)(lambda: clear(1))
    x_stage(0)
    for arr in range(n_arr):
        if arr + 1 < n_arr:
            x_stage(arr + 1)
        z_stage(arr)
    for arr in range(n_arr):

        @pl.loop(0, 2 * rows)
        def _(i):
            sib_copy(arr, i).wait_send()

        @pl.loop(0, rows)
        def _(i):
            x_copy(arr, i).wait_send()

        each_far(lambda way, dst_row: z_copy(arr, way, dst_row).wait_send())


def scatter_sums(parts):
    count = lax.axis_size("dp")
    rows = count // 4
    any_spec = pl.BlockSpec(memory_space=pl.ANY)
    vmem_spec = pl.BlockSpec(memory_space=pltpu.VMEM)
    shapes = [(p.shape[0] // count, p.shape[1]) for p in parts]

    def buffers(*lead):
        return [pltpu.VMEM(lead + s, jnp.bfloat16) for s in shapes]

    dma = pltpu.SemaphoreType.DMA
    return pl.pallas_call(
        partial(scatter_body, rows),
        out_shape=tuple(jax.ShapeDtypeStruct(s, jnp.float32) for s in shapes),
        in_specs=[any_spec] * 3,
        out_specs=(vmem_spec,) * 3,
        scratch_shapes=buffers(2 * rows)
        + buffers(2 * rows)
        + buffers(rows)
        + buffers(rows)
        + buffers(rows)
        + buffers(2, rows)
        + [
            dma((3, 2 * rows)),
            dma((3, 2 * rows)),
            dma((3, 2 * rows)),
            dma((3, rows)),
            dma((3, rows)),
            dma((3, rows)),
            dma((3, 2, rows)),
        ],
        compiler_params=pltpu.CompilerParams(
            collective_id=2, has_side_effects=True, vmem_limit_bytes=56 << 20
        ),
        name="scatter_sums",
    )(*parts)


def dot_nn(left, right):
    return lax.dot_general(left, right, (((1,), (0,)), ((), ())), preferred_element_type=jnp.float32)


def dot_nt(left, right):
    return lax.dot_general(left, right, (((1,), (1,)), ((), ())), preferred_element_type=jnp.float32)


def dot_tn(left, right):
    return lax.dot_general(left, right, (((0,), (0,)), ((), ())), preferred_element_type=jnp.float32)


def low(array):
    return array.astype(jnp.bfloat16)


def wide(array):
    return array.astype(jnp.float32)


def row_sum(array):
    return jnp.sum(array, 0, keepdims=True)


def row_mean(array):
    return jnp.mean(array, -1, keepdims=True)


def blocks_body(*refs):
    (
        attn_hbm, up_hbm, down_hbm, x_ref, mask_ref,
        seg_out, g_down, g_up, g_attn, stats,
        w_attn, w_up, w_down, norms, maps,
        h_buf, out_buf, xhat1, rstd1, xhat2, rstd2, a_s, qkv_s, mixed_s, c_s, act_s, slope_s,
        lse_pack, bias_pack, gm_s, go_s, gmix_s, enc_s, u_s, small_acc, stage, relay_tx, relay_rx,
        w_sem, out_sem, stage_sem, relay_ssem, relay_rsem,
    ) = refs
    seg = lax.axis_index("segment")
    here = lax.axis_index("dp")
    is_enc = seg == 0
    is_dec = seg == 1
    total_rows, features = x_ref.shape
    images = out_buf.shape[0]
    patches = total_rows // images
    hidden = w_up.shape[1]
    head_dim = features // HEADS
    pairs = features // 128
    chunk = features
    code_rows = relay_tx.shape[1]

    def rows(m):
        return pl.ds(pl.multiple_of(m * patches, patches), patches)

    def cols(j, width):
        return pl.ds(pl.multiple_of(j * width, width), width)

    def weight_copies():
        return [
            pltpu.make_async_copy(src, dst, w_sem.at[i])
            for i, (src, dst) in enumerate(
                ((attn_hbm, w_attn), (up_hbm, w_up), (down_hbm, w_down))
            )
        ]

    def relay(m):
        return pltpu.make_async_remote_copy(
            src_ref=relay_tx.at[m],
            dst_ref=relay_rx.at[m],
            send_sem=relay_ssem.at[m],
            recv_sem=relay_rsem.at[m],
            device_id=(1 - seg, here),
            device_id_type=MESH_ID,
        )

    def result(m):
        return pltpu.make_async_copy(out_buf.at[m], seg_out.at[rows(m)], out_sem.at[m])

    def energy(slot, tensor, keep):
        square = row_sum(tensor * tensor * keep)
        total = square[:, :128]
        for j in range(1, pairs):
            total = total + square[:, j * 128 : (j + 1) * 128]
        stats[slot : slot + 1, :] += total

    def code_mask(array):
        return jnp.where(
            lax.broadcasted_iota(jnp.int32, array.shape, 0) < CODE_BITS, array, 0.0
        )

    def normalize(values, xhat, rstd, rs, slot):
        gain, bias = norms[slot : slot + 1, :], norms[slot + 1 : slot + 2, :]
        centered = values - row_mean(values)
        scale = lax.rsqrt(row_mean(centered * centered) + norm_eps)
        hat = centered * scale
        xhat[rs, :] = low(hat)
        rstd[rs, :] = scale
        return low(hat * gain + bias)

    def norm_back(grad, xhat, rstd, rs, norm):
        gain, slot = norms[norm : norm + 1, :], code_rows + norm
        hat = wide(xhat[rs, :])
        small_acc[slot : slot + 1, :] += row_sum(grad * hat)
        small_acc[slot + 1 : slot + 2, :] += row_sum(grad)
        scaled = grad * gain
        return rstd[rs, :] * (scaled - row_mean(scaled) - hat * row_mean(scaled * hat))

    lane = lax.broadcasted_iota(jnp.int32, (1, 128), 1)
    halves = [low(wide(lane < head_dim)), low(wide(lane >= head_dim))]
    in_first = lax.broadcasted_iota(jnp.int32, (patches, 128), 1) < head_dim

    def head_row(head):
        return low(wide(jnp.logical_and(lane < 48, lax.rem(lane, 16) == head)))

    def three_terms(values):
        first = wide(low(values))
        rest = values - first
        second = wide(low(rest))
        third = wide(low(rest - second))
        return jnp.where(lane < 16, first, jnp.where(lane < 32, second, third))

    def forward(m, _):
        rs = rows(m)

        @pl.when(is_enc)
        def _():
            h_buf[...] = wide(x_ref[rs, :])

        @pl.when(is_dec)
        def _():
            relay(m).wait_recv()
            h_buf[...] = dot_tn(relay_rx[m], maps[...])

        keep = jnp.concatenate([mask_ref[rs, :]] * pairs, axis=1)
        bias_pack[rs, :] = low(jnp.where(lane == 48, (1.0 - mask_ref[rs, :]) * -1e30, 0.0))
        a_s[rs, :] = normalize(h_buf[...], xhat1, rstd1, rs, 0)
        for j in range(3):
            part = dot_nn(a_s[rs, :], w_attn[:, j * features : (j + 1) * features])
            if j == 0:
                part = part * (LOG2E / math.sqrt(head_dim))
            qkv_s[rs, j * features : (j + 1) * features] = low(part)
        one_lane = low(wide(jnp.broadcast_to(lane == 48, (patches, 128))))

        def heads(j, lse):
            query = qkv_s[rs, cols(j, 128)]
            key = qkv_s[rs, cols(j + pairs, 128)]
            value = qkv_s[rs, cols(j + 2 * pairs, 128)]
            query = jnp.concatenate([query, one_lane], axis=1)
            outs = []
            for i in range(2):
                keys_one = jnp.concatenate([key * halves[i], bias_pack[rs, :]], axis=1)
                scores = dot_nt(query, keys_one)
                top = jnp.max(scores, -1, keepdims=True)
                weight = low(jnp.exp2(scores - top))
                mixed = dot_nn(weight, value * halves[i] + halves[1 - i])
                count = mixed[:, (1 - i) * head_dim : (1 - i) * head_dim + 1]
                outs.append(mixed * (1.0 / count))
                head = 2 * j + i
                lse = jnp.where(
                    jnp.logical_and(lane < 48, lax.rem(lane, 16) == head),
                    top + jnp.log2(count),
                    lse,
                )
            mixed_s[rs, cols(j, 128)] = low(jnp.where(in_first, outs[0], outs[1]))
            return lse

        lse = lax.fori_loop(0, pairs, heads, jnp.zeros((patches, 128), jnp.float32))
        lse_pack[rs, :] = low(
            jnp.where(lane < 48, three_terms(-lse), jnp.where(lane == 48, 1.0, 0.0))
        )
        attn_out = dot_nn(mixed_s[rs, :], w_attn[:, 3 * features : 4 * features])
        energy(1, attn_out, keep)
        h_buf[...] += attn_out
        c_s[rs, :] = normalize(h_buf[...], xhat2, rstd2, rs, 2)

        def up(j, _):
            pre = dot_nn(c_s[rs, :], w_up[:, cols(j, chunk)])
            phi = 0.5 + 0.5 * lax.erf(pre * math.sqrt(0.5))
            act_s[rs, cols(j, chunk)] = low(pre * phi)
            slope_s[rs, cols(j, chunk)] = low(
                phi + pre * (jnp.exp(-0.5 * pre * pre) * (1.0 / math.sqrt(2.0 * math.pi)))
            )
            return 0

        lax.fori_loop(0, hidden // chunk, up, 0)
        mlp_out = dot_nn(act_s[rs, :], w_down[...])
        energy(2, mlp_out, keep)
        block_out = h_buf[...] + mlp_out
        energy(0, block_out, keep)
        stats[3:4, :] += row_sum(mask_ref[rs, :])

        @pl.when(is_enc)
        def _():
            enc_s[rs, :] = low(block_out)
            code_pre = code_mask(dot_nt(maps[...], enc_s[rs, :]))
            u_s[m] = code_pre
            scale = lax.rsqrt(row_sum(code_pre * code_pre) + 1.0)
            relay_tx[m] = low(jnp.tanh(2.0 * math.sqrt(CODE_BITS) * (code_pre * scale)))
            relay(m).start()

        @pl.when(is_dec)
        def _():
            out_buf[m] = block_out
            result(m).start()

        return 0

    def backward(step, _):
        m = images - 1 - step
        rs = rows(m)

        @pl.when(is_enc)
        def _():
            relay(m).wait_recv()
            code_pre = u_s[m]
            scale = lax.rsqrt(row_sum(code_pre * code_pre) + 1.0)
            unit = code_pre * scale
            factor = 2.0 * math.sqrt(CODE_BITS)
            bent = jnp.tanh(factor * unit)
            g_unit = wide(relay_rx[m]) * (factor * (1.0 - bent * bent))
            g_u = low((g_unit - unit * row_sum(g_unit * unit)) * scale)
            small_acc[0:code_rows, :] += dot_nn(g_u, enc_s[rs, :])
            h_buf[...] = dot_tn(g_u, maps[...])

        @pl.when(is_dec)
        def _():
            h_buf[...] = wide(x_ref[rs, :])

        gm_s[rs, :] = low(h_buf[...])

        def down(j, _):
            g_act = dot_nt(gm_s[rs, :], w_down[cols(j, chunk), :])
            slope_s[rs, cols(j, chunk)] = low(g_act * wide(slope_s[rs, cols(j, chunk)]))
            return 0

        lax.fori_loop(0, hidden // chunk, down, 0)
        g_c = dot_nt(slope_s[rs, :], w_up[...])
        h_buf[...] += norm_back(g_c, xhat2, rstd2, rs, 2)
        go_s[rs, :] = low(h_buf[...])
        gmix_s[...] = low(dot_nt(go_s[rs, :], w_attn[:, 3 * features : 4 * features]))
        product = wide(gmix_s[...]) * wide(mixed_s[rs, :])
        high = low(product)
        head_of = lax.broadcasted_iota(jnp.int32, (features, 128), 0) // head_dim
        lane_of = lax.broadcasted_iota(jnp.int32, (features, 128), 1)
        pick = low(wide(jnp.logical_and(lane_of < 48, lax.rem(lane_of, 16) == head_of)))
        inner = dot_nn(high, pick) + dot_nn(low(product - wide(high)), pick)
        inner_pack = low(three_terms(-inner))

        def heads(j, _):
            at = [cols(j + i * pairs, 128) for i in range(3)]
            query, key, value = [qkv_s[rs, place] for place in at]
            g_mixed = gmix_s[:, cols(j, 128)]
            query_more = jnp.concatenate([query, lse_pack[rs, :]], axis=1)
            g_more = jnp.concatenate([g_mixed, inner_pack], axis=1)
            found = []
            for i in range(2):
                extra = bias_pack[rs, :] + head_row(2 * j + i)
                probs = jnp.exp2(
                    dot_nt(query_more, jnp.concatenate([key * halves[i], extra], axis=1))
                )
                g_probs = dot_nt(g_more, jnp.concatenate([value * halves[i], extra], axis=1))
                probs_low = low(probs)
                g_scores = low(probs * g_probs)
                found.append(
                    (
                        dot_nn(g_scores, key),
                        dot_tn(g_scores, query),
                        dot_tn(probs_low, g_mixed),
                    )
                )
            scales = (1.0 / math.sqrt(head_dim), 1.0 / LOG2E, 1.0)
            for i in range(3):
                joined = jnp.where(in_first, found[0][i], found[1][i])
                qkv_s[rs, at[i]] = low(joined * scales[i])
            return 0

        lax.fori_loop(0, pairs, heads, 0)
        g_a = dot_nt(qkv_s[rs, :], w_attn[:, : 3 * features])
        g_h = h_buf[...] + norm_back(g_a, xhat1, rstd1, rs, 0)

        @pl.when(is_enc)
        def _():
            out_buf[m] = g_h
            result(m).start()

        @pl.when(is_dec)
        def _():
            g_z = low(g_h)
            small_acc[0:code_rows, :] += dot_nn(relay_rx[m], g_z)
            relay_tx[m] = low(code_mask(dot_nt(maps[...], g_z)))
            relay(m).start()

        return 0

    barrier = pltpu.get_barrier_semaphore()
    pl.semaphore_signal(barrier, inc=1, device_id=(1 - seg, here), device_id_type=MESH_ID)
    for copy in weight_copies():
        copy.start()
    stats[...] = jnp.zeros_like(stats)
    small_acc[...] = jnp.zeros_like(small_acc)
    pl.semaphore_wait(barrier, 1)
    for copy in weight_copies():
        copy.wait()
    small = wide(w_attn[:, 4 * features :]).T
    maps[...] = low(code_mask(small[:code_rows]))
    norms[0:4, :] = small[CODE_BITS : CODE_BITS + 4]
    lax.fori_loop(0, images, forward, 0)
    lax.fori_loop(0, images, backward, 0)

    tasks = []
    for j in range(hidden // chunk):
        at = slice(j * chunk, (j + 1) * chunk)
        tasks.append((act_s, at, gm_s, slice(None), g_down.at[at]))
    for j in range(hidden // chunk):
        at = slice(j * chunk, (j + 1) * chunk)
        tasks.append((c_s, slice(None), slope_s, at, g_up.at[:, at]))
    for j in range(3):
        at = slice(j * features, (j + 1) * features)
        tasks.append((a_s, slice(None), qkv_s, at, g_attn.at[:, at]))
    tasks.append(
        (mixed_s, slice(None), go_s, slice(None), g_attn.at[:, 3 * features : 4 * features])
    )
    pending = []
    for i, (left, left_at, right, right_at, place) in enumerate(tasks):
        if i >= 2:
            pending[i - 2].wait()
        stage[i % 2] = low(dot_tn(left[:, left_at], right[:, right_at]))
        pending.append(pltpu.make_async_copy(stage.at[i % 2], place, stage_sem.at[i % 2]))
        pending[i].start()
    pending[-2].wait()
    small_grad = jnp.concatenate(
        [
            small_acc[0:CODE_BITS, :],
            small_acc[code_rows : code_rows + 4, :],
            jnp.zeros((128 - CODE_BITS - 4, features), jnp.float32),
        ],
        axis=0,
    ).T
    stage[len(tasks) % 2, :, :128] = low(small_grad)
    last = pltpu.make_async_copy(
        stage.at[len(tasks) % 2, :, pl.ds(0, 128)],
        g_attn.at[:, pl.ds(4 * features, 128)],
        stage_sem.at[len(tasks) % 2],
    )
    last.start()
    pending[-1].wait()
    last.wait()
    for m in range(images):
        result(m).wait()
        relay(m).wait_send()


def run_blocks(attn_all, up_all, down_all, x, mask):
    images, patches, features = x.shape
    total = images * patches
    hidden = up_all.shape[1]
    code_rows = -(-CODE_BITS // 16) * 16
    bf16, f32 = jnp.bfloat16, jnp.float32
    any_spec = pl.BlockSpec(memory_space=pl.ANY)
    vmem_spec = pl.BlockSpec(memory_space=pltpu.VMEM)
    dma = pltpu.SemaphoreType.DMA
    scratch = [
        (attn_all.shape, bf16), (up_all.shape, bf16), (down_all.shape, bf16),
        ((8, features), f32), ((code_rows, features), bf16),
        ((patches, features), f32), ((images, patches, features), f32),
        ((total, features), bf16), ((total, 1), f32), ((total, features), bf16), ((total, 1), f32),
        ((total, features), bf16), ((total, 3 * features), bf16), ((total, features), bf16),
        ((total, features), bf16), ((total, hidden), bf16), ((total, hidden), bf16),
        ((total, 128), bf16), ((total, 128), bf16),
        ((total, features), bf16), ((total, features), bf16), ((patches, features), bf16),
        ((total, features), bf16), ((images, code_rows, patches), f32),
        ((code_rows + 8, features), f32), ((2, features, features), bf16),
        ((images, code_rows, patches), bf16), ((images, code_rows, patches), bf16),
    ]
    return pl.pallas_call(
        blocks_body,
        out_shape=(
            jax.ShapeDtypeStruct((total, features), f32),
            jax.ShapeDtypeStruct(down_all.shape, bf16),
            jax.ShapeDtypeStruct(up_all.shape, bf16),
            jax.ShapeDtypeStruct(attn_all.shape, bf16),
            jax.ShapeDtypeStruct((8, 128), f32),
        ),
        in_specs=[any_spec] * 3 + [vmem_spec] * 2,
        out_specs=(any_spec,) * 4 + (vmem_spec,),
        scratch_shapes=[pltpu.VMEM(s, t) for s, t in scratch]
        + [dma((3,)), dma((images,)), dma((2,)), dma((images,)), dma((images,))],
        compiler_params=pltpu.CompilerParams(
            collective_id=3, has_side_effects=True, vmem_limit_bytes=60 << 20
        ),
        name="both_blocks",
    )(attn_all, up_all, down_all, x.reshape(total, features), mask)


def on_device(
    segment_input,
    image_extent,
    norm1_gain,
    norm1_bias,
    norm2_gain,
    norm2_bias,
    qkv_weight,
    out_weight,
    up_weight,
    down_weight,
    code_maps,
):
    _, images, patches, features = segment_input.shape
    qkv_width = qkv_weight.shape[2]
    small = jnp.concatenate(
        [code_maps[0]]
        + [v[0][:, None] for v in (norm1_gain, norm1_bias, norm2_gain, norm2_bias)],
        axis=1,
    )
    small = jnp.pad(small, ((0, 0), (0, 128 - small.shape[1])))
    shards = (
        jnp.concatenate([qkv_weight[0], out_weight[0], small], axis=1),
        up_weight[0],
        down_weight[0],
    )
    by_kernel = shards[0].shape[0] % 16 == 0
    if by_kernel:
        attn_all, up_all, down_all = gather_blocks(shards)
    else:
        attn_all, up_all, down_all = [lax.all_gather(s, "dp", axis=0, tiled=True) for s in shards]
    validity = extent_mask(image_extent, patches)
    mask = jnp.broadcast_to(validity.reshape(-1, 1), (images * patches, 128))
    segment_output, down_grad, up_grad, attn_grad, stats = run_blocks(
        attn_all, up_all, down_all, segment_input[0], mask
    )
    parts = (down_grad, up_grad, attn_grad)
    if by_kernel:
        down_shard, up_shard, attn_shard = scatter_sums(parts)
    else:
        down_shard, up_shard, attn_shard = [
            lax.psum_scatter(v.astype(jnp.float32), "dp", scatter_dimension=0, tiled=True)
            for v in parts
        ]
    stats = lax.psum(stats, "dp")
    small_shard = attn_shard[:, qkv_width + features :]
    norm_shards = [small_shard[:, CODE_BITS + i][None] for i in range(4)]
    rms_stats = jnp.sqrt(jnp.sum(stats[:3], 1) / (stats[3, 0] * features))[None]
    return (
        segment_output.reshape(segment_input.shape),
        rms_stats,
        norm_shards[0],
        norm_shards[1],
        norm_shards[2],
        norm_shards[3],
        attn_shard[:, :qkv_width][None],
        attn_shard[:, qkv_width : qkv_width + features][None],
        up_shard[None],
        down_shard[None],
        small_shard[:, :CODE_BITS][None],
    )


def solution(mesh):
    return jax.shard_map(
        on_device,
        mesh=mesh,
        in_specs=(
            P("segment", "dp", None, None),
            P("dp", None),
            P("segment", "dp"),
            P("segment", "dp"),
            P("segment", "dp"),
            P("segment", "dp"),
            P("segment", "dp", None),
            P("segment", "dp", None),
            P("segment", "dp", None),
            P("segment", "dp", None),
            P("segment", "dp", None),
        ),
        out_specs=(
            P("segment", "dp", None, None),
            P("segment", None),
            P("segment", "dp"),
            P("segment", "dp"),
            P("segment", "dp"),
            P("segment", "dp"),
            P("segment", "dp", None),
            P("segment", "dp", None),
            P("segment", "dp", None),
            P("segment", "dp", None),
            P("segment", "dp", None),
        ),
        check_vma=False,
    )
```

```python
from functools import partial
import math

import jax
import jax.numpy as jnp
from jax import lax
from jax.experimental import pallas as pl
from jax.experimental.pallas import tpu as pltpu
from jax.sharding import PartitionSpec as P

HEADS = 12
CODE_BITS = 18
GH = 16
GW = 24
LOG2E = math.log2(math.e)
VMEM_BYTES = 62 << 20


norm_eps = 1e-06


def extent_mask(extent, patches):
    bucket = extent[:, 0:1]
    line_len = jnp.where(bucket == 0, GW, GH)
    position = jnp.arange(patches, dtype=jnp.int32)[None, :]
    inside = (position // line_len < extent[:, 1:2]) & (position % line_len < extent[:, 2:3])
    return inside.astype(jnp.float32)


MESH_ID = pl.DeviceIdType.MESH
ATTN, UP, DOWN = 0, 1, 2


def dot_nn(left, right):
    return lax.dot_general(left, right, (((1,), (0,)), ((), ())), preferred_element_type=jnp.float32)


def dot_nt(left, right):
    return lax.dot_general(left, right, (((1,), (1,)), ((), ())), preferred_element_type=jnp.float32)


def dot_tn(left, right):
    return lax.dot_general(left, right, (((0,), (0,)), ((), ())), preferred_element_type=jnp.float32)


def low(array):
    return array.astype(jnp.bfloat16)


def wide(array):
    return array.astype(jnp.float32)


def row_sum(array):
    return jnp.sum(array, 0, keepdims=True)


def row_mean(array):
    return jnp.mean(array, -1, keepdims=True)


def remote(src, dst, ssem, rsem, to):
    return pltpu.make_async_remote_copy(
        src_ref=src,
        dst_ref=dst,
        send_sem=ssem,
        recv_sem=rsem,
        device_id=to,
        device_id_type=MESH_ID,
    )


class Place:
    def __init__(self, rows):
        self.rows = rows
        self.seg = lax.axis_index("segment")
        self.here = lax.axis_index("dp")
        self.core = lax.rem(self.here, 2)
        self.col = lax.rem(self.here // 2, 2)
        self.row = self.here // 4
        self.sib = (self.seg, self.here + 1 - 2 * self.core)
        self.across = (self.seg, self.here + 2 - 4 * self.col)
        self.up = (self.seg, self.here + 4)
        self.down = (self.seg, self.here - 4)
        self.other = (1 - self.seg, self.here)
        self.has_up = self.row < rows - 1
        self.has_down = self.row > 0

    def meet(self, in_plane):
        barrier = pltpu.get_barrier_semaphore()

        def greet(to):
            pl.semaphore_signal(barrier, inc=1, device_id=to, device_id_type=MESH_ID)

        greet(self.other)
        if not in_plane:
            pl.semaphore_wait(barrier, 1)
            return
        greet(self.sib)
        greet(self.across)
        pl.when(self.has_up)(lambda: greet(self.up))
        pl.when(self.has_down)(lambda: greet(self.down))
        both = jnp.logical_and(self.has_up, self.has_down)
        pl.semaphore_wait(barrier, jnp.where(both, 5, 4))


class Gather:
    def __init__(self, place, weights, heights, send_sem, recv_sem):
        self.at, self.weights, self.heights = place, weights, heights
        self.send_sem, self.recv_sem = send_sem, recv_sem

    def copy(self, arr, src, slot, to):
        height = self.heights[arr]
        block = self.weights[arr].at[pl.ds(pl.multiple_of(src * height, height), height)]
        return remote(block, block, self.send_sem.at[arr, slot], self.recv_sem.at[arr, src], to)

    def index(self, src_row, src_col):
        return (src_row * 2 + src_col) * 2 + self.at.core

    def to_sib(self, arr, src_row, src_col):
        slot = 3 * self.at.rows + src_row * 2 + src_col
        return self.copy(arr, self.index(src_row, src_col), slot, self.at.sib)

    def to_across(self, arr, src_row):
        slot = 2 * self.at.rows + src_row
        return self.copy(arr, self.index(src_row, self.at.col), slot, self.at.across)

    def to_up(self, arr, src_row):
        return self.copy(arr, self.index(src_row, self.at.col), src_row, self.at.up)

    def to_down(self, arr, src_row):
        slot = self.at.rows + src_row
        return self.copy(arr, self.index(src_row, self.at.col), slot, self.at.down)

    def arrive(self, arr, src_row, src_col):
        self.copy(arr, self.index(src_row, src_col), 0, self.at.sib).wait_recv()

    def own(self, arr):
        row = self.at.row
        pl.when(self.at.has_up)(lambda: self.to_up(arr, row).start())
        pl.when(self.at.has_down)(lambda: self.to_down(arr, row).start())
        self.to_across(arr, row).start()
        self.to_sib(arr, row, self.at.col).start()

    def away(self, arr, dist):
        at = self.at

        @pl.when(at.row - dist >= 0)
        def _():
            src = at.row - dist
            self.arrive(arr, src, at.col)
            pl.when(at.has_up)(lambda: self.to_up(arr, src).start())
            self.to_across(arr, src).start()
            self.to_sib(arr, src, at.col).start()

        @pl.when(at.row + dist < at.rows)
        def _():
            src = at.row + dist
            self.arrive(arr, src, at.col)
            pl.when(at.has_down)(lambda: self.to_down(arr, src).start())
            self.to_across(arr, src).start()
            self.to_sib(arr, src, at.col).start()

    def crossed(self, arr):
        at = self.at

        def one(src):
            self.arrive(arr, src, 1 - at.col)
            self.to_sib(arr, src, 1 - at.col).start()

        one(at.row)
        for dist in range(1, at.rows):
            pl.when(at.row - dist >= 0)(lambda: one(at.row - dist))
            pl.when(at.row + dist < at.rows)(lambda: one(at.row + dist))

    def paired(self, arr):
        @pl.loop(0, 2 * self.at.rows)
        def _(i):
            self.copy(arr, 2 * i + 1 - self.at.core, 0, self.at.sib).wait_recv()

    def sent(self, arr):
        at = self.at

        @pl.loop(0, at.rows)
        def _(i):
            self.to_sib(arr, i, 0).wait_send()
            self.to_sib(arr, i, 1).wait_send()
            self.to_across(arr, i).wait_send()
            pl.when(jnp.logical_and(i <= at.row, at.has_up))(
                lambda: self.to_up(arr, i).wait_send()
            )
            pl.when(jnp.logical_and(i >= at.row, at.has_down))(
                lambda: self.to_down(arr, i).wait_send()
            )


class Scatter:
    def __init__(self, place, parts, heights, sibs, crosses, lines, sems):
        self.at, self.parts, self.heights = place, parts, heights
        self.sibs, self.crosses, self.lines = sibs, crosses, lines
        self.sib_s, self.sib_r, self.x_s, self.x_r, self.z_s, self.z_r = sems

    def block(self, arr, dst):
        height = self.heights[arr]
        return self.parts[arr].at[pl.ds(pl.multiple_of(dst * height, height), height)]

    def mine(self, arr, pair):
        return self.block(arr, 2 * pair + self.at.core)

    def from_sib(self, arr, pair):
        if arr != ATTN:
            return self.sibs[arr].at[pair]
        height = self.heights[arr]
        return self.sibs[arr].at[pl.ds(pl.multiple_of(pair * height, height), height)]

    def sib_copy(self, arr, pair):
        return remote(
            self.block(arr, 2 * pair + 1 - self.at.core),
            self.from_sib(arr, pair),
            self.sib_s.at[arr, pair],
            self.sib_r.at[arr, pair],
            self.at.sib,
        )

    def x_copy(self, arr, dst_row):
        return remote(
            self.mine(arr, 2 * dst_row + 1 - self.at.col),
            self.crosses[arr].at[dst_row],
            self.x_s.at[arr, dst_row],
            self.x_r.at[arr, dst_row],
            self.at.across,
        )

    def x_arrived(self, arr, dst_row):
        self.x_copy(arr, dst_row).wait_recv()

    def z_slot(self, way, dst_row, to_row):
        return jnp.where(jnp.logical_and(way == 1, dst_row == to_row), self.at.rows, dst_row)

    def z_copy(self, arr, way, dst_row, slot):
        return remote(
            self.mine(arr, 2 * dst_row + self.at.col),
            self.lines[arr].at[slot],
            self.z_s.at[arr, dst_row],
            self.z_r.at[arr, slot],
            (self.at.seg, self.at.here + 4 - 8 * way),
        )

    def each_far(self, body, dists=None):
        at = self.at
        for dist in dists or range(at.rows - 1, 0, -1):

            @pl.loop(0, 2)
            def _(way):
                dst_row = at.row + (1 - 2 * way) * dist
                pl.when(jnp.logical_and(dst_row >= 0, dst_row < at.rows))(
                    lambda: body(way, dst_row)
                )

    def clear(self):
        rows = self.at.rows

        def zero(lines, slot):
            lines[slot] = jnp.zeros(lines.shape[1:], jnp.bfloat16)

        @pl.when(jnp.logical_not(self.at.has_down))
        def _():
            for lines in self.lines:
                for slot in range(rows):
                    zero(lines, slot)

        @pl.when(jnp.logical_not(self.at.has_up))
        def _():
            for lines in self.lines:
                for slot in [*range(rows - 1), rows]:
                    zero(lines, slot)

    def start_pairs(self, arr):
        def go(dst_row, at_col):
            self.sib_copy(arr, 2 * dst_row + at_col).start()

        self.each_far(lambda way, dst_row: go(dst_row, 1 - self.at.col))
        go(self.at.row, 1 - self.at.col)
        self.each_far(lambda way, dst_row: go(dst_row, self.at.col))
        go(self.at.row, self.at.col)

    def pair_sum(self, arr, pair):
        self.sib_copy(arr, pair).wait_recv()
        return wide(self.mine(arr, pair)[...]) + wide(self.from_sib(arr, pair)[...])

    def x_one(self, arr, dst_row):
        pair = 2 * dst_row + 1 - self.at.col
        self.mine(arr, pair)[...] = low(self.pair_sum(arr, pair))
        self.x_copy(arr, dst_row).start()

    def x_stage(self, arr):
        self.each_far(lambda way, dst_row: self.x_one(arr, dst_row))
        self.x_one(arr, self.at.row)

    def column_sum(self, arr, dst_row):
        self.x_arrived(arr, dst_row)
        total = self.pair_sum(arr, 2 * dst_row + self.at.col)
        return total + wide(self.crosses[arr][dst_row])

    def z_stage(self, arr, dists=None):
        at = self.at

        def go(way, dst_row):
            behind = at.row - 1 + 2 * way

            @pl.when(jnp.logical_and(behind >= 0, behind < at.rows))
            def _():
                self.z_copy(arr, way, dst_row, dst_row).wait_recv()

            total = self.column_sum(arr, dst_row) + wide(self.lines[arr][dst_row])
            self.mine(arr, 2 * dst_row + at.col)[...] = low(total)
            slot = self.z_slot(way, dst_row, at.row + 1 - 2 * way)
            self.z_copy(arr, way, dst_row, slot).start()

        self.each_far(go, dists)

    def final(self, arr):
        at = self.at
        pl.when(at.has_down)(lambda: self.z_copy(arr, 0, at.row, at.row).wait_recv())
        pl.when(at.has_up)(lambda: self.z_copy(arr, 1, at.row, at.rows).wait_recv())
        total = self.column_sum(arr, at.row) + wide(self.lines[arr][at.row])
        return total + wide(self.lines[arr][at.rows])

    def sent(self, arr):
        @pl.loop(0, self.at.rows)
        def _(i):
            self.sib_copy(arr, 2 * i).wait_send()
            self.sib_copy(arr, 2 * i + 1).wait_send()
            self.x_copy(arr, i).wait_send()

        self.each_far(lambda way, dst_row: self.z_copy(arr, way, dst_row, 0).wait_send())


class Total:
    def __init__(self, place, pair, sib, cross, lines, sems):
        self.at, self.pair, self.sib, self.cross, self.lines = place, pair, sib, cross, lines
        self.near_s, self.near_r, self.z_s, self.z_r = sems

    def sib_copy(self, own):
        return remote(own, self.sib, self.near_s.at[0], self.near_r.at[0], self.at.sib)

    def x_copy(self):
        return remote(self.pair, self.cross, self.near_s.at[1], self.near_r.at[1], self.at.across)

    def z_copy(self, way, src_row):
        line = self.lines.at[src_row]
        to = (self.at.seg, self.at.here + 4 - 8 * way)
        return remote(line, line, self.z_s.at[way, src_row], self.z_r.at[src_row], to)

    def cross_over(self, own):
        self.sib_copy(own).wait_recv()
        self.pair[...] = own[...] + self.sib[...]
        self.x_copy().start()

    def along(self):
        self.x_copy().wait_recv()
        self.lines[self.at.row] = self.pair[...] + self.cross[...]
        pl.when(self.at.has_up)(lambda: self.z_copy(0, self.at.row).start())
        pl.when(self.at.has_down)(lambda: self.z_copy(1, self.at.row).start())

    def away(self, dist):
        at = self.at

        @pl.when(at.row - dist >= 0)
        def _():
            src = at.row - dist
            self.z_copy(0, src).wait_recv()
            pl.when(at.has_up)(lambda: self.z_copy(0, src).start())

        @pl.when(at.row + dist < at.rows)
        def _():
            src = at.row + dist
            self.z_copy(1, src).wait_recv()
            pl.when(at.has_down)(lambda: self.z_copy(1, src).start())

    def sent(self, own):
        at = self.at
        self.sib_copy(own).wait_send()
        self.x_copy().wait_send()

        @pl.loop(0, at.rows)
        def _(i):
            pl.when(jnp.logical_and(i <= at.row, at.has_up))(
                lambda: self.z_copy(0, i).wait_send()
            )
            pl.when(jnp.logical_and(i >= at.row, at.has_down))(
                lambda: self.z_copy(1, i).wait_send()
            )


def blocks_body(fused, rows, names, *refs):
    r = dict(zip(names, refs))
    at = Place(rows)
    is_enc = at.seg == 0
    is_dec = at.seg == 1
    x_ref, mask_ref, seg_out, stats = r["x"], r["mask"], r["seg_out"], r["stats"]
    w_attn, w_up, w_down = weights = [r["w_attn"], r["w_up"], r["w_down"]]
    norms, maps, h_buf = r["norms"], r["maps"], r["h"]
    a_s, qkv_s, mixed_s, c_s = r["a"], r["qkv"], r["mixed"], r["c"]
    act_s, slope_s, gm_s, go_s, gmix_s = r["act"], r["slope"], r["gm"], r["go"], r["gmix"]
    xhats, rstds = (r["xhat1"], r["xhat2"]), (r["rstd1"], r["rstd2"])
    lse_pack, bias_pack = r["lse_pack"], r["bias_pack"]
    u_s, small_acc, relay_tx, relay_rx = r["u"], r["small_acc"], r["relay_tx"], r["relay_rx"]
    enc_s = gm_s
    total_rows, features = x_ref.shape
    images = h_buf.shape[0]
    patches = total_rows // images
    hidden = w_up.shape[1]
    head_dim = features // HEADS
    pairs = features // 128
    chunk = features
    code_rows = relay_tx.shape[1]

    def rows_of(m):
        return pl.ds(pl.multiple_of(m * patches, patches), patches)

    def cols(j, width):
        return pl.ds(pl.multiple_of(j * width, width), width)

    def relay(m):
        return remote(
            relay_tx.at[m], relay_rx.at[m], r["relay_s"].at[m], r["relay_r"].at[m], at.other
        )

    def result(m):
        return pltpu.make_async_copy(h_buf.at[m], seg_out.at[rows_of(m)], r["out_sem"].at[m])

    def energy(slot, tensor, rs):
        square = row_sum(tensor * tensor * jnp.concatenate([mask_ref[rs, :]] * pairs, axis=1))
        total = square[:, :128]
        for j in range(1, pairs):
            total = total + square[:, j * 128 : (j + 1) * 128]
        stats[slot : slot + 1, :] += total

    def code_mask(array):
        return jnp.where(
            lax.broadcasted_iota(jnp.int32, array.shape, 0) < CODE_BITS, array, 0.0
        )

    def normalize(values, which, rs):
        gain, bias = norms[2 * which : 2 * which + 1, :], norms[2 * which + 1 : 2 * which + 2, :]
        centered = values - row_mean(values)
        scale = lax.rsqrt(row_mean(centered * centered) + norm_eps)
        hat = centered * scale
        xhats[which][rs, :] = low(hat)
        rstds[which][rs, :] = scale
        return low(hat * gain + bias)

    def norm_back(grad, which, rs):
        gain, slot = norms[2 * which : 2 * which + 1, :], code_rows + 2 * which
        hat = wide(xhats[which][rs, :])
        small_acc[slot : slot + 1, :] += row_sum(grad * hat)
        small_acc[slot + 1 : slot + 2, :] += row_sum(grad)
        scaled = grad * gain
        back = scaled - row_mean(scaled) - hat * row_mean(scaled * hat)
        return rstds[which][rs, :] * back

    lane = lax.broadcasted_iota(jnp.int32, (1, 128), 1)
    halves = [low(wide(lane < head_dim)), low(wide(lane >= head_dim))]
    in_first = lax.broadcasted_iota(jnp.int32, (patches, 128), 1) < head_dim
    one_lane = low(wide(jnp.broadcast_to(lane == 48, (patches, 128))))

    def head_lanes(head):
        return jnp.logical_and(lane < 48, lax.rem(lane, 16) == head)

    def three_terms(values):
        first = wide(low(values))
        rest = values - first
        second = wide(low(rest))
        third = wide(low(rest - second))
        return jnp.where(lane < 16, first, jnp.where(lane < 32, second, third))

    def attention(m, hooks=()):
        rs = rows_of(m)
        bias_pack[rs, :] = low(jnp.where(lane == 48, (1.0 - mask_ref[rs, :]) * -1e30, 0.0))
        a_s[rs, :] = normalize(h_buf[m], 0, rs)
        for j in range(3):
            part = dot_nn(a_s[rs, :], w_attn[:, j * features : (j + 1) * features])
            if j == 0:
                part = part * (LOG2E / math.sqrt(head_dim))
            qkv_s[rs, j * features : (j + 1) * features] = low(part)

        def heads(j, lse):
            query = qkv_s[rs, cols(j, 128)]
            key = qkv_s[rs, cols(j + pairs, 128)]
            value = qkv_s[rs, cols(j + 2 * pairs, 128)]
            query = jnp.concatenate([query, one_lane], axis=1)
            outs = []
            for i in range(2):
                keys_one = jnp.concatenate([key * halves[i], bias_pack[rs, :]], axis=1)
                scores = dot_nt(query, keys_one)
                top = jnp.max(scores, -1, keepdims=True)
                weight = low(jnp.exp2(scores - top))
                mixed = dot_nn(weight, value * halves[i] + halves[1 - i])
                count = mixed[:, (1 - i) * head_dim : (1 - i) * head_dim + 1]
                outs.append(mixed * (1.0 / count))
                lse = jnp.where(head_lanes(2 * j + i), top + jnp.log2(count), lse)
            mixed_s[rs, cols(j, 128)] = low(jnp.where(in_first, outs[0], outs[1]))
            return lse

        lse = jnp.zeros((patches, 128), jnp.float32)
        for part in range(3):
            lse = lax.fori_loop(part * pairs // 3, (part + 1) * pairs // 3, heads, lse)
            for hook in hooks[part : part + 1]:
                hook()
        lse_pack[rs, :] = low(
            jnp.where(lane < 48, three_terms(-lse), jnp.where(lane == 48, 1.0, 0.0))
        )
        attn_out = dot_nn(mixed_s[rs, :], w_attn[:, 3 * features : 4 * features])
        energy(1, attn_out, rs)
        h_buf[m] += attn_out
        c_s[rs, :] = normalize(h_buf[m], 1, rs)

    def widen(m):
        rs = rows_of(m)

        def up(j, _):
            pre = dot_nn(c_s[rs, :], w_up[:, cols(j, chunk)])
            phi = 0.5 + 0.5 * lax.erf(pre * math.sqrt(0.5))
            act_s[rs, cols(j, chunk)] = low(pre * phi)
            slope_s[rs, cols(j, chunk)] = low(
                phi + pre * (jnp.exp(-0.5 * pre * pre) * (1.0 / math.sqrt(2.0 * math.pi)))
            )
            return 0

        lax.fori_loop(0, hidden // chunk, up, 0)

    def narrow(m):
        rs = rows_of(m)
        mlp_out = dot_nn(act_s[rs, :hidden], w_down[...])
        energy(2, mlp_out, rs)
        h_buf[m] += mlp_out
        energy(0, h_buf[m], rs)
        stats[3:4, :] += row_sum(mask_ref[rs, :])

    def forward(m, _):
        rs = rows_of(m)

        @pl.when(is_dec)
        def _():
            relay(m).wait_recv()
            h_buf[m] = dot_tn(relay_rx[m], maps[...])
            attention(m)
            widen(m)

        narrow(m)

        @pl.when(is_enc)
        def _():
            enc_s[rs, :] = low(h_buf[m])
            code_pre = code_mask(dot_nt(maps[...], enc_s[rs, :]))
            u_s[m] = code_pre
            scale = lax.rsqrt(row_sum(code_pre * code_pre) + 1.0)
            relay_tx[m] = low(jnp.tanh(2.0 * math.sqrt(CODE_BITS) * (code_pre * scale)))
            relay(m).start()

        pl.when(is_dec)(lambda: result(m).start())
        return 0

    def mlp_back(m):
        rs = rows_of(m)

        @pl.when(is_enc)
        def _():
            relay(m).wait_recv()
            code_pre = u_s[m]
            scale = lax.rsqrt(row_sum(code_pre * code_pre) + 1.0)
            unit = code_pre * scale
            factor = 2.0 * math.sqrt(CODE_BITS)
            bent = jnp.tanh(factor * unit)
            g_unit = wide(relay_rx[m]) * (factor * (1.0 - bent * bent))
            g_u = low((g_unit - unit * row_sum(g_unit * unit)) * scale)
            small_acc[0:code_rows, :] += dot_nn(g_u, enc_s[rs, :])
            h_buf[m] = dot_tn(g_u, maps[...])

        @pl.when(is_dec)
        def _():
            result(m).wait()
            h_buf[m] = wide(x_ref[rs, :])

        gm_s[rs, :] = low(h_buf[m])

        def down(j, _):
            g_act = dot_nt(gm_s[rs, :], w_down[cols(j, chunk), :])
            slope_s[rs, cols(j, chunk)] = low(g_act * wide(slope_s[rs, cols(j, chunk)]))
            return 0

        lax.fori_loop(0, hidden // chunk, down, 0)
        g_c = dot_nt(slope_s[rs, :], w_up[...])
        h_buf[m] += norm_back(g_c, 1, rs)
        go_s[rs, :] = low(h_buf[m])

    def attn_back(m, hooks=()):
        rs = rows_of(m)
        gmix_s[...] = low(dot_nt(go_s[rs, :], w_attn[:, 3 * features : 4 * features]))
        product = wide(gmix_s[...]) * wide(mixed_s[rs, :])
        high = low(product)
        head_of = lax.broadcasted_iota(jnp.int32, (features, 128), 0) // head_dim
        lane_of = lax.broadcasted_iota(jnp.int32, (features, 128), 1)
        pick = low(wide(jnp.logical_and(lane_of < 48, lax.rem(lane_of, 16) == head_of)))
        inner = dot_nn(high, pick) + dot_nn(low(product - wide(high)), pick)
        inner_pack = low(three_terms(-inner))

        def heads(j, _):
            places = [cols(j + i * pairs, 128) for i in range(3)]
            query, key, value = [qkv_s[rs, place] for place in places]
            g_mixed = gmix_s[:, cols(j, 128)]
            query_more = jnp.concatenate([query, lse_pack[rs, :]], axis=1)
            g_more = jnp.concatenate([g_mixed, inner_pack], axis=1)
            found = []
            for i in range(2):
                extra = bias_pack[rs, :] + low(wide(head_lanes(2 * j + i)))
                probs = jnp.exp2(
                    dot_nt(query_more, jnp.concatenate([key * halves[i], extra], axis=1))
                )
                g_probs = dot_nt(g_more, jnp.concatenate([value * halves[i], extra], axis=1))
                g_scores = low(probs * g_probs)
                found.append(
                    (
                        dot_nn(g_scores, key),
                        dot_tn(g_scores, query),
                        dot_tn(low(probs), g_mixed),
                    )
                )
            scales = (1.0 / math.sqrt(head_dim), 1.0 / LOG2E, 1.0)
            for i in range(3):
                joined = jnp.where(in_first, found[0][i], found[1][i])
                qkv_s[rs, places[i]] = low(joined * scales[i])
            return 0

        for part in range(3):
            lax.fori_loop(part * pairs // 3, (part + 1) * pairs // 3, heads, 0)
            for hook in hooks[part : part + 1]:
                hook()
        g_a = dot_nt(qkv_s[rs, :], w_attn[:, : 3 * features])
        h_buf[m] += norm_back(g_a, 0, rs)

        @pl.when(is_enc)
        def _():
            result(m).start()

        @pl.when(is_dec)
        def _():
            g_z = low(h_buf[m])
            small_acc[0:code_rows, :] += dot_nn(relay_rx[m], g_z)
            relay_tx[m] = low(code_mask(dot_nt(maps[...], g_z)))
            relay(m).start()

    def take_small():
        small = wide(w_attn[:, 4 * features :]).T
        maps[...] = low(code_mask(small[:code_rows]))
        norms[0:4, :] = small[CODE_BITS : CODE_BITS + 4]

    def start_image(m):
        h_buf[m] = wide(x_ref[rows_of(m), :])

    def up_grads():
        for j in range(hidden // chunk):
            place = slice(j * chunk, (j + 1) * chunk)
            w_up[:, place] = low(dot_tn(c_s[...], slope_s[:, place]))

    def attn_grads():
        for j in range(3):
            place = slice(j * features, (j + 1) * features)
            w_attn[:, place] = low(dot_tn(a_s[...], qkv_s[:, place]))
        w_attn[:, 3 * features : 4 * features] = low(dot_tn(mixed_s[...], go_s[...]))
        small_grad = jnp.concatenate(
            [
                small_acc[0:CODE_BITS, :],
                small_acc[code_rows : code_rows + 4, :],
                jnp.zeros((128 - CODE_BITS - 4, features), jnp.float32),
            ],
            axis=0,
        )
        w_attn[:, 4 * features :] = low(small_grad.T)

    def fresh():
        stats[...] = jnp.zeros_like(stats)
        small_acc[...] = jnp.zeros_like(small_acc)

    def before_relay():
        @pl.when(is_dec)
        def _():
            stats[...] = jnp.zeros_like(stats)

    if not fused:
        copies = [
            pltpu.make_async_copy(r[name], weights[arr], r["own_sem"].at[arr])
            for arr, name in enumerate(("attn_all", "up_all", "down_all"))
        ]
        for copy in copies:
            copy.start()
        fresh()
        at.meet(False)
        for copy in copies:
            copy.wait()
        take_small()
        for m in range(images):
            start_image(m)
            attention(m)
            widen(m)
        before_relay()
        lax.fori_loop(0, images, forward, 0)
        for m in reversed(range(images)):
            mlp_back(m)
            attn_back(m)
        w_down[...] = low(dot_tn(act_s[:, :hidden], gm_s[...]))
        up_grads()
        attn_grads()
        for arr, name in enumerate(("g_attn", "g_up", "g_down")):
            copy = pltpu.make_async_copy(weights[arr], r[name], r["own_sem"].at[arr])
            copy.start()
            copy.wait()
        for m in range(images):
            pl.when(is_enc)(lambda: result(m).wait())
            relay(m).wait_send()
        return

    heights = (r["qkv_in"].shape[0], r["up_in"].shape[0], r["down_in"].shape[0])
    own_rows = [
        pl.ds(pl.multiple_of(at.here * height, height), height) for height in heights
    ]
    own_copies = [
        pltpu.make_async_copy(src, dst, r["own_sem"].at[i])
        for i, (src, dst) in enumerate(
            (
                (r["qkv_in"], w_attn.at[own_rows[ATTN], pl.ds(0, 3 * features)]),
                (r["out_in"], w_attn.at[own_rows[ATTN], pl.ds(3 * features, features)]),
                (r["small_in"], w_attn.at[own_rows[ATTN], pl.ds(4 * features, 128)]),
                (r["up_in"], w_up.at[own_rows[UP]]),
                (r["down_in"], w_down.at[own_rows[DOWN]]),
            )
        )
    ]
    gather = Gather(at, weights, heights, r["g_send"], r["g_recv"])
    scatter = Scatter(
        at,
        weights,
        heights,
        (act_s, r["sib_u"], r["sib_d"]),
        (r["x_a"], r["x_u"], r["x_d"]),
        (r["z_a"], r["z_u"], r["z_d"]),
        [r[name] for name in ("sib_s", "sib_r", "x_s", "x_r", "z_s", "z_r")],
    )
    total = Total(
        at,
        r["t_pair"],
        r["t_sib"],
        r["t_cross"],
        r["t_lines"],
        [r[name] for name in ("t_near_s", "t_near_r", "t_z_s", "t_z_r")],
    )
    for copy in own_copies:
        copy.start()
    at.meet(True)
    for copy in own_copies[:3]:
        copy.wait()
    gather.own(ATTN)
    fresh()
    scatter.clear()
    for m in range(images):
        start_image(m)
    gather.away(ATTN, 1)
    gather.away(ATTN, 2)
    own_copies[3].wait()
    gather.own(UP)
    gather.away(ATTN, 3)
    gather.crossed(ATTN)
    gather.away(UP, 1)
    gather.paired(ATTN)
    take_small()

    def own_down():
        own_copies[4].wait()
        gather.own(DOWN)

    attention(0, [lambda: gather.away(UP, 2), own_down, lambda: gather.away(UP, 3)])
    attention(
        1,
        [
            lambda: gather.away(DOWN, 1),
            lambda: gather.away(DOWN, 2),
            lambda: gather.crossed(UP),
        ],
    )
    gather.away(DOWN, 3)
    gather.paired(UP)
    for m in range(images):
        widen(m)
    gather.crossed(DOWN)
    gather.paired(DOWN)
    for arr in range(3):
        gather.sent(arr)
    before_relay()
    lax.fori_loop(0, images, forward, 0)
    total.sib_copy(stats).start()
    mlp_back(1)
    total.cross_over(stats)
    attn_back(1)
    mlp_back(0)
    total.along()

    def down_block(pair):
        span = 2 * heights[DOWN]
        place = pl.ds(pl.multiple_of(pair * span, span), span)
        w_down[place, :] = low(dot_tn(act_s[:, place], gm_s[...]))
        scatter.sib_copy(DOWN, pair).start()

    scatter.each_far(lambda way, dst_row: down_block(2 * dst_row + 1 - at.col))
    down_block(2 * at.row + 1 - at.col)
    scatter.x_stage(DOWN)
    scatter.each_far(lambda way, dst_row: down_block(2 * dst_row + at.col))
    down_block(2 * at.row + at.col)
    total.away(1)
    up_grads()
    scatter.start_pairs(UP)
    scatter.x_stage(UP)
    total.away(2)
    attn_back(
        0,
        [
            lambda: scatter.z_stage(DOWN, [3]),
            lambda: scatter.z_stage(DOWN, [2]),
            lambda: scatter.z_stage(DOWN, [1]),
        ],
    )
    attn_grads()
    scatter.start_pairs(ATTN)
    scatter.x_stage(ATTN)
    total.away(3)
    sums = total.lines[0]
    for i in range(1, rows):
        sums = sums + total.lines[i]
    sums = jnp.sum(sums, -1, keepdims=True)
    scale = 128.0 / (sums[3:4] * features)
    found = jnp.sqrt(sums * scale)
    row_no = lax.broadcasted_iota(jnp.int32, (8, 128), 0)
    lane_no = lax.broadcasted_iota(jnp.int32, (8, 128), 1)
    r["rms"][...] = row_sum(jnp.where(row_no == lane_no, found, 0.0))[:, :3]
    r["down_out"][...] = scatter.final(DOWN)
    scatter.z_stage(UP)
    r["up_out"][...] = scatter.final(UP)
    scatter.z_stage(ATTN)
    last = scatter.final(ATTN)
    r["qkv_out"][...] = last[:, : 3 * features]
    r["out_out"][...] = last[:, 3 * features : 4 * features]
    small = last[:, 4 * features :]
    r["maps_out"][...] = small[:, :CODE_BITS]
    small = jnp.concatenate(
        [small, jnp.zeros((128 - small.shape[0], 128), jnp.float32)], axis=0
    ).T
    for i in range(4):
        r["norm_out"][i : i + 1, :] = small[CODE_BITS + i : CODE_BITS + i + 1, : heights[ATTN]]
    for m in range(images):
        pl.when(is_enc)(lambda: result(m).wait())
        relay(m).wait_send()
    for arr in range(3):
        scatter.sent(arr)
    total.sent(stats)


def run_blocks(fused, operands, x, mask, rows):
    images, patches, features = x.shape
    total = images * patches
    hidden = 4 * features
    attn_width = 4 * features + 128
    code_rows = -(-CODE_BITS // 16) * 16
    bf16, f32 = jnp.bfloat16, jnp.float32
    any_spec = pl.BlockSpec(memory_space=pl.ANY)
    vmem_spec = pl.BlockSpec(memory_space=pltpu.VMEM)
    dma = pltpu.SemaphoreType.DMA
    ins = dict(operands, x=x.reshape(total, features), mask=mask)
    outs = {"seg_out": ((total, features), f32)}
    full = {"a": (features, attn_width), "u": (features, hidden), "d": (hidden, features)}
    buffers = {
        "w_attn": (full["a"], bf16), "w_up": (full["u"], bf16), "w_down": (full["d"], bf16),
        "norms": ((8, features), f32), "maps": ((code_rows, features), bf16),
        "h": ((images, patches, features), f32),
        "xhat1": ((total, features), bf16), "rstd1": ((total, 1), f32),
        "xhat2": ((total, features), bf16), "rstd2": ((total, 1), f32),
        "a": ((total, features), bf16), "qkv": ((total, 3 * features), bf16),
        "mixed": ((total, features), bf16), "c": ((total, features), bf16),
        "act": ((total, attn_width), bf16), "slope": ((total, hidden), bf16),
        "lse_pack": ((total, 128), bf16), "bias_pack": ((total, 128), bf16),
        "gm": ((total, features), bf16), "go": ((total, features), bf16),
        "gmix": ((patches, features), bf16),
        "u": ((images, code_rows, patches), f32), "small_acc": ((code_rows + 8, features), f32),
        "relay_tx": ((images, code_rows, patches), bf16),
        "relay_rx": ((images, code_rows, patches), bf16),
    }
    sems = {"relay_s": (images,), "relay_r": (images,), "out_sem": (images,)}
    in_vmem = ["x", "mask", "small_in"]
    if fused:
        outs["rms"] = ((1, 3), f32)
        shards = {
            "a": (operands["qkv_in"].shape[0], attn_width),
            "u": operands["up_in"].shape,
            "d": operands["down_in"].shape,
        }
        outs["qkv_out"] = (operands["qkv_in"].shape, f32)
        outs["out_out"] = (operands["out_in"].shape, f32)
        outs["up_out"] = (shards["u"], f32)
        outs["down_out"] = (shards["d"], f32)
        outs["maps_out"] = ((shards["a"][0], CODE_BITS), f32)
        outs["norm_out"] = ((4, shards["a"][0]), f32)
        buffers["stats"] = ((8, 128), f32)
        for name, shape in shards.items():
            if name != "a":
                buffers["sib_" + name] = ((2 * rows,) + shape, bf16)
            buffers["x_" + name] = ((rows,) + shape, bf16)
            buffers["z_" + name] = ((rows + 1,) + shape, bf16)
        for name in ("t_pair", "t_sib", "t_cross"):
            buffers[name] = ((8, 128), f32)
        buffers["t_lines"] = ((rows, 8, 128), f32)
        sems.update(
            own_sem=(5,), g_send=(3, 5 * rows), g_recv=(3, 4 * rows),
            sib_s=(3, 2 * rows), sib_r=(3, 2 * rows), x_s=(3, rows), x_r=(3, rows),
            z_s=(3, rows), z_r=(3, rows + 1),
            t_near_s=(2,), t_near_r=(2,), t_z_s=(2, rows), t_z_r=(rows,),
        )
    else:
        outs["g_attn"] = (full["a"], bf16)
        outs["g_up"] = (full["u"], bf16)
        outs["g_down"] = (full["d"], bf16)
        outs["stats"] = ((8, 128), f32)
        sems["own_sem"] = (3,)
    names = [*ins, *outs, *buffers, *sems]
    out_any = ("seg_out", "g_attn", "g_up", "g_down")
    found = pl.pallas_call(
        partial(blocks_body, fused, rows, names),
        out_shape=tuple(jax.ShapeDtypeStruct(s, t) for s, t in outs.values()),
        in_specs=[vmem_spec if n in in_vmem else any_spec for n in ins],
        out_specs=tuple(any_spec if n in out_any else vmem_spec for n in outs),
        scratch_shapes=[pltpu.VMEM(s, t) for s, t in buffers.values()]
        + [dma(s) for s in sems.values()],
        compiler_params=pltpu.CompilerParams(
            collective_id=1, has_side_effects=True, vmem_limit_bytes=VMEM_BYTES
        ),
        name="both_blocks",
    )(*ins.values())
    return dict(zip(outs, found))


def on_device(
    segment_input,
    image_extent,
    norm1_gain,
    norm1_bias,
    norm2_gain,
    norm2_bias,
    qkv_weight,
    out_weight,
    up_weight,
    down_weight,
    code_maps,
):
    _, images, patches, features = segment_input.shape
    qkv_width = qkv_weight.shape[2]
    count = lax.axis_size("dp")
    small = jnp.concatenate(
        [code_maps[0]]
        + [v[0][:, None] for v in (norm1_gain, norm1_bias, norm2_gain, norm2_bias)],
        axis=1,
    )
    small = jnp.pad(small, ((0, 0), (0, 128 - small.shape[1])))
    validity = extent_mask(image_extent, patches)
    mask = jnp.broadcast_to(validity.reshape(-1, 1), (images * patches, 128))
    x = segment_input[0]
    if qkv_weight.shape[1] % 16 == 0 and count % 4 == 0:
        operands = {
            "qkv_in": qkv_weight[0],
            "out_in": out_weight[0],
            "small_in": small,
            "up_in": up_weight[0],
            "down_in": down_weight[0],
        }
        found = run_blocks(True, operands, x, mask, count // 4)
        rms_stats = found["rms"]
        qkv_shard, out_shard = found["qkv_out"], found["out_out"]
        up_shard, down_shard = found["up_out"], found["down_out"]
        maps_shard = found["maps_out"]
        norm_shards = [found["norm_out"][i : i + 1] for i in range(4)]
    else:
        attn = jnp.concatenate([qkv_weight[0], out_weight[0], small], axis=1)
        operands = {
            name: lax.all_gather(shard, "dp", axis=0, tiled=True)
            for name, shard in (
                ("attn_all", attn),
                ("up_all", up_weight[0]),
                ("down_all", down_weight[0]),
            )
        }
        found = run_blocks(False, operands, x, mask, 1)
        attn_shard, up_shard, down_shard = [
            lax.psum_scatter(
                found[name].astype(jnp.float32), "dp", scatter_dimension=0, tiled=True
            )
            for name in ("g_attn", "g_up", "g_down")
        ]
        stats = lax.psum(found["stats"], "dp")
        rms_stats = jnp.sqrt(jnp.sum(stats[:3], 1) / (stats[3, 0] * features))[None]
        qkv_shard = attn_shard[:, :qkv_width]
        out_shard = attn_shard[:, qkv_width : qkv_width + features]
        small_shard = attn_shard[:, qkv_width + features :]
        maps_shard = small_shard[:, :CODE_BITS]
        norm_shards = [small_shard[:, CODE_BITS + i][None] for i in range(4)]
    return (
        found["seg_out"].reshape(segment_input.shape),
        rms_stats,
        *norm_shards,
        qkv_shard[None],
        out_shard[None],
        up_shard[None],
        down_shard[None],
        maps_shard[None],
    )


def solution(mesh):
    return jax.shard_map(
        on_device,
        mesh=mesh,
        in_specs=(
            P("segment", "dp", None, None),
            P("dp", None),
            P("segment", "dp"),
            P("segment", "dp"),
            P("segment", "dp"),
            P("segment", "dp"),
            P("segment", "dp", None),
            P("segment", "dp", None),
            P("segment", "dp", None),
            P("segment", "dp", None),
            P("segment", "dp", None),
        ),
        out_specs=(
            P("segment", "dp", None, None),
            P("segment", None),
            P("segment", "dp"),
            P("segment", "dp"),
            P("segment", "dp"),
            P("segment", "dp"),
            P("segment", "dp", None),
            P("segment", "dp", None),
            P("segment", "dp", None),
            P("segment", "dp", None),
            P("segment", "dp", None),
        ),
        check_vma=False,
    )
```

```python
from functools import partial
import math

import jax
import jax.numpy as jnp
from jax import lax
from jax.experimental import pallas as pl
from jax.experimental.pallas import tpu as pltpu
from jax.sharding import PartitionSpec as P

HEADS = 12
CODE_BITS = 18
GH = 16
GW = 24
LOG2E = math.log2(math.e)
VMEM_BYTES = 62 << 20


norm_eps = 1e-06


MESH_ID = pl.DeviceIdType.MESH
ATTN, UP, DOWN = 0, 1, 2


def dot_nn(left, right):
    return lax.dot_general(left, right, (((1,), (0,)), ((), ())), preferred_element_type=jnp.float32)


def dot_nt(left, right):
    return lax.dot_general(left, right, (((1,), (1,)), ((), ())), preferred_element_type=jnp.float32)


def dot_tn(left, right):
    return lax.dot_general(left, right, (((0,), (0,)), ((), ())), preferred_element_type=jnp.float32)


def low(array):
    return array.astype(jnp.bfloat16)


def wide(array):
    return array.astype(jnp.float32)


def beside(arrays):
    return jnp.concatenate(arrays, axis=1)


def beneath(arrays):
    return jnp.concatenate(arrays, axis=0)


def row_sum(array):
    return jnp.sum(array, 0, keepdims=True)


def row_mean(array):
    return jnp.mean(array, -1, keepdims=True)


def remote(src, dst, ssem, rsem, to):
    return pltpu.make_async_remote_copy(
        src_ref=src,
        dst_ref=dst,
        send_sem=ssem,
        recv_sem=rsem,
        device_id=to,
        device_id_type=MESH_ID,
    )


class Place:
    def __init__(self, rows):
        self.rows = rows
        self.seg = lax.axis_index("segment")
        self.here = lax.axis_index("dp")
        self.core = lax.rem(self.here, 2)
        self.col = lax.rem(self.here // 2, 2)
        self.row = self.here // 4
        self.sib = (self.seg, self.here + 1 - 2 * self.core)
        self.across = (self.seg, self.here + 2 - 4 * self.col)
        self.up = (self.seg, self.here + 4)
        self.down = (self.seg, self.here - 4)
        self.other = (1 - self.seg, self.here)
        self.has_up = self.row < rows - 1
        self.has_down = self.row > 0

    def meet(self, in_plane):
        barrier = pltpu.get_barrier_semaphore()

        def greet(to):
            pl.semaphore_signal(barrier, inc=1, device_id=to, device_id_type=MESH_ID)

        greet(self.other)
        if not in_plane:
            pl.semaphore_wait(barrier, 1)
            return
        greet(self.sib)
        greet(self.across)
        pl.when(self.has_up)(lambda: greet(self.up))
        pl.when(self.has_down)(lambda: greet(self.down))
        both = jnp.logical_and(self.has_up, self.has_down)
        pl.semaphore_wait(barrier, jnp.where(both, 5, 4))


class Gather:
    def __init__(self, place, weights, heights, send_sem, recv_sem):
        self.at, self.weights, self.heights = place, weights, heights
        self.send_sem, self.recv_sem = send_sem, recv_sem

    def copy(self, arr, src, slot, to):
        height = self.heights[arr]
        block = self.weights[arr].at[pl.ds(pl.multiple_of(src * height, height), height)]
        return remote(block, block, self.send_sem.at[arr, slot], self.recv_sem.at[arr, src], to)

    def index(self, src_row, src_col):
        return (src_row * 2 + src_col) * 2 + self.at.core

    def to_sib(self, arr, src_row, src_col):
        slot = 3 * self.at.rows + src_row * 2 + src_col
        return self.copy(arr, self.index(src_row, src_col), slot, self.at.sib)

    def to_across(self, arr, src_row):
        slot = 2 * self.at.rows + src_row
        return self.copy(arr, self.index(src_row, self.at.col), slot, self.at.across)

    def to_up(self, arr, src_row):
        return self.copy(arr, self.index(src_row, self.at.col), src_row, self.at.up)

    def to_down(self, arr, src_row):
        slot = self.at.rows + src_row
        return self.copy(arr, self.index(src_row, self.at.col), slot, self.at.down)

    def arrive(self, arr, src_row, src_col):
        self.copy(arr, self.index(src_row, src_col), 0, self.at.sib).wait_recv()

    def own(self, arr):
        row = self.at.row
        pl.when(self.at.has_up)(lambda: self.to_up(arr, row).start())
        pl.when(self.at.has_down)(lambda: self.to_down(arr, row).start())
        self.to_across(arr, row).start()
        self.to_sib(arr, row, self.at.col).start()

    def away(self, arr, dist):
        at = self.at

        @pl.when(at.row - dist >= 0)
        def _():
            src = at.row - dist
            self.arrive(arr, src, at.col)
            pl.when(at.has_up)(lambda: self.to_up(arr, src).start())
            self.to_across(arr, src).start()
            self.to_sib(arr, src, at.col).start()

        @pl.when(at.row + dist < at.rows)
        def _():
            src = at.row + dist
            self.arrive(arr, src, at.col)
            pl.when(at.has_down)(lambda: self.to_down(arr, src).start())
            self.to_across(arr, src).start()
            self.to_sib(arr, src, at.col).start()

    def crossed(self, arr):
        at = self.at

        def one(src):
            self.arrive(arr, src, 1 - at.col)
            self.to_sib(arr, src, 1 - at.col).start()

        one(at.row)
        for dist in range(1, at.rows):
            pl.when(at.row - dist >= 0)(lambda: one(at.row - dist))
            pl.when(at.row + dist < at.rows)(lambda: one(at.row + dist))

    def paired(self, arr):
        @pl.loop(0, 2 * self.at.rows)
        def _(i):
            self.copy(arr, 2 * i + 1 - self.at.core, 0, self.at.sib).wait_recv()

    def sent(self, arr):
        at = self.at

        @pl.loop(0, at.rows)
        def _(i):
            self.to_sib(arr, i, 0).wait_send()
            self.to_sib(arr, i, 1).wait_send()
            self.to_across(arr, i).wait_send()
            pl.when(jnp.logical_and(i <= at.row, at.has_up))(
                lambda: self.to_up(arr, i).wait_send()
            )
            pl.when(jnp.logical_and(i >= at.row, at.has_down))(
                lambda: self.to_down(arr, i).wait_send()
            )


class Scatter:
    def __init__(self, place, parts, heights, sibs, crosses, lines, sems):
        self.at, self.parts, self.heights = place, parts, heights
        self.sibs, self.crosses, self.lines = sibs, crosses, lines
        self.sib_s, self.sib_r, self.x_s, self.x_r, self.z_s, self.z_r = sems

    def block(self, arr, dst):
        height = self.heights[arr]
        return self.parts[arr].at[pl.ds(pl.multiple_of(dst * height, height), height)]

    def mine(self, arr, pair):
        return self.block(arr, 2 * pair + self.at.core)

    def from_sib(self, arr, pair):
        return self.slot(self.sibs, arr, pair)

    def from_across(self, arr, dst_row):
        return self.slot(self.crosses, arr, dst_row + (2 * self.at.rows if arr == ATTN else 0))

    def from_line(self, arr, slot):
        return self.slot(self.lines, arr, slot)

    def slot(self, buffers, arr, slot):
        if arr != ATTN:
            return buffers[arr].at[slot]
        height = self.heights[arr]
        return buffers[arr].at[pl.ds(pl.multiple_of(slot * height, height), height)]

    def sib_copy(self, arr, pair):
        return remote(
            self.block(arr, 2 * pair + 1 - self.at.core),
            self.from_sib(arr, pair),
            self.sib_s.at[arr, pair],
            self.sib_r.at[arr, pair],
            self.at.sib,
        )

    def x_copy(self, arr, dst_row):
        return remote(
            self.mine(arr, 2 * dst_row + 1 - self.at.col),
            self.from_across(arr, dst_row),
            self.x_s.at[arr, dst_row],
            self.x_r.at[arr, dst_row],
            self.at.across,
        )

    def x_arrived(self, arr, dst_row):
        self.x_copy(arr, dst_row).wait_recv()

    def z_slot(self, way, dst_row, to_row):
        return jnp.where(jnp.logical_and(way == 1, dst_row == to_row), self.at.rows, dst_row)

    def z_copy(self, arr, way, dst_row, slot):
        return remote(
            self.mine(arr, 2 * dst_row + self.at.col),
            self.from_line(arr, slot),
            self.z_s.at[arr, dst_row],
            self.z_r.at[arr, slot],
            (self.at.seg, self.at.here + 4 - 8 * way),
        )

    def each_far(self, body, dists=None):
        at = self.at
        for dist in dists or range(at.rows - 1, 0, -1):

            @pl.loop(0, 2)
            def _(way):
                dst_row = at.row + (1 - 2 * way) * dist
                pl.when(jnp.logical_and(dst_row >= 0, dst_row < at.rows))(
                    lambda: body(way, dst_row)
                )

    def clear(self, arr):
        rows = self.at.rows

        def zero(slot):
            place = self.from_line(arr, slot)
            place[...] = jnp.zeros(place.shape, jnp.bfloat16)

        @pl.when(jnp.logical_not(self.at.has_down))
        def _():
            for slot in range(rows):
                zero(slot)

        @pl.when(jnp.logical_not(self.at.has_up))
        def _():
            for slot in [*range(rows - 1), rows]:
                zero(slot)

    def start_pairs(self, arr):
        def go(dst_row, at_col):
            self.sib_copy(arr, 2 * dst_row + at_col).start()

        self.each_far(lambda way, dst_row: go(dst_row, 1 - self.at.col))
        go(self.at.row, 1 - self.at.col)
        self.each_far(lambda way, dst_row: go(dst_row, self.at.col))
        go(self.at.row, self.at.col)

    def pair_sum(self, arr, pair):
        self.sib_copy(arr, pair).wait_recv()
        return wide(self.mine(arr, pair)[...]) + wide(self.from_sib(arr, pair)[...])

    def x_one(self, arr, dst_row):
        pair = 2 * dst_row + 1 - self.at.col
        self.mine(arr, pair)[...] = low(self.pair_sum(arr, pair))
        self.x_copy(arr, dst_row).start()

    def x_stage(self, arr):
        self.each_far(lambda way, dst_row: self.x_one(arr, dst_row))
        self.x_one(arr, self.at.row)

    def column_sum(self, arr, dst_row):
        self.x_arrived(arr, dst_row)
        total = self.pair_sum(arr, 2 * dst_row + self.at.col)
        return total + wide(self.from_across(arr, dst_row)[...])

    def z_stage(self, arr, dists=None):
        at = self.at

        def go(way, dst_row):
            behind = at.row - 1 + 2 * way

            @pl.when(jnp.logical_and(behind >= 0, behind < at.rows))
            def _():
                self.z_copy(arr, way, dst_row, dst_row).wait_recv()

            total = self.column_sum(arr, dst_row) + wide(self.from_line(arr, dst_row)[...])
            self.mine(arr, 2 * dst_row + at.col)[...] = low(total)
            slot = self.z_slot(way, dst_row, at.row + 1 - 2 * way)
            self.z_copy(arr, way, dst_row, slot).start()

        self.each_far(go, dists)

    def final(self, arr):
        at = self.at
        pl.when(at.has_down)(lambda: self.z_copy(arr, 0, at.row, at.row).wait_recv())
        pl.when(at.has_up)(lambda: self.z_copy(arr, 1, at.row, at.rows).wait_recv())
        total = self.column_sum(arr, at.row) + wide(self.from_line(arr, at.row)[...])
        return total + wide(self.from_line(arr, at.rows)[...])

    def sent(self, arr):
        @pl.loop(0, self.at.rows)
        def _(i):
            self.sib_copy(arr, 2 * i).wait_send()
            self.sib_copy(arr, 2 * i + 1).wait_send()
            self.x_copy(arr, i).wait_send()

        self.each_far(lambda way, dst_row: self.z_copy(arr, way, dst_row, 0).wait_send())


class Total:
    def __init__(self, place, pair, sib, cross, lines, sems):
        self.at, self.pair, self.sib, self.cross, self.lines = place, pair, sib, cross, lines
        self.near_s, self.near_r, self.z_s, self.z_r = sems

    def sib_copy(self, own):
        return remote(own, self.sib, self.near_s.at[0], self.near_r.at[0], self.at.sib)

    def x_copy(self):
        return remote(self.pair, self.cross, self.near_s.at[1], self.near_r.at[1], self.at.across)

    def z_copy(self, way, src_row):
        line = self.lines.at[src_row]
        to = (self.at.seg, self.at.here + 4 - 8 * way)
        return remote(line, line, self.z_s.at[way, src_row], self.z_r.at[src_row], to)

    def cross_over(self, own):
        self.sib_copy(own).wait_recv()
        self.pair[...] = own[...] + self.sib[...]
        self.x_copy().start()

    def along(self):
        self.x_copy().wait_recv()
        self.lines[self.at.row] = self.pair[...] + self.cross[...]
        pl.when(self.at.has_up)(lambda: self.z_copy(0, self.at.row).start())
        pl.when(self.at.has_down)(lambda: self.z_copy(1, self.at.row).start())

    def away(self, dist):
        at = self.at

        @pl.when(at.row - dist >= 0)
        def _():
            src = at.row - dist
            self.z_copy(0, src).wait_recv()
            pl.when(at.has_up)(lambda: self.z_copy(0, src).start())

        @pl.when(at.row + dist < at.rows)
        def _():
            src = at.row + dist
            self.z_copy(1, src).wait_recv()
            pl.when(at.has_down)(lambda: self.z_copy(1, src).start())

    def sent(self, own):
        at = self.at
        self.sib_copy(own).wait_send()
        self.x_copy().wait_send()

        @pl.loop(0, at.rows)
        def _(i):
            pl.when(jnp.logical_and(i <= at.row, at.has_up))(
                lambda: self.z_copy(0, i).wait_send()
            )
            pl.when(jnp.logical_and(i >= at.row, at.has_down))(
                lambda: self.z_copy(1, i).wait_send()
            )


def blocks_body(fused, rows, names, *refs):
    r = dict(zip(names, refs))
    at = Place(rows)
    is_enc = at.seg == 0
    is_dec = at.seg == 1
    x_ref, mask_ref, seg_out, stats = r["x"], r["mask"], r["seg_out"], r["stats"]
    extent = r["extent"]
    w_attn, w_up, w_down = weights = [r["w_attn"], r["w_up"], r["w_down"]]
    norms, maps, h_buf = r["norms"], r["maps"], r["h"]
    a_s, qkv_s, mixed_s, c_s = r["a"], r["qkv"], r["mixed"], r["c"]
    act_s, slope_s, gm_s, go_s, gmix_s = r["act"], r["slope"], r["gm"], r["go"], r["gmix"]
    xhats, rstds = (r["xhat1"], r["xhat2"]), (r["rstd1"], r["rstd2"])
    lse_pack, bias_pack, inner_pack = r["lse_pack"], r["bias_pack"], r["inner_pack"]
    u_s, small_acc, relay_tx, relay_rx = r["u"], r["small_acc"], r["relay_tx"], r["relay_rx"]
    enc_s = gm_s
    total_rows, features = x_ref.shape
    images = h_buf.shape[0]
    patches = total_rows // images
    hidden = w_up.shape[1]
    head_dim = features // HEADS
    pairs = features // 128
    chunk = features
    code_rows = relay_tx.shape[1]

    def rows_of(m):
        return pl.ds(pl.multiple_of(m * patches, patches), patches)

    def cols(j, width):
        return pl.ds(pl.multiple_of(j * width, width), width)

    def relay(m):
        return remote(
            relay_tx.at[m], relay_rx.at[m], r["relay_s"].at[m], r["relay_r"].at[m], at.other
        )

    def result(m):
        return pltpu.make_async_copy(h_buf.at[m], seg_out.at[rows_of(m)], r["out_sem"].at[m])

    def energy(slot, tensor, rs):
        square = row_sum(tensor * tensor * jnp.concatenate([mask_ref[rs, :]] * pairs, axis=1))
        total = square[:, :128]
        for j in range(1, pairs):
            total = total + square[:, j * 128 : (j + 1) * 128]
        stats[slot : slot + 1, :] += total

    def code_mask(array):
        return jnp.where(
            lax.broadcasted_iota(jnp.int32, array.shape, 0) < CODE_BITS, array, 0.0
        )

    def normalize(values, which, rs):
        gain, bias = norms[2 * which : 2 * which + 1, :], norms[2 * which + 1 : 2 * which + 2, :]
        centered = values - row_mean(values)
        scale = lax.rsqrt(row_mean(centered * centered) + norm_eps)
        hat = centered * scale
        xhats[which][rs, :] = low(hat)
        rstds[which][rs, :] = scale
        return low(hat * gain + bias)

    def norm_back(grad, which, rs):
        gain, slot = norms[2 * which : 2 * which + 1, :], code_rows + 2 * which
        hat = wide(xhats[which][rs, :])
        small_acc[slot : slot + 1, :] += row_sum(grad * hat)
        small_acc[slot + 1 : slot + 2, :] += row_sum(grad)
        scaled = grad * gain
        back = scaled - row_mean(scaled) - hat * row_mean(scaled * hat)
        return rstds[which][rs, :] * back

    lane = lax.broadcasted_iota(jnp.int32, (1, 128), 1)
    halves = [low(wide(lane < head_dim)), low(wide(lane >= head_dim))]
    one_lane = low(wide(jnp.broadcast_to(lane == 48, (patches, 128))))

    def head_lanes(head):
        return jnp.logical_and(lane < 48, lax.rem(lane, 16) == head)

    def three_terms(values):
        first = wide(low(values))
        rest = values - first
        second = wide(low(rest))
        third = wide(low(rest - second))
        return jnp.where(lane < 16, first, jnp.where(lane < 32, second, third))

    def attention(m, hooks=()):
        rs = rows_of(m)
        bias_pack[rs, :] = low(jnp.where(lane == 48, (1.0 - mask_ref[rs, :]) * -1e30, 0.0))
        a_s[rs, :] = normalize(h_buf[m], 0, rs)
        for j in range(3):
            part = dot_nn(a_s[rs, :], w_attn[:, j * features : (j + 1) * features])
            if j == 0:
                part = part * (LOG2E / math.sqrt(head_dim))
            qkv_s[rs, j * features : (j + 1) * features] = low(part)

        ones = [jnp.broadcast_to(half, (patches, 128)) for half in halves]

        def heads(j, carry):
            tops, counts = carry
            query = qkv_s[rs, cols(j, 128)]
            key = qkv_s[rs, cols(j + pairs, 128)]
            value = qkv_s[rs, cols(j + 2 * pairs, 128)]
            bias = bias_pack[rs, :]
            keys = beneath([beside([key * half, bias]) for half in halves])
            values = beneath([beside([value * half, one]) for half, one in zip(halves, ones)])
            scores = dot_nt(beside([query, one_lane]), keys)
            parts = [scores[:, :patches], scores[:, patches:]]
            top = [jnp.max(part, -1, keepdims=True) for part in parts]
            weight = beside([low(jnp.exp2(part - peak)) for part, peak in zip(parts, top)])
            found = dot_nn(weight, values)
            count = found[:, 128:]
            mixed_s[rs, cols(j, 128)] = low(found[:, :128] * (1.0 / count))
            first, second = head_lanes(2 * j), head_lanes(2 * j + 1)
            tops = jnp.where(first, top[0], jnp.where(second, top[1], tops))
            turned = pltpu.roll(count, head_dim, 1)
            counts = jnp.where(first, count, jnp.where(second, turned, counts))
            return tops, counts

        carry = (
            jnp.zeros((patches, 128), jnp.float32),
            jnp.ones((patches, 128), jnp.float32),
        )
        if hooks:
            for part in range(3):
                span = (part * pairs // 3, (part + 1) * pairs // 3)
                carry = lax.fori_loop(*span, heads, carry)
                hooks[part]()
        else:
            for j in range(pairs):
                carry = heads(j, carry)
        lse = carry[0] + jnp.log2(carry[1])
        lse_pack[rs, :] = low(
            jnp.where(lane < 48, three_terms(-lse), jnp.where(lane == 48, 1.0, 0.0))
        )
        attn_out = dot_nn(mixed_s[rs, :], w_attn[:, 3 * features : 4 * features])
        energy(1, attn_out, rs)
        h_buf[m] += attn_out
        c_s[rs, :] = normalize(h_buf[m], 1, rs)

    def widen(m):
        rs = rows_of(m)

        def up(j, _):
            pre = dot_nn(c_s[rs, :], w_up[:, cols(j, chunk)])
            phi = 0.5 + 0.5 * lax.erf(pre * math.sqrt(0.5))
            act_s[rs, cols(j, chunk)] = low(pre * phi)
            slope_s[rs, cols(j, chunk)] = low(
                phi + pre * (jnp.exp(-0.5 * pre * pre) * (1.0 / math.sqrt(2.0 * math.pi)))
            )
            return 0

        lax.fori_loop(0, hidden // chunk, up, 0)

    def narrow(m):
        rs = rows_of(m)
        mlp_out = dot_nn(act_s[rs, :hidden], w_down[...])
        energy(2, mlp_out, rs)
        h_buf[m] += mlp_out
        energy(0, h_buf[m], rs)
        stats[3:4, :] += row_sum(mask_ref[rs, :])

    def forward(m, _):
        rs = rows_of(m)

        @pl.when(is_dec)
        def _():
            relay(m).wait_recv()
            h_buf[m] = dot_tn(relay_rx[m], maps[...])
            attention(m)
            widen(m)

        narrow(m)

        @pl.when(is_enc)
        def _():
            enc_s[rs, :] = low(h_buf[m])
            code_pre = code_mask(dot_nt(maps[...], enc_s[rs, :]))
            u_s[m] = code_pre
            scale = lax.rsqrt(row_sum(code_pre * code_pre) + 1.0)
            relay_tx[m] = low(jnp.tanh(2.0 * math.sqrt(CODE_BITS) * (code_pre * scale)))
            relay(m).start()

        pl.when(is_dec)(lambda: result(m).start())
        return 0

    def open_back(m):
        rs = rows_of(m)

        @pl.when(is_enc)
        def _():
            relay(m).wait_recv()
            code_pre = u_s[m]
            scale = lax.rsqrt(row_sum(code_pre * code_pre) + 1.0)
            unit = code_pre * scale
            factor = 2.0 * math.sqrt(CODE_BITS)
            bent = jnp.tanh(factor * unit)
            g_unit = wide(relay_rx[m]) * (factor * (1.0 - bent * bent))
            g_u = low((g_unit - unit * row_sum(g_unit * unit)) * scale)
            small_acc[0:code_rows, :] += dot_nn(g_u, enc_s[rs, :])
            h_buf[m] = dot_tn(g_u, maps[...])

        @pl.when(is_dec)
        def _():
            result(m).wait()
            h_buf[m] = wide(x_ref[rs, :])

    def mlp_back(m):
        rs = rows_of(m)
        gm_s[rs, :] = low(h_buf[m])

        def down(j, _):
            g_act = dot_nt(gm_s[rs, :], w_down[cols(j, chunk), :])
            slope_s[rs, cols(j, chunk)] = low(g_act * wide(slope_s[rs, cols(j, chunk)]))
            return 0

        lax.fori_loop(0, hidden // chunk, down, 0)
        g_c = dot_nt(slope_s[rs, :hidden], w_up[...])
        h_buf[m] += norm_back(g_c, 1, rs)
        go_s[rs, :] = low(h_buf[m])

    def attn_back_open(m):
        rs = rows_of(m)
        gmix_s[...] = low(dot_nt(go_s[rs, :], w_attn[:, 3 * features : 4 * features]))
        product = wide(gmix_s[...]) * wide(mixed_s[rs, :])
        high = low(product)
        head_of = lax.broadcasted_iota(jnp.int32, (features, 128), 0) // head_dim
        lane_of = lax.broadcasted_iota(jnp.int32, (features, 128), 1)
        pick = low(wide(jnp.logical_and(lane_of < 48, lax.rem(lane_of, 16) == head_of)))
        inner = dot_nn(high, pick) + dot_nn(low(product - wide(high)), pick)
        inner_pack[...] = low(three_terms(-inner))

    def attn_back_heads(m, first, last):
        rs = rows_of(m)

        def split(both):
            return beneath([both[:, :patches], both[:, patches:]])

        def front(j):
            query, key, value = [qkv_s[rs, cols(j + i * pairs, 128)] for i in range(3)]
            extra = [bias_pack[rs, :] + low(wide(head_lanes(2 * j + i))) for i in range(2)]
            keys = beneath([beside([key * halves[i], extra[i]]) for i in range(2)])
            values = beneath([beside([value * halves[i], extra[i]]) for i in range(2)])
            probs = jnp.exp2(dot_nt(beside([query, lse_pack[rs, :]]), keys))
            g_probs = dot_nt(beside([gmix_s[:, cols(j, 128)], inner_pack[...]]), values)
            return low(probs * g_probs), low(probs)

        def back(j, g_scores, probs):
            places = [cols(j + i * pairs, 128) for i in range(3)]
            query, key = qkv_s[rs, places[0]], qkv_s[rs, places[1]]
            g_mixed = gmix_s[:, cols(j, 128)]
            g_query = dot_nn(g_scores, beneath([key * half for half in halves]))
            g_key = dot_tn(split(g_scores), beneath([query * half for half in halves]))
            g_value = dot_tn(split(probs), beneath([g_mixed * half for half in halves]))
            qkv_s[rs, places[0]] = low(g_query * (1.0 / math.sqrt(head_dim)))
            qkv_s[rs, places[1]] = low(g_key * (1.0 / LOG2E))
            qkv_s[rs, places[2]] = low(g_value)

        ready = front(first)
        for j in range(first, last):
            after = front(j + 1) if j + 1 < last else None
            back(j, *ready)
            ready = after

    def attn_back_close(m):
        rs = rows_of(m)
        g_a = dot_nt(qkv_s[rs, :], w_attn[:, : 3 * features])
        h_buf[m] += norm_back(g_a, 0, rs)

    def close_back(m):
        rs = rows_of(m)

        @pl.when(is_enc)
        def _():
            result(m).start()

        @pl.when(is_dec)
        def _():
            g_z = low(h_buf[m])
            small_acc[0:code_rows, :] += dot_nn(relay_rx[m], g_z)
            relay_tx[m] = low(code_mask(dot_nt(maps[...], g_z)))
            relay(m).start()

    def attn_back(m):
        attn_back_open(m)
        attn_back_heads(m, 0, pairs)
        attn_back_close(m)

    def fill_mask():
        patch = lax.broadcasted_iota(jnp.int32, (patches, 128), 0).astype(jnp.float32)
        for m in range(images):
            wide_grid = extent[m, 0] == 0
            length = jnp.where(wide_grid, float(GW), float(GH))
            line = jnp.floor((patch + 0.5) * jnp.where(wide_grid, 1.0 / GW, 1.0 / GH))
            inside = jnp.logical_and(
                line < extent[m, 1].astype(jnp.float32),
                patch - line * length < extent[m, 2].astype(jnp.float32),
            )
            mask_ref[m * patches : (m + 1) * patches, :] = wide(inside)

    def pack_small():
        maps_in = r["maps_in"][...]
        vectors = beneath([r["norm%d_in" % i][...] for i in range(4)])

        def lanes(count, start):
            row_no = lax.broadcasted_iota(jnp.int32, (count, 128), 0)
            return low(wide(lax.broadcasted_iota(jnp.int32, (count, 128), 1) == row_no + start))

        return low(
            dot_nn(maps_in, lanes(CODE_BITS, 0)) + dot_tn(vectors, lanes(4, CODE_BITS))
        )

    def take_small():
        small = wide(w_attn[:, 4 * features :]).T
        maps[...] = low(code_mask(small[:code_rows]))
        norms[0:4, :] = small[CODE_BITS : CODE_BITS + 4]

    def start_image(m):
        h_buf[m] = wide(x_ref[rows_of(m), :])

    def up_grads():
        for j in range(hidden // chunk):
            place = slice(j * chunk, (j + 1) * chunk)
            w_up[:, place] = low(dot_tn(c_s[...], slope_s[:, place]))

    def attn_grads():
        for j in range(3):
            place = slice(j * features, (j + 1) * features)
            w_attn[:, place] = low(dot_tn(a_s[...], qkv_s[:, place]))
        w_attn[:, 3 * features : 4 * features] = low(dot_tn(mixed_s[...], go_s[...]))
        small_grad = jnp.concatenate(
            [
                small_acc[0:CODE_BITS, :],
                small_acc[code_rows : code_rows + 4, :],
                jnp.zeros((128 - CODE_BITS - 4, features), jnp.float32),
            ],
            axis=0,
        )
        w_attn[:, 4 * features :] = low(small_grad.T)

    def fresh():
        fill_mask()
        stats[...] = jnp.zeros_like(stats)
        small_acc[...] = jnp.zeros_like(small_acc)

    def before_relay():
        @pl.when(is_dec)
        def _():
            stats[...] = jnp.zeros_like(stats)

    if not fused:
        copies = [
            pltpu.make_async_copy(r[name], weights[arr], r["own_sem"].at[arr])
            for arr, name in enumerate(("attn_all", "up_all", "down_all"))
        ]
        for copy in copies:
            copy.start()
        fresh()
        at.meet(False)
        for copy in copies:
            copy.wait()
        take_small()
        for m in range(images):
            start_image(m)
            attention(m)
            widen(m)
        before_relay()
        lax.fori_loop(0, images, forward, 0)
        for m in reversed(range(images)):
            open_back(m)
            mlp_back(m)
            attn_back(m)
            close_back(m)
        w_down[...] = low(dot_tn(act_s[:, :hidden], gm_s[...]))
        up_grads()
        attn_grads()
        for arr, name in enumerate(("g_attn", "g_up", "g_down")):
            copy = pltpu.make_async_copy(weights[arr], r[name], r["own_sem"].at[arr])
            copy.start()
            copy.wait()
        for m in range(images):
            pl.when(is_enc)(lambda: result(m).wait())
            relay(m).wait_send()
        return

    heights = (r["qkv_in"].shape[0], r["up_in"].shape[0], r["down_in"].shape[0])
    own_rows = [
        pl.ds(pl.multiple_of(at.here * height, height), height) for height in heights
    ]
    own_copies = [
        pltpu.make_async_copy(src, dst, r["own_sem"].at[i])
        for i, (src, dst) in enumerate(
            (
                (r["qkv_in"], w_attn.at[own_rows[ATTN], pl.ds(0, 3 * features)]),
                (r["out_in"], w_attn.at[own_rows[ATTN], pl.ds(3 * features, features)]),
                (r["up_in"], w_up.at[own_rows[UP]]),
                (r["down_in"], w_down.at[own_rows[DOWN]]),
            )
        )
    ]
    gather = Gather(at, weights, heights, r["g_send"], r["g_recv"])
    scatter = Scatter(
        at,
        weights,
        heights,
        (act_s, r["sib_u"], r["sib_d"]),
        (act_s, r["x_u"], r["x_d"]),
        (slope_s, r["z_u"], r["z_d"]),
        [r[name] for name in ("sib_s", "sib_r", "x_s", "x_r", "z_s", "z_r")],
    )
    total = Total(
        at,
        r["t_pair"],
        r["t_sib"],
        r["t_cross"],
        r["t_lines"],
        [r[name] for name in ("t_near_s", "t_near_r", "t_z_s", "t_z_r")],
    )
    for copy in own_copies:
        copy.start()
    at.meet(True)
    w_attn[own_rows[ATTN], 4 * features :] = pack_small()
    for copy in own_copies[:2]:
        copy.wait()
    gather.own(ATTN)
    fresh()
    scatter.clear(UP)
    scatter.clear(DOWN)
    for m in range(images):
        start_image(m)
    gather.away(ATTN, 1)
    gather.away(ATTN, 2)
    own_copies[2].wait()
    gather.own(UP)
    gather.away(ATTN, 3)
    gather.crossed(ATTN)
    gather.away(UP, 1)
    gather.paired(ATTN)
    take_small()

    def own_down():
        own_copies[3].wait()
        gather.own(DOWN)

    attention(0, [lambda: gather.away(UP, 2), own_down, lambda: gather.away(UP, 3)])
    attention(
        1,
        [
            lambda: gather.away(DOWN, 1),
            lambda: gather.away(DOWN, 2),
            lambda: gather.crossed(UP),
        ],
    )
    gather.away(DOWN, 3)
    gather.paired(UP)
    for m in range(images):
        widen(m)
    gather.crossed(DOWN)
    gather.paired(DOWN)
    for arr in range(3):
        gather.sent(arr)
    before_relay()
    lax.fori_loop(0, images, forward, 0)
    total.sib_copy(stats).start()

    def backward(step, _):
        m = images - 1 - step
        open_back(m)
        mlp_back(m)

        @pl.when(jnp.logical_or(is_dec, m > 0))
        def _():
            attn_back(m)
            close_back(m)

        return 0

    lax.fori_loop(0, images, backward, 0)
    total.cross_over(stats)

    def down_block(pair):
        span = 2 * heights[DOWN]
        place = pl.ds(pl.multiple_of(pair * span, span), span)
        w_down[place, :] = low(dot_tn(act_s[:, place], gm_s[...]))
        scatter.sib_copy(DOWN, pair).start()

    scatter.each_far(lambda way, dst_row: down_block(2 * dst_row + 1 - at.col))
    down_block(2 * at.row + 1 - at.col)
    scatter.x_stage(DOWN)
    total.along()
    scatter.each_far(lambda way, dst_row: down_block(2 * dst_row + at.col))
    down_block(2 * at.row + at.col)
    up_grads()
    total.away(1)
    scatter.start_pairs(UP)
    scatter.x_stage(UP)
    total.away(2)
    pl.when(is_enc)(lambda: attn_back_open(0))
    for part in range(3):
        pl.when(is_enc)(
            lambda: attn_back_heads(0, part * pairs // 3, (part + 1) * pairs // 3)
        )
        scatter.z_stage(DOWN, [3 - part])

    @pl.when(is_enc)
    def _():
        attn_back_close(0)
        close_back(0)

    attn_grads()
    scatter.start_pairs(ATTN)
    scatter.z_stage(UP, [3, 2])
    scatter.clear(ATTN)
    scatter.x_stage(ATTN)
    total.away(3)
    sums = total.lines[0]
    for i in range(1, rows):
        sums = sums + total.lines[i]
    sums = jnp.sum(sums, -1, keepdims=True)
    scale = 128.0 / (sums[3:4] * features)
    found = jnp.sqrt(sums * scale)
    row_no = lax.broadcasted_iota(jnp.int32, (8, 128), 0)
    lane_no = lax.broadcasted_iota(jnp.int32, (8, 128), 1)
    r["rms"][...] = row_sum(jnp.where(row_no == lane_no, found, 0.0))[:, :3]
    r["down_out"][...] = scatter.final(DOWN)
    scatter.z_stage(UP, [1])
    r["up_out"][...] = scatter.final(UP)
    scatter.z_stage(ATTN)
    last = scatter.final(ATTN)
    r["qkv_out"][...] = last[:, : 3 * features]
    r["out_out"][...] = last[:, 3 * features : 4 * features]
    small = last[:, 4 * features :]
    r["maps_out"][...] = small[:, :CODE_BITS]
    small = jnp.concatenate(
        [small, jnp.zeros((128 - small.shape[0], 128), jnp.float32)], axis=0
    ).T
    for i in range(4):
        r["norm%d_out" % i][...] = small[CODE_BITS + i : CODE_BITS + i + 1, : heights[ATTN]]
    for m in range(images):
        pl.when(is_enc)(lambda: result(m).wait())
        relay(m).wait_send()
    for arr in range(3):
        scatter.sent(arr)
    total.sent(stats)


def run_blocks(fused, operands, x, extent, rows):
    images, patches, features = x.shape
    total = images * patches
    hidden = 4 * features
    attn_width = 4 * features + 128
    code_rows = -(-CODE_BITS // 16) * 16
    bf16, f32 = jnp.bfloat16, jnp.float32
    any_spec = pl.BlockSpec(memory_space=pl.ANY)
    vmem_spec = pl.BlockSpec(memory_space=pltpu.VMEM)
    dma = pltpu.SemaphoreType.DMA
    ins = dict(operands, x=x.reshape(total, features), extent=extent)
    outs = {"seg_out": ((total, features), f32)}
    full = {"a": (features, attn_width), "u": (features, hidden), "d": (hidden, features)}
    buffers = {
        "w_attn": (full["a"], bf16), "w_up": (full["u"], bf16), "w_down": (full["d"], bf16),
        "mask": ((total, 128), f32),
        "norms": ((8, features), f32), "maps": ((code_rows, features), bf16),
        "h": ((images, patches, features), f32),
        "xhat1": ((total, features), bf16), "rstd1": ((total, 1), f32),
        "xhat2": ((total, features), bf16), "rstd2": ((total, 1), f32),
        "a": ((total, features), bf16), "qkv": ((total, 3 * features), bf16),
        "mixed": ((total, features), bf16), "c": ((total, features), bf16),
        "act": ((total, attn_width), bf16), "slope": ((total, attn_width), bf16),
        "lse_pack": ((total, 128), bf16), "bias_pack": ((total, 128), bf16),
        "inner_pack": ((patches, 128), bf16),
        "gm": ((total, features), bf16), "go": ((total, features), bf16),
        "gmix": ((patches, features), bf16),
        "u": ((images, code_rows, patches), f32), "small_acc": ((code_rows + 8, features), f32),
        "relay_tx": ((images, code_rows, patches), bf16),
        "relay_rx": ((images, code_rows, patches), bf16),
    }
    sems = {"relay_s": (images,), "relay_r": (images,), "out_sem": (images,)}
    in_vmem = ["x", "maps_in", *("norm%d_in" % i for i in range(4))]
    smem_spec = pl.BlockSpec(memory_space=pltpu.SMEM)
    if fused:
        outs["rms"] = ((1, 3), f32)
        shards = {
            "a": (operands["qkv_in"].shape[0], attn_width),
            "u": operands["up_in"].shape,
            "d": operands["down_in"].shape,
        }
        outs["qkv_out"] = (operands["qkv_in"].shape, f32)
        outs["out_out"] = (operands["out_in"].shape, f32)
        outs["up_out"] = (shards["u"], f32)
        outs["down_out"] = (shards["d"], f32)
        outs["maps_out"] = ((shards["a"][0], CODE_BITS), f32)
        for i in range(4):
            outs["norm%d_out" % i] = ((1, shards["a"][0]), f32)
        buffers["stats"] = ((8, 128), f32)
        for name, shape in shards.items():
            if name != "a":
                buffers["sib_" + name] = ((2 * rows,) + shape, bf16)
                buffers["x_" + name] = ((rows,) + shape, bf16)
                buffers["z_" + name] = ((rows + 1,) + shape, bf16)
        for name in ("t_pair", "t_sib", "t_cross"):
            buffers[name] = ((8, 128), f32)
        buffers["t_lines"] = ((rows, 8, 128), f32)
        sems.update(
            own_sem=(4,), g_send=(3, 5 * rows), g_recv=(3, 4 * rows),
            sib_s=(3, 2 * rows), sib_r=(3, 2 * rows), x_s=(3, rows), x_r=(3, rows),
            z_s=(3, rows), z_r=(3, rows + 1),
            t_near_s=(2,), t_near_r=(2,), t_z_s=(2, rows), t_z_r=(rows,),
        )
    else:
        outs["g_attn"] = (full["a"], bf16)
        outs["g_up"] = (full["u"], bf16)
        outs["g_down"] = (full["d"], bf16)
        outs["stats"] = ((8, 128), f32)
        sems["own_sem"] = (3,)
    names = [*ins, *outs, *buffers, *sems]
    out_any = ("seg_out", "g_attn", "g_up", "g_down")
    found = pl.pallas_call(
        partial(blocks_body, fused, rows, names),
        out_shape=tuple(jax.ShapeDtypeStruct(s, t) for s, t in outs.values()),
        in_specs=[
            vmem_spec if n in in_vmem else smem_spec if n == "extent" else any_spec for n in ins
        ],
        out_specs=tuple(any_spec if n in out_any else vmem_spec for n in outs),
        scratch_shapes=[pltpu.VMEM(s, t) for s, t in buffers.values()]
        + [dma(s) for s in sems.values()],
        compiler_params=pltpu.CompilerParams(
            collective_id=1, has_side_effects=True, vmem_limit_bytes=VMEM_BYTES
        ),
        name="both_blocks",
    )(*ins.values())
    return dict(zip(outs, found))


def hand_over_body(count, *refs):
    steps = [refs[i * count : (i + 1) * count] for i in range(3)]
    sems = refs[3 * count :]
    copies = [
        [pltpu.make_async_copy(src, dst, sem.at[i]) for i, (src, dst) in enumerate(zip(*pair))]
        for pair, sem in zip(((steps[0], steps[2]), (steps[2], steps[1])), sems)
    ]
    for copy in copies[0]:
        copy.start()
    for copy, after in zip(*copies):
        copy.wait()
        after.start()
    for copy in copies[1]:
        copy.wait()


def hand_over(arrays):
    any_spec = pl.BlockSpec(memory_space=pl.ANY)
    return pl.pallas_call(
        partial(hand_over_body, len(arrays)),
        out_shape=tuple(jax.ShapeDtypeStruct(v.shape, v.dtype) for v in arrays),
        in_specs=[any_spec] * len(arrays),
        out_specs=(any_spec,) * len(arrays),
        scratch_shapes=[pltpu.VMEM(v.shape, v.dtype) for v in arrays]
        + [pltpu.SemaphoreType.DMA((len(arrays),))] * 2,
        name="hand_over",
    )(*arrays)


def on_device(
    segment_input,
    image_extent,
    norm1_gain,
    norm1_bias,
    norm2_gain,
    norm2_bias,
    qkv_weight,
    out_weight,
    up_weight,
    down_weight,
    code_maps,
):
    _, images, patches, features = segment_input.shape
    qkv_width = qkv_weight.shape[2]
    count = lax.axis_size("dp")
    x = segment_input[0]
    if qkv_weight.shape[1] % 16 == 0 and count % 4 == 0:
        operands = {
            "qkv_in": qkv_weight[0],
            "out_in": out_weight[0],
            "maps_in": code_maps[0],
            "norm0_in": norm1_gain,
            "norm1_in": norm1_bias,
            "norm2_in": norm2_gain,
            "norm3_in": norm2_bias,
            "up_in": up_weight[0],
            "down_in": down_weight[0],
        }
        found = run_blocks(True, operands, x, image_extent, count // 4)
        names = ["seg_out", "rms", *("norm%d_out" % i for i in range(4))]
        names += ["qkv_out", "out_out", "up_out", "down_out", "maps_out"]
        results = hand_over([found[name] for name in names])
    else:
        small = jnp.concatenate(
            [code_maps[0]]
            + [v[0][:, None] for v in (norm1_gain, norm1_bias, norm2_gain, norm2_bias)],
            axis=1,
        )
        small = jnp.pad(small, ((0, 0), (0, 128 - small.shape[1])))
        attn = jnp.concatenate([qkv_weight[0], out_weight[0], small], axis=1)
        operands = {
            name: lax.all_gather(shard, "dp", axis=0, tiled=True)
            for name, shard in (
                ("attn_all", attn),
                ("up_all", up_weight[0]),
                ("down_all", down_weight[0]),
            )
        }
        found = run_blocks(False, operands, x, image_extent, 1)
        attn_shard, up_shard, down_shard = [
            lax.psum_scatter(
                found[name].astype(jnp.float32), "dp", scatter_dimension=0, tiled=True
            )
            for name in ("g_attn", "g_up", "g_down")
        ]
        stats = lax.psum(found["stats"], "dp")
        rms_stats = jnp.sqrt(jnp.sum(stats[:3], 1) / (stats[3, 0] * features))[None]
        small_shard = attn_shard[:, qkv_width + features :]
        results = [
            found["seg_out"],
            rms_stats,
            *(small_shard[:, CODE_BITS + i][None] for i in range(4)),
            attn_shard[:, :qkv_width],
            attn_shard[:, qkv_width : qkv_width + features],
            up_shard,
            down_shard,
            small_shard[:, :CODE_BITS],
        ]
    return (
        results[0].reshape(segment_input.shape),
        *results[1:6],
        *(v[None] for v in results[6:]),
    )


def solution(mesh):
    return jax.shard_map(
        on_device,
        mesh=mesh,
        in_specs=(
            P("segment", "dp", None, None),
            P("dp", None),
            P("segment", "dp"),
            P("segment", "dp"),
            P("segment", "dp"),
            P("segment", "dp"),
            P("segment", "dp", None),
            P("segment", "dp", None),
            P("segment", "dp", None),
            P("segment", "dp", None),
            P("segment", "dp", None),
        ),
        out_specs=(
            P("segment", "dp", None, None),
            P("segment", None),
            P("segment", "dp"),
            P("segment", "dp"),
            P("segment", "dp"),
            P("segment", "dp"),
            P("segment", "dp", None),
            P("segment", "dp", None),
            P("segment", "dp", None),
            P("segment", "dp", None),
            P("segment", "dp", None),
        ),
        check_vma=False,
    )
```

```python
from functools import partial
import math

import jax
import jax.numpy as jnp
from jax import lax
from jax.experimental import pallas as pl
from jax.experimental.pallas import tpu as pltpu
from jax.sharding import PartitionSpec as P

HEADS = 12
CODE_BITS = 18
GH = 16
GW = 24
LOG2E = math.log2(math.e)
VMEM_BYTES = 62 << 20


norm_eps = 1e-06


MESH_ID = pl.DeviceIdType.MESH
ATTN, UP, DOWN, REST = 0, 1, 2, 3


def dot_nn(left, right):
    return lax.dot_general(left, right, (((1,), (0,)), ((), ())), preferred_element_type=jnp.float32)


def dot_nt(left, right):
    return lax.dot_general(left, right, (((1,), (1,)), ((), ())), preferred_element_type=jnp.float32)


def dot_tn(left, right):
    return lax.dot_general(left, right, (((0,), (0,)), ((), ())), preferred_element_type=jnp.float32)


def low(array):
    return array.astype(jnp.bfloat16)


def wide(array):
    return array.astype(jnp.float32)


def beside(arrays):
    return jnp.concatenate(arrays, axis=1)


def beneath(arrays):
    return jnp.concatenate(arrays, axis=0)


def row_sum(array):
    return jnp.sum(array, 0, keepdims=True)


def row_mean(array):
    return jnp.mean(array, -1, keepdims=True)


def remote(src, dst, ssem, rsem, to):
    return pltpu.make_async_remote_copy(
        src_ref=src,
        dst_ref=dst,
        send_sem=ssem,
        recv_sem=rsem,
        device_id=to,
        device_id_type=MESH_ID,
    )


class Place:
    def __init__(self, rows):
        self.rows = rows
        self.seg = lax.axis_index("segment")
        self.here = lax.axis_index("dp")
        self.core = lax.rem(self.here, 2)
        self.col = lax.rem(self.here // 2, 2)
        self.row = self.here // 4
        self.sib = (self.seg, self.here + 1 - 2 * self.core)
        self.across = (self.seg, self.here + 2 - 4 * self.col)
        self.up = (self.seg, self.here + 4)
        self.down = (self.seg, self.here - 4)
        self.other = (1 - self.seg, self.here)
        self.has_up = self.row < rows - 1
        self.has_down = self.row > 0

    def meet(self, in_plane):
        barrier = pltpu.get_barrier_semaphore()

        def greet(to):
            pl.semaphore_signal(barrier, inc=1, device_id=to, device_id_type=MESH_ID)

        greet(self.other)
        if not in_plane:
            pl.semaphore_wait(barrier, 1)
            return
        greet(self.sib)
        greet(self.across)
        pl.when(self.has_up)(lambda: greet(self.up))
        pl.when(self.has_down)(lambda: greet(self.down))
        both = jnp.logical_and(self.has_up, self.has_down)
        pl.semaphore_wait(barrier, jnp.where(both, 5, 4))


class Blocks:
    def __init__(self, ref, stride, first, height, split):
        self.ref, self.stride, self.first, self.height = ref, stride, first, height
        self.split = split

    def of(self, device):
        start = pl.multiple_of(device * self.stride + self.first, self.height)
        return self.ref.at[pl.ds(start, self.height)]


class Gather:
    def __init__(self, place, arrays, send_sem, recv_sem):
        self.at, self.arrays = place, arrays
        self.send_sem, self.recv_sem = send_sem, recv_sem

    def copy(self, arr, src, slot, to):
        block = self.arrays[arr].of(src)
        return remote(block, block, self.send_sem.at[arr, slot], self.recv_sem.at[arr, src], to)

    def sender(self, arr, src_row, src_col, way, to):
        pair = src_row * 2 + src_col
        return self.copy(arr, pair * 2 + self.at.core, 2 * self.at.rows * way + pair, to)

    def to_up(self, arr, src_row, src_col):
        return self.sender(arr, src_row, src_col, 0, self.at.up)

    def to_down(self, arr, src_row, src_col):
        return self.sender(arr, src_row, src_col, 1, self.at.down)

    def to_sib(self, arr, src_row, src_col):
        return self.sender(arr, src_row, src_col, 2, self.at.sib)

    def to_across(self, arr, src_row):
        return self.sender(arr, src_row, self.at.col, 3, self.at.across)

    def arrive(self, arr, src_row, src_col):
        self.sender(arr, src_row, src_col, 0, self.at.sib).wait_recv()

    def along(self, arr, src_col):
        row = self.at.row
        pl.when(self.at.has_up)(lambda: self.to_up(arr, row, src_col).start())
        pl.when(self.at.has_down)(lambda: self.to_down(arr, row, src_col).start())
        self.to_sib(arr, row, src_col).start()

    def own_across(self, arr):
        self.to_across(arr, self.at.row).start()

    def own(self, arr):
        self.along(arr, self.at.col)
        if not self.arrays[arr].split:
            self.own_across(arr)

    def turn(self, arr):
        self.arrive(arr, self.at.row, 1 - self.at.col)
        self.along(arr, 1 - self.at.col)

    def away(self, arr, dist):
        at = self.at
        split = self.arrays[arr].split

        def one(src_row, src_col, forward, more):
            self.arrive(arr, src_row, src_col)
            pl.when(more)(lambda: forward(arr, src_row, src_col).start())
            if not split:
                self.to_across(arr, src_row).start()
            self.to_sib(arr, src_row, src_col).start()

        for src_col in (at.col, 1 - at.col)[: 2 if split else 1]:
            pl.when(at.row - dist >= 0)(
                lambda: one(at.row - dist, src_col, self.to_up, at.has_up)
            )
            pl.when(at.row + dist < at.rows)(
                lambda: one(at.row + dist, src_col, self.to_down, at.has_down)
            )

    def crossed(self, arr):
        at = self.at

        def one(src):
            self.arrive(arr, src, 1 - at.col)
            self.to_sib(arr, src, 1 - at.col).start()

        one(at.row)
        for dist in range(1, at.rows):
            pl.when(at.row - dist >= 0)(lambda: one(at.row - dist))
            pl.when(at.row + dist < at.rows)(lambda: one(at.row + dist))

    def paired(self, arr):
        @pl.loop(0, 2 * self.at.rows)
        def _(i):
            self.copy(arr, 2 * i + 1 - self.at.core, 0, self.at.sib).wait_recv()

    def sent(self, arr):
        at = self.at

        @pl.loop(0, at.rows)
        def _(i):
            self.to_sib(arr, i, 0).wait_send()
            self.to_sib(arr, i, 1).wait_send()
            if not self.arrays[arr].split:
                self.to_across(arr, i).wait_send()
            for src_col in (at.col, 1 - at.col)[: 2 if self.arrays[arr].split else 1]:
                pl.when(jnp.logical_and(i <= at.row, at.has_up))(
                    lambda: self.to_up(arr, i, src_col).wait_send()
                )
                pl.when(jnp.logical_and(i >= at.row, at.has_down))(
                    lambda: self.to_down(arr, i, src_col).wait_send()
                )

        if self.arrays[arr].split:
            self.to_across(arr, at.row).wait_send()


class Scatter:
    def __init__(self, place, arrays, sibs, crosses, lines, sems):
        self.at, self.arrays = place, arrays
        self.sibs, self.crosses, self.lines = sibs, crosses, lines
        self.sib_s, self.sib_r, self.x_s, self.x_r, self.z_s, self.z_r = sems

    def mine(self, arr, pair):
        return self.arrays[arr].of(2 * pair + self.at.core)

    def from_sib(self, arr, pair):
        return self.slot(self.sibs, arr, pair)

    def from_across(self, arr, dst_row):
        return self.slot(self.crosses, arr, dst_row + (2 * self.at.rows if arr == ATTN else 0))

    def from_line(self, arr, slot):
        return self.slot(self.lines, arr, slot)

    def slot(self, buffers, arr, slot):
        if arr != ATTN:
            return buffers[arr].at[slot]
        height = self.arrays[arr].height
        return buffers[arr].at[pl.ds(pl.multiple_of(slot * height, height), height)]

    def sib_copy(self, arr, pair):
        return remote(
            self.arrays[arr].of(2 * pair + 1 - self.at.core),
            self.from_sib(arr, pair),
            self.sib_s.at[arr, pair],
            self.sib_r.at[arr, pair],
            self.at.sib,
        )

    def x_copy(self, arr, dst_row):
        slot = 0 if self.arrays[arr].split else dst_row
        return remote(
            self.mine(arr, 2 * dst_row + 1 - self.at.col),
            self.from_across(arr, slot),
            self.x_s.at[arr, slot],
            self.x_r.at[arr, slot],
            self.at.across,
        )

    def z_slot(self, arr, way, dst_row, dst_col, to_row):
        slot = jnp.where(jnp.logical_and(way == 1, dst_row == to_row), self.at.rows, dst_row)
        return slot + (self.at.rows + 1) * dst_col if self.arrays[arr].split else slot

    def z_copy(self, arr, way, dst_row, dst_col, slot):
        pair = 2 * dst_row + dst_col
        return remote(
            self.mine(arr, pair),
            self.from_line(arr, slot),
            self.z_s.at[arr, pair],
            self.z_r.at[arr, slot],
            (self.at.seg, self.at.here + 4 - 8 * way),
        )

    def each_far(self, body, dists=None):
        at = self.at
        for dist in dists or range(at.rows - 1, 0, -1):

            @pl.loop(0, 2)
            def _(way):
                dst_row = at.row + (1 - 2 * way) * dist
                pl.when(jnp.logical_and(dst_row >= 0, dst_row < at.rows))(
                    lambda: body(way, dst_row)
                )

    def clear(self, arr):
        rows = self.at.rows

        def zero(slot):
            for more in range(2 if self.arrays[arr].split else 1):
                place = self.from_line(arr, slot + more * (rows + 1))
                place[...] = jnp.zeros(place.shape, jnp.bfloat16)

        @pl.when(jnp.logical_not(self.at.has_down))
        def _():
            for slot in range(rows):
                zero(slot)

        @pl.when(jnp.logical_not(self.at.has_up))
        def _():
            for slot in [*range(rows - 1), rows]:
                zero(slot)

    def start_pairs(self, arr):
        def go(dst_row, at_col):
            self.sib_copy(arr, 2 * dst_row + at_col).start()

        self.each_far(lambda way, dst_row: go(dst_row, 1 - self.at.col))
        go(self.at.row, 1 - self.at.col)
        self.each_far(lambda way, dst_row: go(dst_row, self.at.col))
        go(self.at.row, self.at.col)

    def pair_sum(self, arr, pair):
        self.sib_copy(arr, pair).wait_recv()
        return wide(self.mine(arr, pair)[...]) + wide(self.from_sib(arr, pair)[...])

    def x_one(self, arr, dst_row):
        pair = 2 * dst_row + 1 - self.at.col
        self.mine(arr, pair)[...] = low(self.pair_sum(arr, pair))
        self.x_copy(arr, dst_row).start()

    def x_stage(self, arr):
        self.each_far(lambda way, dst_row: self.x_one(arr, dst_row))
        self.x_one(arr, self.at.row)

    def crossed(self, arr, dst_row):
        self.x_copy(arr, dst_row).wait_recv()
        return wide(self.from_across(arr, 0 if self.arrays[arr].split else dst_row)[...])

    def z_stage(self, arr, dists):
        at = self.at
        split = self.arrays[arr].split

        def go(way, dst_row, dst_col):
            behind = at.row - 1 + 2 * way
            slot = self.z_slot(arr, way, dst_row, dst_col, at.row)

            @pl.when(jnp.logical_and(behind >= 0, behind < at.rows))
            def _():
                self.z_copy(arr, way, dst_row, dst_col, slot).wait_recv()

            total = self.pair_sum(arr, 2 * dst_row + dst_col)
            if not split:
                total = total + self.crossed(arr, dst_row)
            total = total + wide(self.from_line(arr, slot)[...])
            self.mine(arr, 2 * dst_row + dst_col)[...] = low(total)
            slot = self.z_slot(arr, way, dst_row, dst_col, at.row + 1 - 2 * way)
            self.z_copy(arr, way, dst_row, dst_col, slot).start()

        if not split:
            self.each_far(lambda way, dst_row: go(way, dst_row, at.col), dists)
            return

        def both(way, dst_row):
            @pl.loop(0, 2)
            def _(dst_col):
                go(way, dst_row, dst_col)

        self.each_far(both, dists)

    def lines_end(self, arr, dst_col):
        at = self.at
        slots = [self.z_slot(arr, way, at.row, dst_col, at.row) for way in range(2)]
        for way, has in enumerate((at.has_down, at.has_up)):
            pl.when(has)(
                lambda: self.z_copy(arr, way, at.row, dst_col, slots[way]).wait_recv()
            )
        total = self.pair_sum(arr, 2 * at.row + dst_col)
        return total + sum(wide(self.from_line(arr, slot)[...]) for slot in slots)

    def turn(self, arr):
        at = self.at
        total = self.lines_end(arr, 1 - at.col)
        self.mine(arr, 2 * at.row + 1 - at.col)[...] = low(total)
        self.x_copy(arr, at.row).start()

    def final(self, arr):
        return self.lines_end(arr, self.at.col) + self.crossed(arr, self.at.row)

    def sent(self, arr):
        split = self.arrays[arr].split

        @pl.loop(0, self.at.rows)
        def _(i):
            self.sib_copy(arr, 2 * i).wait_send()
            self.sib_copy(arr, 2 * i + 1).wait_send()
            if not split:
                self.x_copy(arr, i).wait_send()

        if split:
            self.x_copy(arr, self.at.row).wait_send()

        def lines(way, dst_row):
            for dst_col in (self.at.col, 1 - self.at.col)[: 2 if split else 1]:
                self.z_copy(arr, way, dst_row, dst_col, 0).wait_send()

        self.each_far(lines)


class Total:
    def __init__(self, place, pair, sib, cross, lines, sems):
        self.at, self.pair, self.sib, self.cross, self.lines = place, pair, sib, cross, lines
        self.near_s, self.near_r, self.z_s, self.z_r = sems

    def sib_copy(self, own):
        return remote(own, self.sib, self.near_s.at[0], self.near_r.at[0], self.at.sib)

    def x_copy(self):
        return remote(self.pair, self.cross, self.near_s.at[1], self.near_r.at[1], self.at.across)

    def z_copy(self, way, src_row):
        line = self.lines.at[src_row]
        to = (self.at.seg, self.at.here + 4 - 8 * way)
        return remote(line, line, self.z_s.at[way, src_row], self.z_r.at[src_row], to)

    def cross_over(self, own):
        self.sib_copy(own).wait_recv()
        self.pair[...] = own[...] + self.sib[...]
        self.x_copy().start()

    def along(self):
        self.x_copy().wait_recv()
        self.lines[self.at.row] = self.pair[...] + self.cross[...]
        pl.when(self.at.has_up)(lambda: self.z_copy(0, self.at.row).start())
        pl.when(self.at.has_down)(lambda: self.z_copy(1, self.at.row).start())

    def away(self, dist):
        at = self.at

        @pl.when(at.row - dist >= 0)
        def _():
            src = at.row - dist
            self.z_copy(0, src).wait_recv()
            pl.when(at.has_up)(lambda: self.z_copy(0, src).start())

        @pl.when(at.row + dist < at.rows)
        def _():
            src = at.row + dist
            self.z_copy(1, src).wait_recv()
            pl.when(at.has_down)(lambda: self.z_copy(1, src).start())

    def sent(self, own):
        at = self.at
        self.sib_copy(own).wait_send()
        self.x_copy().wait_send()

        @pl.loop(0, at.rows)
        def _(i):
            pl.when(jnp.logical_and(i <= at.row, at.has_up))(
                lambda: self.z_copy(0, i).wait_send()
            )
            pl.when(jnp.logical_and(i >= at.row, at.has_down))(
                lambda: self.z_copy(1, i).wait_send()
            )


def blocks_body(fused, rows, names, *refs):
    r = dict(zip(names, refs))
    at = Place(rows)
    is_enc = at.seg == 0
    is_dec = at.seg == 1
    x_ref, mask_ref, seg_out, stats = r["x"], r["mask"], r["seg_out"], r["stats"]
    extent = r["extent"]
    w_attn, w_up, w_down = weights = [r["w_attn"], r["w_up"], r["w_down"]]
    norms, maps, h_buf = r["norms"], r["maps"], r["h"]
    a_s, qkv_s, mixed_s, c_s = r["a"], r["qkv"], r["mixed"], r["c"]
    act_s, slope_s, gm_s, go_s, gmix_s = r["act"], r["slope"], r["gm"], r["go"], r["gmix"]
    xhats, rstds = (r["xhat1"], r["xhat2"]), (r["rstd1"], r["rstd2"])
    lse_pack, bias_pack, inner_pack = r["lse_pack"], r["bias_pack"], r["inner_pack"]
    u_s, small_acc, relay_tx, relay_rx = r["u"], r["small_acc"], r["relay_tx"], r["relay_rx"]
    enc_s = gm_s
    total_rows, features = x_ref.shape
    images = h_buf.shape[0]
    patches = total_rows // images
    hidden = w_up.shape[1]
    head_dim = features // HEADS
    pairs = features // 128
    chunk = features
    code_rows = relay_tx.shape[1]

    def rows_of(m):
        return pl.ds(pl.multiple_of(m * patches, patches), patches)

    def cols(j, width):
        return pl.ds(pl.multiple_of(j * width, width), width)

    def relay(m):
        return remote(
            relay_tx.at[m], relay_rx.at[m], r["relay_s"].at[m], r["relay_r"].at[m], at.other
        )

    def result(m):
        return pltpu.make_async_copy(h_buf.at[m], seg_out.at[rows_of(m)], r["out_sem"].at[m])

    def energy(slot, tensor, rs):
        square = row_sum(tensor * tensor * jnp.concatenate([mask_ref[rs, :]] * pairs, axis=1))
        total = square[:, :128]
        for j in range(1, pairs):
            total = total + square[:, j * 128 : (j + 1) * 128]
        stats[slot : slot + 1, :] += total

    def code_mask(array):
        return jnp.where(
            lax.broadcasted_iota(jnp.int32, array.shape, 0) < CODE_BITS, array, 0.0
        )

    def normalize(values, which, rs):
        gain, bias = norms[2 * which : 2 * which + 1, :], norms[2 * which + 1 : 2 * which + 2, :]
        centered = values - row_mean(values)
        scale = lax.rsqrt(row_mean(centered * centered) + norm_eps)
        hat = centered * scale
        xhats[which][rs, :] = low(hat)
        rstds[which][rs, :] = scale
        return low(hat * gain + bias)

    def norm_back(grad, which, rs):
        gain, slot = norms[2 * which : 2 * which + 1, :], code_rows + 2 * which
        hat = wide(xhats[which][rs, :])
        small_acc[slot : slot + 1, :] += row_sum(grad * hat)
        small_acc[slot + 1 : slot + 2, :] += row_sum(grad)
        scaled = grad * gain
        back = scaled - row_mean(scaled) - hat * row_mean(scaled * hat)
        return rstds[which][rs, :] * back

    lane = lax.broadcasted_iota(jnp.int32, (1, 128), 1)
    halves = [low(wide(lane < head_dim)), low(wide(lane >= head_dim))]
    one_lane = low(wide(jnp.broadcast_to(lane == 48, (patches, 128))))

    def head_lanes(head):
        return jnp.logical_and(lane < 48, lax.rem(lane, 16) == head)

    def three_terms(values):
        first = wide(low(values))
        rest = values - first
        second = wide(low(rest))
        third = wide(low(rest - second))
        return jnp.where(lane < 16, first, jnp.where(lane < 32, second, third))

    def attention(m, hooks=()):
        rs = rows_of(m)
        bias_pack[rs, :] = low(jnp.where(lane == 48, (1.0 - mask_ref[rs, :]) * -1e30, 0.0))
        a_s[rs, :] = normalize(h_buf[m], 0, rs)
        for j in range(3):
            part = dot_nn(a_s[rs, :], w_attn[:, j * features : (j + 1) * features])
            if j == 0:
                part = part * (LOG2E / math.sqrt(head_dim))
            qkv_s[rs, j * features : (j + 1) * features] = low(part)

        ones = [jnp.broadcast_to(half, (patches, 128)) for half in halves]

        def heads(j, carry):
            tops, counts = carry
            query = qkv_s[rs, cols(j, 128)]
            key = qkv_s[rs, cols(j + pairs, 128)]
            value = qkv_s[rs, cols(j + 2 * pairs, 128)]
            bias = bias_pack[rs, :]
            keys = beneath([beside([key * half, bias]) for half in halves])
            values = beneath([beside([value * half, one]) for half, one in zip(halves, ones)])
            scores = dot_nt(beside([query, one_lane]), keys)
            parts = [scores[:, :patches], scores[:, patches:]]
            top = [jnp.max(part, -1, keepdims=True) for part in parts]
            weight = beside([low(jnp.exp2(part - peak)) for part, peak in zip(parts, top)])
            found = dot_nn(weight, values)
            count = found[:, 128:]
            mixed_s[rs, cols(j, 128)] = low(found[:, :128] * (1.0 / count))
            first, second = head_lanes(2 * j), head_lanes(2 * j + 1)
            tops = jnp.where(first, top[0], jnp.where(second, top[1], tops))
            turned = pltpu.roll(count, head_dim, 1)
            counts = jnp.where(first, count, jnp.where(second, turned, counts))
            return tops, counts

        carry = (
            jnp.zeros((patches, 128), jnp.float32),
            jnp.ones((patches, 128), jnp.float32),
        )
        if hooks:
            for part in range(3):
                span = (part * pairs // 3, (part + 1) * pairs // 3)
                carry = lax.fori_loop(*span, heads, carry)
                hooks[part]()
        else:
            for j in range(pairs):
                carry = heads(j, carry)
        lse = carry[0] + jnp.log2(carry[1])
        lse_pack[rs, :] = low(
            jnp.where(lane < 48, three_terms(-lse), jnp.where(lane == 48, 1.0, 0.0))
        )
        attn_out = dot_nn(mixed_s[rs, :], w_attn[:, 3 * features : 4 * features])
        energy(1, attn_out, rs)
        h_buf[m] += attn_out
        c_s[rs, :] = normalize(h_buf[m], 1, rs)

    def widen(m):
        rs = rows_of(m)

        def up(j, _):
            pre = dot_nn(c_s[rs, :], w_up[:, cols(j, chunk)])
            phi = 0.5 + 0.5 * lax.erf(pre * math.sqrt(0.5))
            act_s[rs, cols(j, chunk)] = low(pre * phi)
            slope_s[rs, cols(j, chunk)] = low(
                phi + pre * (jnp.exp(-0.5 * pre * pre) * (1.0 / math.sqrt(2.0 * math.pi)))
            )
            return 0

        lax.fori_loop(0, hidden // chunk, up, 0)

    def narrow(m):
        rs = rows_of(m)
        mlp_out = dot_nn(act_s[rs, :hidden], w_down[...])
        energy(2, mlp_out, rs)
        h_buf[m] += mlp_out
        energy(0, h_buf[m], rs)
        stats[3:4, :] += row_sum(mask_ref[rs, :])

    def forward(m, _):
        rs = rows_of(m)

        @pl.when(is_dec)
        def _():
            relay(m).wait_recv()
            h_buf[m] = dot_tn(relay_rx[m], maps[...])
            attention(m)
            widen(m)

        narrow(m)

        @pl.when(is_enc)
        def _():
            enc_s[rs, :] = low(h_buf[m])
            code_pre = code_mask(dot_nt(maps[...], enc_s[rs, :]))
            u_s[m] = code_pre
            scale = lax.rsqrt(row_sum(code_pre * code_pre) + 1.0)
            relay_tx[m] = low(jnp.tanh(2.0 * math.sqrt(CODE_BITS) * (code_pre * scale)))
            relay(m).start()

        pl.when(is_dec)(lambda: result(m).start())
        return 0

    def open_back(m):
        rs = rows_of(m)

        @pl.when(is_enc)
        def _():
            relay(m).wait_recv()
            code_pre = u_s[m]
            scale = lax.rsqrt(row_sum(code_pre * code_pre) + 1.0)
            unit = code_pre * scale
            factor = 2.0 * math.sqrt(CODE_BITS)
            bent = jnp.tanh(factor * unit)
            g_unit = wide(relay_rx[m]) * (factor * (1.0 - bent * bent))
            g_u = low((g_unit - unit * row_sum(g_unit * unit)) * scale)
            small_acc[0:code_rows, :] += dot_nn(g_u, enc_s[rs, :])
            h_buf[m] = dot_tn(g_u, maps[...])

        @pl.when(is_dec)
        def _():
            result(m).wait()
            h_buf[m] = wide(x_ref[rs, :])

    def mlp_back(m):
        rs = rows_of(m)
        gm_s[rs, :] = low(h_buf[m])

        def down(j, _):
            g_act = dot_nt(gm_s[rs, :], w_down[cols(j, chunk), :])
            slope_s[rs, cols(j, chunk)] = low(g_act * wide(slope_s[rs, cols(j, chunk)]))
            return 0

        lax.fori_loop(0, hidden // chunk, down, 0)
        g_c = dot_nt(slope_s[rs, :hidden], w_up[...])
        h_buf[m] += norm_back(g_c, 1, rs)
        go_s[rs, :] = low(h_buf[m])

    def attn_back_open(m):
        rs = rows_of(m)
        gmix_s[...] = low(dot_nt(go_s[rs, :], w_attn[:, 3 * features : 4 * features]))
        product = wide(gmix_s[...]) * wide(mixed_s[rs, :])
        high = low(product)
        head_of = lax.broadcasted_iota(jnp.int32, (features, 128), 0) // head_dim
        lane_of = lax.broadcasted_iota(jnp.int32, (features, 128), 1)
        pick = low(wide(jnp.logical_and(lane_of < 48, lax.rem(lane_of, 16) == head_of)))
        inner = dot_nn(high, pick) + dot_nn(low(product - wide(high)), pick)
        inner_pack[...] = low(three_terms(-inner))

    def attn_back_heads(m, first, last):
        rs = rows_of(m)

        def split(both):
            return beneath([both[:, :patches], both[:, patches:]])

        def front(j):
            query, key, value = [qkv_s[rs, cols(j + i * pairs, 128)] for i in range(3)]
            extra = [bias_pack[rs, :] + low(wide(head_lanes(2 * j + i))) for i in range(2)]
            keys = beneath([beside([key * halves[i], extra[i]]) for i in range(2)])
            values = beneath([beside([value * halves[i], extra[i]]) for i in range(2)])
            probs = jnp.exp2(dot_nt(beside([query, lse_pack[rs, :]]), keys))
            g_probs = dot_nt(beside([gmix_s[:, cols(j, 128)], inner_pack[...]]), values)
            return low(probs * g_probs), low(probs)

        def back(j, g_scores, probs):
            places = [cols(j + i * pairs, 128) for i in range(3)]
            query, key = qkv_s[rs, places[0]], qkv_s[rs, places[1]]
            g_mixed = gmix_s[:, cols(j, 128)]
            g_query = dot_nn(g_scores, beneath([key * half for half in halves]))
            g_key = dot_tn(split(g_scores), beneath([query * half for half in halves]))
            g_value = dot_tn(split(probs), beneath([g_mixed * half for half in halves]))
            qkv_s[rs, places[0]] = low(g_query * (1.0 / math.sqrt(head_dim)))
            qkv_s[rs, places[1]] = low(g_key * (1.0 / LOG2E))
            qkv_s[rs, places[2]] = low(g_value)

        ready = front(first)
        for j in range(first, last):
            after = front(j + 1) if j + 1 < last else None
            back(j, *ready)
            ready = after

    def attn_back_close(m):
        rs = rows_of(m)
        g_a = dot_nt(qkv_s[rs, :], w_attn[:, : 3 * features])
        h_buf[m] += norm_back(g_a, 0, rs)

    def close_back(m):
        rs = rows_of(m)

        @pl.when(is_enc)
        def _():
            result(m).start()

        @pl.when(is_dec)
        def _():
            g_z = low(h_buf[m])
            small_acc[0:code_rows, :] += dot_nn(relay_rx[m], g_z)
            relay_tx[m] = low(code_mask(dot_nt(maps[...], g_z)))
            relay(m).start()

    def attn_back(m):
        attn_back_open(m)
        attn_back_heads(m, 0, pairs)
        attn_back_close(m)

    def fill_mask():
        patch = lax.broadcasted_iota(jnp.int32, (patches, 128), 0).astype(jnp.float32)
        for m in range(images):
            wide_grid = extent[m, 0] == 0
            length = jnp.where(wide_grid, float(GW), float(GH))
            line = jnp.floor((patch + 0.5) * jnp.where(wide_grid, 1.0 / GW, 1.0 / GH))
            inside = jnp.logical_and(
                line < extent[m, 1].astype(jnp.float32),
                patch - line * length < extent[m, 2].astype(jnp.float32),
            )
            mask_ref[m * patches : (m + 1) * patches, :] = wide(inside)

    def pack_small():
        maps_in = r["maps_in"][...]
        vectors = beneath([r["norm%d_in" % i][...] for i in range(4)])

        def lanes(count, start):
            row_no = lax.broadcasted_iota(jnp.int32, (count, 128), 0)
            return low(wide(lax.broadcasted_iota(jnp.int32, (count, 128), 1) == row_no + start))

        return low(
            dot_nn(maps_in, lanes(CODE_BITS, 0)) + dot_tn(vectors, lanes(4, CODE_BITS))
        )

    def take_small():
        small = wide(w_attn[:, 4 * features :]).T
        maps[...] = low(code_mask(small[:code_rows]))
        norms[0:4, :] = small[CODE_BITS : CODE_BITS + 4]

    def start_image(m):
        h_buf[m] = wide(x_ref[rows_of(m), :])

    def up_grads():
        for j in range(hidden // chunk):
            place = slice(j * chunk, (j + 1) * chunk)
            w_up[:, place] = low(dot_tn(c_s[...], slope_s[:, place]))

    def attn_grads():
        for j in range(3):
            place = slice(j * features, (j + 1) * features)
            w_attn[:, place] = low(dot_tn(a_s[...], qkv_s[:, place]))
        w_attn[:, 3 * features : 4 * features] = low(dot_tn(mixed_s[...], go_s[...]))
        small_grad = jnp.concatenate(
            [
                small_acc[0:CODE_BITS, :],
                small_acc[code_rows : code_rows + 4, :],
                jnp.zeros((128 - CODE_BITS - 4, features), jnp.float32),
            ],
            axis=0,
        )
        w_attn[:, 4 * features :] = low(small_grad.T)

    def fresh():
        fill_mask()
        stats[...] = jnp.zeros_like(stats)
        small_acc[...] = jnp.zeros_like(small_acc)

    def before_relay():
        @pl.when(is_dec)
        def _():
            stats[...] = jnp.zeros_like(stats)

    if not fused:
        copies = [
            pltpu.make_async_copy(r[name], weights[arr], r["own_sem"].at[arr])
            for arr, name in enumerate(("attn_all", "up_all", "down_all"))
        ]
        for copy in copies:
            copy.start()
        fresh()
        at.meet(False)
        for copy in copies:
            copy.wait()
        take_small()
        for m in range(images):
            start_image(m)
            attention(m)
            widen(m)
        before_relay()
        lax.fori_loop(0, images, forward, 0)
        for m in reversed(range(images)):
            open_back(m)
            mlp_back(m)
            attn_back(m)
            close_back(m)
        w_down[...] = low(dot_tn(act_s[:, :hidden], gm_s[...]))
        up_grads()
        attn_grads()
        for arr, name in enumerate(("g_attn", "g_up", "g_down")):
            copy = pltpu.make_async_copy(weights[arr], r[name], r["own_sem"].at[arr])
            copy.start()
            copy.wait()
        for m in range(images):
            pl.when(is_enc)(lambda: result(m).wait())
            relay(m).wait_send()
        return

    heights = (r["qkv_in"].shape[0], r["up_in"].shape[0], r["down_in"].shape[0])
    own_rows = [
        pl.ds(pl.multiple_of(at.here * height, height), height) for height in heights
    ]
    own_copies = [
        pltpu.make_async_copy(src, dst, r["own_sem"].at[i])
        for i, (src, dst) in enumerate(
            (
                (r["qkv_in"], w_attn.at[own_rows[ATTN], pl.ds(0, 3 * features)]),
                (r["out_in"], w_attn.at[own_rows[ATTN], pl.ds(3 * features, features)]),
                (r["up_in"], w_up.at[own_rows[UP]]),
                (r["down_in"], w_down.at[own_rows[DOWN]]),
            )
        )
    ]
    half = heights[DOWN] // 2
    arrays = [
        Blocks(w_attn, heights[ATTN], 0, heights[ATTN], False),
        Blocks(w_up, heights[UP], 0, heights[UP], False),
        Blocks(w_down, 2 * half, 0, half, False),
        Blocks(w_down, 2 * half, half, half, True),
    ]
    gather = Gather(at, arrays, r["g_send"], r["g_recv"])
    scatter = Scatter(
        at,
        arrays,
        (act_s, r["sib_u"], r["sib_d"], r["sib_r"]),
        (act_s, r["x_u"], r["x_d"], r["x_r"]),
        (slope_s, r["z_u"], r["z_d"], r["z_r"]),
        [r[name] for name in ("sib_ssem", "sib_rsem", "x_ssem", "x_rsem", "z_ssem", "z_rsem")],
    )
    total = Total(
        at,
        r["t_pair"],
        r["t_sib"],
        r["t_cross"],
        r["t_lines"],
        [r[name] for name in ("t_near_s", "t_near_r", "t_z_s", "t_z_r")],
    )
    for copy in own_copies:
        copy.start()
    at.meet(True)
    w_attn[own_rows[ATTN], 4 * features :] = pack_small()
    for copy in own_copies[:2]:
        copy.wait()
    gather.own(ATTN)
    fresh()
    for arr in (UP, DOWN, REST):
        scatter.clear(arr)
    for m in range(images):
        start_image(m)
    for copy in own_copies[2:]:
        copy.wait()
    gather.away(ATTN, 1)
    gather.away(ATTN, 2)
    gather.own_across(REST)
    gather.own(UP)
    gather.away(ATTN, 3)
    gather.crossed(ATTN)
    gather.away(UP, 1)
    gather.paired(ATTN)
    take_small()

    def between(*steps):
        def hook():
            for step, *what in steps:
                step(*what)

        return hook

    attention(
        0,
        [
            between((gather.away, UP, 2), (gather.own, DOWN)),
            between((gather.away, UP, 3)),
            between((gather.own, REST), (gather.turn, REST)),
        ],
    )
    attention(
        1,
        [
            between((gather.away, DOWN, 1), (gather.away, DOWN, 2)),
            between((gather.away, DOWN, 3), (gather.away, REST, 1)),
            between((gather.crossed, UP)),
        ],
    )
    gather.paired(UP)
    widen(0)
    gather.away(REST, 2)
    widen(1)
    gather.away(REST, 3)
    gather.crossed(DOWN)
    gather.paired(DOWN)
    gather.paired(REST)
    for arr in range(4):
        gather.sent(arr)
    before_relay()
    lax.fori_loop(0, images, forward, 0)
    total.sib_copy(stats).start()

    def backward(step, _):
        m = images - 1 - step
        open_back(m)
        mlp_back(m)

        @pl.when(jnp.logical_or(is_dec, m > 0))
        def _():
            attn_back(m)
            close_back(m)

        return 0

    lax.fori_loop(0, images, backward, 0)
    total.cross_over(stats)

    def down_block(pair):
        span = 4 * half
        place = pl.ds(pl.multiple_of(pair * span, span), span)
        w_down[place, :] = low(dot_tn(act_s[:, place], gm_s[...]))
        scatter.sib_copy(DOWN, pair).start()
        scatter.sib_copy(REST, pair).start()

    def last_heads(part):
        pl.when(is_enc)(
            lambda: attn_back_heads(0, part * pairs // 3, (part + 1) * pairs // 3)
        )

    scatter.each_far(lambda way, dst_row: down_block(2 * dst_row + 1 - at.col))
    down_block(2 * at.row + 1 - at.col)
    scatter.x_stage(DOWN)
    scatter.each_far(lambda way, dst_row: down_block(2 * dst_row + at.col))
    down_block(2 * at.row + at.col)
    scatter.z_stage(REST, [3])
    pl.when(is_enc)(lambda: attn_back_open(0))
    total.along()
    up_grads()
    scatter.start_pairs(UP)
    scatter.z_stage(REST, [2])
    total.away(1)
    last_heads(0)
    scatter.z_stage(DOWN, [3])
    scatter.x_stage(UP)
    last_heads(1)
    last_heads(2)
    scatter.z_stage(UP, [3])

    @pl.when(is_enc)
    def _():
        attn_back_close(0)
        close_back(0)

    attn_grads()
    total.away(2)
    scatter.z_stage(UP, [2])
    scatter.start_pairs(ATTN)
    scatter.z_stage(REST, [1])
    scatter.clear(ATTN)
    scatter.x_stage(ATTN)
    total.away(3)
    scatter.z_stage(UP, [1])
    r["up_out"][...] = scatter.final(UP)
    scatter.z_stage(ATTN, [3])
    scatter.z_stage(DOWN, [2])
    scatter.z_stage(ATTN, [2])
    scatter.turn(REST)
    scatter.z_stage(DOWN, [1])
    scatter.z_stage(ATTN, [1])
    sums = total.lines[0]
    for i in range(1, rows):
        sums = sums + total.lines[i]
    sums = jnp.sum(sums, -1, keepdims=True)
    scale = 128.0 / (sums[3:4] * features)
    found = jnp.sqrt(sums * scale)
    row_no = lax.broadcasted_iota(jnp.int32, (8, 128), 0)
    lane_no = lax.broadcasted_iota(jnp.int32, (8, 128), 1)
    r["rms"][...] = row_sum(jnp.where(row_no == lane_no, found, 0.0))[:, :3]
    r["down_out"][:half, :] = scatter.final(DOWN)
    r["down_out"][half:, :] = scatter.final(REST)
    last = scatter.final(ATTN)
    r["qkv_out"][...] = last[:, : 3 * features]
    r["out_out"][...] = last[:, 3 * features : 4 * features]
    small = last[:, 4 * features :]
    r["maps_out"][...] = small[:, :CODE_BITS]
    small = jnp.concatenate(
        [small, jnp.zeros((128 - small.shape[0], 128), jnp.float32)], axis=0
    ).T
    for i in range(4):
        r["norm%d_out" % i][...] = small[CODE_BITS + i : CODE_BITS + i + 1, : heights[ATTN]]
    for m in range(images):
        pl.when(is_enc)(lambda: result(m).wait())
        relay(m).wait_send()
    for arr in range(4):
        scatter.sent(arr)
    total.sent(stats)


def run_blocks(fused, operands, x, extent, rows):
    images, patches, features = x.shape
    total = images * patches
    hidden = 4 * features
    attn_width = 4 * features + 128
    code_rows = -(-CODE_BITS // 16) * 16
    bf16, f32 = jnp.bfloat16, jnp.float32
    any_spec = pl.BlockSpec(memory_space=pl.ANY)
    vmem_spec = pl.BlockSpec(memory_space=pltpu.VMEM)
    dma = pltpu.SemaphoreType.DMA
    ins = dict(operands, x=x.reshape(total, features), extent=extent)
    outs = {"seg_out": ((total, features), f32)}
    full = {"a": (features, attn_width), "u": (features, hidden), "d": (hidden, features)}
    buffers = {
        "w_attn": (full["a"], bf16), "w_up": (full["u"], bf16), "w_down": (full["d"], bf16),
        "mask": ((total, 128), f32),
        "norms": ((8, features), f32), "maps": ((code_rows, features), bf16),
        "h": ((images, patches, features), f32),
        "xhat1": ((total, features), bf16), "rstd1": ((total, 1), f32),
        "xhat2": ((total, features), bf16), "rstd2": ((total, 1), f32),
        "a": ((total, features), bf16), "qkv": ((total, 3 * features), bf16),
        "mixed": ((total, features), bf16), "c": ((total, features), bf16),
        "act": ((total, attn_width), bf16), "slope": ((total, attn_width), bf16),
        "lse_pack": ((total, 128), bf16), "bias_pack": ((total, 128), bf16),
        "inner_pack": ((patches, 128), bf16),
        "gm": ((total, features), bf16), "go": ((total, features), bf16),
        "gmix": ((patches, features), bf16),
        "u": ((images, code_rows, patches), f32), "small_acc": ((code_rows + 8, features), f32),
        "relay_tx": ((images, code_rows, patches), bf16),
        "relay_rx": ((images, code_rows, patches), bf16),
    }
    sems = {"relay_s": (images,), "relay_r": (images,), "out_sem": (images,)}
    in_vmem = ["x", "maps_in", *("norm%d_in" % i for i in range(4))]
    smem_spec = pl.BlockSpec(memory_space=pltpu.SMEM)
    if fused:
        outs["rms"] = ((1, 3), f32)
        shards = {
            "a": (operands["qkv_in"].shape[0], attn_width),
            "u": operands["up_in"].shape,
            "d": operands["down_in"].shape,
        }
        outs["qkv_out"] = (operands["qkv_in"].shape, f32)
        outs["out_out"] = (operands["out_in"].shape, f32)
        outs["up_out"] = (shards["u"], f32)
        outs["down_out"] = (shards["d"], f32)
        outs["maps_out"] = ((shards["a"][0], CODE_BITS), f32)
        for i in range(4):
            outs["norm%d_out" % i] = ((1, shards["a"][0]), f32)
        buffers["stats"] = ((8, 128), f32)
        half = (shards["d"][0] // 2, features)
        for name, shape, split in (("u", shards["u"], 0), ("d", half, 0), ("r", half, 1)):
            buffers["sib_" + name] = ((2 * rows,) + shape, bf16)
            buffers["x_" + name] = ((1 if split else rows,) + shape, bf16)
            buffers["z_" + name] = (((1 + split) * (rows + 1),) + shape, bf16)
        for name in ("t_pair", "t_sib", "t_cross"):
            buffers[name] = ((8, 128), f32)
        buffers["t_lines"] = ((rows, 8, 128), f32)
        sems.update(
            own_sem=(4,), g_send=(4, 8 * rows), g_recv=(4, 4 * rows),
            sib_ssem=(4, 2 * rows), sib_rsem=(4, 2 * rows), x_ssem=(4, rows), x_rsem=(4, rows),
            z_ssem=(4, 2 * rows), z_rsem=(4, 2 * rows + 2),
            t_near_s=(2,), t_near_r=(2,), t_z_s=(2, rows), t_z_r=(rows,),
        )
    else:
        outs["g_attn"] = (full["a"], bf16)
        outs["g_up"] = (full["u"], bf16)
        outs["g_down"] = (full["d"], bf16)
        outs["stats"] = ((8, 128), f32)
        sems["own_sem"] = (3,)
    names = [*ins, *outs, *buffers, *sems]
    out_any = ("seg_out", "g_attn", "g_up", "g_down")
    found = pl.pallas_call(
        partial(blocks_body, fused, rows, names),
        out_shape=tuple(jax.ShapeDtypeStruct(s, t) for s, t in outs.values()),
        in_specs=[
            vmem_spec if n in in_vmem else smem_spec if n == "extent" else any_spec for n in ins
        ],
        out_specs=tuple(any_spec if n in out_any else vmem_spec for n in outs),
        scratch_shapes=[pltpu.VMEM(s, t) for s, t in buffers.values()]
        + [dma(s) for s in sems.values()],
        compiler_params=pltpu.CompilerParams(
            collective_id=1, has_side_effects=True, vmem_limit_bytes=VMEM_BYTES
        ),
        name="both_blocks",
    )(*ins.values())
    return dict(zip(outs, found))


def hand_over_body(count, *refs):
    steps = [refs[i * count : (i + 1) * count] for i in range(3)]
    sems = refs[3 * count :]
    copies = [
        [pltpu.make_async_copy(src, dst, sem.at[i]) for i, (src, dst) in enumerate(zip(*pair))]
        for pair, sem in zip(((steps[0], steps[2]), (steps[2], steps[1])), sems)
    ]
    for copy in copies[0]:
        copy.start()
    for copy, after in zip(*copies):
        copy.wait()
        after.start()
    for copy in copies[1]:
        copy.wait()


def hand_over(arrays):
    any_spec = pl.BlockSpec(memory_space=pl.ANY)
    return pl.pallas_call(
        partial(hand_over_body, len(arrays)),
        out_shape=tuple(jax.ShapeDtypeStruct(v.shape, v.dtype) for v in arrays),
        in_specs=[any_spec] * len(arrays),
        out_specs=(any_spec,) * len(arrays),
        scratch_shapes=[pltpu.VMEM(v.shape, v.dtype) for v in arrays]
        + [pltpu.SemaphoreType.DMA((len(arrays),))] * 2,
        name="hand_over",
    )(*arrays)


def on_device(
    segment_input,
    image_extent,
    norm1_gain,
    norm1_bias,
    norm2_gain,
    norm2_bias,
    qkv_weight,
    out_weight,
    up_weight,
    down_weight,
    code_maps,
):
    _, images, patches, features = segment_input.shape
    qkv_width = qkv_weight.shape[2]
    count = lax.axis_size("dp")
    x = segment_input[0]
    if qkv_weight.shape[1] % 16 == 0 and count % 4 == 0:
        operands = {
            "qkv_in": qkv_weight[0],
            "out_in": out_weight[0],
            "maps_in": code_maps[0],
            "norm0_in": norm1_gain,
            "norm1_in": norm1_bias,
            "norm2_in": norm2_gain,
            "norm3_in": norm2_bias,
            "up_in": up_weight[0],
            "down_in": down_weight[0],
        }
        found = run_blocks(True, operands, x, image_extent, count // 4)
        names = ["seg_out", "rms", *("norm%d_out" % i for i in range(4))]
        names += ["qkv_out", "out_out", "up_out", "down_out", "maps_out"]
        results = hand_over([found[name] for name in names])
    else:
        small = jnp.concatenate(
            [code_maps[0]]
            + [v[0][:, None] for v in (norm1_gain, norm1_bias, norm2_gain, norm2_bias)],
            axis=1,
        )
        small = jnp.pad(small, ((0, 0), (0, 128 - small.shape[1])))
        attn = jnp.concatenate([qkv_weight[0], out_weight[0], small], axis=1)
        operands = {
            name: lax.all_gather(shard, "dp", axis=0, tiled=True)
            for name, shard in (
                ("attn_all", attn),
                ("up_all", up_weight[0]),
                ("down_all", down_weight[0]),
            )
        }
        found = run_blocks(False, operands, x, image_extent, 1)
        attn_shard, up_shard, down_shard = [
            lax.psum_scatter(
                found[name].astype(jnp.float32), "dp", scatter_dimension=0, tiled=True
            )
            for name in ("g_attn", "g_up", "g_down")
        ]
        stats = lax.psum(found["stats"], "dp")
        rms_stats = jnp.sqrt(jnp.sum(stats[:3], 1) / (stats[3, 0] * features))[None]
        small_shard = attn_shard[:, qkv_width + features :]
        results = [
            found["seg_out"],
            rms_stats,
            *(small_shard[:, CODE_BITS + i][None] for i in range(4)),
            attn_shard[:, :qkv_width],
            attn_shard[:, qkv_width : qkv_width + features],
            up_shard,
            down_shard,
            small_shard[:, :CODE_BITS],
        ]
    return (
        results[0].reshape(segment_input.shape),
        *results[1:6],
        *(v[None] for v in results[6:]),
    )


def solution(mesh):
    return jax.shard_map(
        on_device,
        mesh=mesh,
        in_specs=(
            P("segment", "dp", None, None),
            P("dp", None),
            P("segment", "dp"),
            P("segment", "dp"),
            P("segment", "dp"),
            P("segment", "dp"),
            P("segment", "dp", None),
            P("segment", "dp", None),
            P("segment", "dp", None),
            P("segment", "dp", None),
            P("segment", "dp", None),
        ),
        out_specs=(
            P("segment", "dp", None, None),
            P("segment", None),
            P("segment", "dp"),
            P("segment", "dp"),
            P("segment", "dp"),
            P("segment", "dp"),
            P("segment", "dp", None),
            P("segment", "dp", None),
            P("segment", "dp", None),
            P("segment", "dp", None),
            P("segment", "dp", None),
        ),
        check_vma=False,
    )
```

```python
from functools import partial
import math

import jax
import jax.numpy as jnp
from jax import lax
from jax.experimental import pallas as pl
from jax.experimental.pallas import tpu as pltpu
from jax.sharding import PartitionSpec as P

HEADS = 12
CODE_BITS = 18
GH = 16
GW = 24
LOG2E = math.log2(math.e)
VMEM_BYTES = 62 << 20


norm_eps = 1e-06


MESH_ID = pl.DeviceIdType.MESH
ATTN, UP, DOWN, REST = 0, 1, 2, 3


def dot_nn(left, right):
    return lax.dot_general(left, right, (((1,), (0,)), ((), ())), preferred_element_type=jnp.float32)


def dot_nt(left, right):
    return lax.dot_general(left, right, (((1,), (1,)), ((), ())), preferred_element_type=jnp.float32)


def dot_tn(left, right):
    return lax.dot_general(left, right, (((0,), (0,)), ((), ())), preferred_element_type=jnp.float32)


def low(array):
    return array.astype(jnp.bfloat16)


def wide(array):
    return array.astype(jnp.float32)


def beside(arrays):
    return jnp.concatenate(arrays, axis=1)


def beneath(arrays):
    return jnp.concatenate(arrays, axis=0)


def row_sum(array):
    return jnp.sum(array, 0, keepdims=True)


def row_mean(array):
    return jnp.mean(array, -1, keepdims=True)


def remote(src, dst, ssem, rsem, to):
    return pltpu.make_async_remote_copy(
        src_ref=src,
        dst_ref=dst,
        send_sem=ssem,
        recv_sem=rsem,
        device_id=to,
        device_id_type=MESH_ID,
    )


class Place:
    def __init__(self, rows):
        self.rows = rows
        self.seg = lax.axis_index("segment")
        self.here = lax.axis_index("dp")
        self.core = lax.rem(self.here, 2)
        self.col = lax.rem(self.here // 2, 2)
        self.row = self.here // 4
        self.sib = (self.seg, self.here + 1 - 2 * self.core)
        self.across = (self.seg, self.here + 2 - 4 * self.col)
        self.up = (self.seg, self.here + 4)
        self.down = (self.seg, self.here - 4)
        self.other = (1 - self.seg, self.here)
        self.has_up = self.row < rows - 1
        self.has_down = self.row > 0

    def meet(self, in_plane):
        barrier = pltpu.get_barrier_semaphore()

        def greet(to):
            pl.semaphore_signal(barrier, inc=1, device_id=to, device_id_type=MESH_ID)

        greet(self.other)
        if not in_plane:
            pl.semaphore_wait(barrier, 1)
            return
        greet(self.sib)
        greet(self.across)
        pl.when(self.has_up)(lambda: greet(self.up))
        pl.when(self.has_down)(lambda: greet(self.down))
        both = jnp.logical_and(self.has_up, self.has_down)
        pl.semaphore_wait(barrier, jnp.where(both, 5, 4))


class Blocks:
    def __init__(self, ref, stride, first, height, split):
        self.ref, self.stride, self.first, self.height = ref, stride, first, height
        self.split = split

    def of(self, device):
        start = pl.multiple_of(device * self.stride + self.first, self.height)
        return self.ref.at[pl.ds(start, self.height)]


class Gather:
    def __init__(self, place, arrays, send_sem, recv_sem):
        self.at, self.arrays = place, arrays
        self.send_sem, self.recv_sem = send_sem, recv_sem

    def copy(self, arr, src, slot, to):
        block = self.arrays[arr].of(src)
        return remote(block, block, self.send_sem.at[arr, slot], self.recv_sem.at[arr, src], to)

    def sender(self, arr, src_row, src_col, way, to):
        pair = src_row * 2 + src_col
        return self.copy(arr, pair * 2 + self.at.core, 2 * self.at.rows * way + pair, to)

    def to_up(self, arr, src_row, src_col):
        return self.sender(arr, src_row, src_col, 0, self.at.up)

    def to_down(self, arr, src_row, src_col):
        return self.sender(arr, src_row, src_col, 1, self.at.down)

    def to_sib(self, arr, src_row, src_col):
        return self.sender(arr, src_row, src_col, 2, self.at.sib)

    def to_across(self, arr, src_row):
        return self.sender(arr, src_row, self.at.col, 3, self.at.across)

    def arrive(self, arr, src_row, src_col):
        self.sender(arr, src_row, src_col, 0, self.at.sib).wait_recv()

    def along(self, arr, src_col):
        row = self.at.row
        pl.when(self.at.has_up)(lambda: self.to_up(arr, row, src_col).start())
        pl.when(self.at.has_down)(lambda: self.to_down(arr, row, src_col).start())
        self.to_sib(arr, row, src_col).start()

    def own_across(self, arr):
        self.to_across(arr, self.at.row).start()

    def own(self, arr):
        self.along(arr, self.at.col)
        if not self.arrays[arr].split:
            self.own_across(arr)

    def turn(self, arr):
        self.arrive(arr, self.at.row, 1 - self.at.col)
        self.along(arr, 1 - self.at.col)

    def away(self, arr, dist):
        at = self.at
        split = self.arrays[arr].split

        def one(src_row, src_col, forward, more):
            self.arrive(arr, src_row, src_col)
            pl.when(more)(lambda: forward(arr, src_row, src_col).start())
            if not split:
                self.to_across(arr, src_row).start()
            self.to_sib(arr, src_row, src_col).start()

        for src_col in (at.col, 1 - at.col)[: 2 if split else 1]:
            pl.when(at.row - dist >= 0)(
                lambda: one(at.row - dist, src_col, self.to_up, at.has_up)
            )
            pl.when(at.row + dist < at.rows)(
                lambda: one(at.row + dist, src_col, self.to_down, at.has_down)
            )

    def crossed(self, arr):
        at = self.at

        def one(src):
            self.arrive(arr, src, 1 - at.col)
            self.to_sib(arr, src, 1 - at.col).start()

        one(at.row)
        for dist in range(1, at.rows):
            pl.when(at.row - dist >= 0)(lambda: one(at.row - dist))
            pl.when(at.row + dist < at.rows)(lambda: one(at.row + dist))

    def paired(self, arr):
        @pl.loop(0, 2 * self.at.rows)
        def _(i):
            self.copy(arr, 2 * i + 1 - self.at.core, 0, self.at.sib).wait_recv()

    def sent(self, arr):
        at = self.at

        @pl.loop(0, at.rows)
        def _(i):
            self.to_sib(arr, i, 0).wait_send()
            self.to_sib(arr, i, 1).wait_send()
            if not self.arrays[arr].split:
                self.to_across(arr, i).wait_send()
            for src_col in (at.col, 1 - at.col)[: 2 if self.arrays[arr].split else 1]:
                pl.when(jnp.logical_and(i <= at.row, at.has_up))(
                    lambda: self.to_up(arr, i, src_col).wait_send()
                )
                pl.when(jnp.logical_and(i >= at.row, at.has_down))(
                    lambda: self.to_down(arr, i, src_col).wait_send()
                )

        if self.arrays[arr].split:
            self.to_across(arr, at.row).wait_send()


class Scatter:
    def __init__(self, place, arrays, sibs, crosses, lines, sems):
        self.at, self.arrays = place, arrays
        self.sibs, self.crosses, self.lines = sibs, crosses, lines
        self.sib_s, self.sib_r, self.x_s, self.x_r, self.z_s, self.z_r = sems

    def mine(self, arr, pair):
        return self.arrays[arr].of(2 * pair + self.at.core)

    def from_sib(self, arr, pair):
        return self.slot(self.sibs, arr, pair)

    def from_across(self, arr, dst_row):
        return self.slot(self.crosses, arr, dst_row + (2 * self.at.rows if arr == ATTN else 0))

    def from_line(self, arr, slot):
        return self.slot(self.lines, arr, slot)

    def slot(self, buffers, arr, slot):
        if arr != ATTN:
            return buffers[arr].at[slot]
        height = self.arrays[arr].height
        return buffers[arr].at[pl.ds(pl.multiple_of(slot * height, height), height)]

    def sib_copy(self, arr, pair):
        return remote(
            self.arrays[arr].of(2 * pair + 1 - self.at.core),
            self.from_sib(arr, pair),
            self.sib_s.at[arr, pair],
            self.sib_r.at[arr, pair],
            self.at.sib,
        )

    def x_copy(self, arr, dst_row):
        slot = 0 if self.arrays[arr].split else dst_row
        return remote(
            self.mine(arr, 2 * dst_row + 1 - self.at.col),
            self.from_across(arr, slot),
            self.x_s.at[arr, slot],
            self.x_r.at[arr, slot],
            self.at.across,
        )

    def z_slot(self, arr, way, dst_row, dst_col, to_row):
        slot = jnp.where(jnp.logical_and(way == 1, dst_row == to_row), self.at.rows, dst_row)
        return slot + (self.at.rows + 1) * dst_col if self.arrays[arr].split else slot

    def z_copy(self, arr, way, dst_row, dst_col, slot):
        pair = 2 * dst_row + dst_col
        return remote(
            self.mine(arr, pair),
            self.from_line(arr, slot),
            self.z_s.at[arr, pair],
            self.z_r.at[arr, slot],
            (self.at.seg, self.at.here + 4 - 8 * way),
        )

    def each_far(self, body, dists=None):
        at = self.at
        for dist in dists or range(at.rows - 1, 0, -1):

            @pl.loop(0, 2)
            def _(way):
                dst_row = at.row + (1 - 2 * way) * dist
                pl.when(jnp.logical_and(dst_row >= 0, dst_row < at.rows))(
                    lambda: body(way, dst_row)
                )

    def clear(self, arr):
        rows = self.at.rows

        def zero(slot):
            for more in range(2 if self.arrays[arr].split else 1):
                place = self.from_line(arr, slot + more * (rows + 1))
                place[...] = jnp.zeros(place.shape, jnp.bfloat16)

        @pl.when(jnp.logical_not(self.at.has_down))
        def _():
            for slot in range(rows):
                zero(slot)

        @pl.when(jnp.logical_not(self.at.has_up))
        def _():
            for slot in [*range(rows - 1), rows]:
                zero(slot)

    def start_pairs(self, arr):
        def go(dst_row, at_col):
            self.sib_copy(arr, 2 * dst_row + at_col).start()

        self.each_far(lambda way, dst_row: go(dst_row, 1 - self.at.col))
        go(self.at.row, 1 - self.at.col)
        self.each_far(lambda way, dst_row: go(dst_row, self.at.col))
        go(self.at.row, self.at.col)

    def pair_sum(self, arr, pair):
        self.sib_copy(arr, pair).wait_recv()
        return wide(self.mine(arr, pair)[...]) + wide(self.from_sib(arr, pair)[...])

    def x_one(self, arr, dst_row):
        pair = 2 * dst_row + 1 - self.at.col
        self.mine(arr, pair)[...] = low(self.pair_sum(arr, pair))
        self.x_copy(arr, dst_row).start()

    def x_stage(self, arr):
        self.each_far(lambda way, dst_row: self.x_one(arr, dst_row))
        self.x_one(arr, self.at.row)

    def crossed(self, arr, dst_row):
        self.x_copy(arr, dst_row).wait_recv()
        return wide(self.from_across(arr, 0 if self.arrays[arr].split else dst_row)[...])

    def z_stage(self, arr, dists):
        at = self.at
        split = self.arrays[arr].split

        def go(way, dst_row, dst_col):
            behind = at.row - 1 + 2 * way
            slot = self.z_slot(arr, way, dst_row, dst_col, at.row)

            @pl.when(jnp.logical_and(behind >= 0, behind < at.rows))
            def _():
                self.z_copy(arr, way, dst_row, dst_col, slot).wait_recv()

            total = self.pair_sum(arr, 2 * dst_row + dst_col)
            if not split:
                total = total + self.crossed(arr, dst_row)
            total = total + wide(self.from_line(arr, slot)[...])
            self.mine(arr, 2 * dst_row + dst_col)[...] = low(total)
            slot = self.z_slot(arr, way, dst_row, dst_col, at.row + 1 - 2 * way)
            self.z_copy(arr, way, dst_row, dst_col, slot).start()

        if not split:
            self.each_far(lambda way, dst_row: go(way, dst_row, at.col), dists)
            return

        def both(way, dst_row):
            @pl.loop(0, 2)
            def _(dst_col):
                go(way, dst_row, dst_col)

        self.each_far(both, dists)

    def lines_end(self, arr, dst_col):
        at = self.at
        slots = [self.z_slot(arr, way, at.row, dst_col, at.row) for way in range(2)]
        for way, has in enumerate((at.has_down, at.has_up)):
            pl.when(has)(
                lambda: self.z_copy(arr, way, at.row, dst_col, slots[way]).wait_recv()
            )
        total = self.pair_sum(arr, 2 * at.row + dst_col)
        return total + sum(wide(self.from_line(arr, slot)[...]) for slot in slots)

    def turn(self, arr):
        at = self.at
        total = self.lines_end(arr, 1 - at.col)
        self.mine(arr, 2 * at.row + 1 - at.col)[...] = low(total)
        self.x_copy(arr, at.row).start()

    def final(self, arr):
        return self.lines_end(arr, self.at.col) + self.crossed(arr, self.at.row)

    def sent(self, arr):
        split = self.arrays[arr].split

        @pl.loop(0, self.at.rows)
        def _(i):
            self.sib_copy(arr, 2 * i).wait_send()
            self.sib_copy(arr, 2 * i + 1).wait_send()
            if not split:
                self.x_copy(arr, i).wait_send()

        if split:
            self.x_copy(arr, self.at.row).wait_send()

        def lines(way, dst_row):
            for dst_col in (self.at.col, 1 - self.at.col)[: 2 if split else 1]:
                self.z_copy(arr, way, dst_row, dst_col, 0).wait_send()

        self.each_far(lines)


class Total:
    def __init__(self, place, pair, sib, cross, lines, sems):
        self.at, self.pair, self.sib, self.cross, self.lines = place, pair, sib, cross, lines
        self.near_s, self.near_r, self.z_s, self.z_r = sems

    def sib_copy(self, own):
        return remote(own, self.sib, self.near_s.at[0], self.near_r.at[0], self.at.sib)

    def x_copy(self):
        return remote(self.pair, self.cross, self.near_s.at[1], self.near_r.at[1], self.at.across)

    def z_copy(self, way, src_row):
        line = self.lines.at[src_row]
        to = (self.at.seg, self.at.here + 4 - 8 * way)
        return remote(line, line, self.z_s.at[way, src_row], self.z_r.at[src_row], to)

    def cross_over(self, own):
        self.sib_copy(own).wait_recv()
        self.pair[...] = own[...] + self.sib[...]
        self.x_copy().start()

    def along(self):
        self.x_copy().wait_recv()
        self.lines[self.at.row] = self.pair[...] + self.cross[...]
        pl.when(self.at.has_up)(lambda: self.z_copy(0, self.at.row).start())
        pl.when(self.at.has_down)(lambda: self.z_copy(1, self.at.row).start())

    def away(self, dist):
        at = self.at

        @pl.when(at.row - dist >= 0)
        def _():
            src = at.row - dist
            self.z_copy(0, src).wait_recv()
            pl.when(at.has_up)(lambda: self.z_copy(0, src).start())

        @pl.when(at.row + dist < at.rows)
        def _():
            src = at.row + dist
            self.z_copy(1, src).wait_recv()
            pl.when(at.has_down)(lambda: self.z_copy(1, src).start())

    def sent(self, own):
        at = self.at
        self.sib_copy(own).wait_send()
        self.x_copy().wait_send()

        @pl.loop(0, at.rows)
        def _(i):
            pl.when(jnp.logical_and(i <= at.row, at.has_up))(
                lambda: self.z_copy(0, i).wait_send()
            )
            pl.when(jnp.logical_and(i >= at.row, at.has_down))(
                lambda: self.z_copy(1, i).wait_send()
            )


def blocks_body(fused, rows, names, *refs):
    r = dict(zip(names, refs))
    at = Place(rows)
    is_enc = at.seg == 0
    is_dec = at.seg == 1
    x_ref, mask_ref, seg_out, stats = r["x"], r["mask"], r["seg_out"], r["stats"]
    extent = r["extent"]
    w_attn, w_up, w_down = weights = [r["w_attn"], r["w_up"], r["w_down"]]
    norms, maps, h_buf = r["norms"], r["maps"], r["h"]
    a_s, qkv_s, mixed_s, c_s = r["a"], r["qkv"], r["mixed"], r["c"]
    act_s, slope_s, gm_s, go_s, gmix_s = r["act"], r["slope"], r["gm"], r["go"], r["gmix"]
    xhats, rstds = (r["xhat1"], r["xhat2"]), (r["rstd1"], r["rstd2"])
    lse_pack, bias_pack, inner_pack = r["lse_pack"], r["bias_pack"], r["inner_pack"]
    u_s, small_acc, relay_tx, relay_rx = r["u"], r["small_acc"], r["relay_tx"], r["relay_rx"]
    enc_s = gm_s
    total_rows, features = x_ref.shape
    images = h_buf.shape[0]
    patches = total_rows // images
    hidden = w_up.shape[1]
    head_dim = features // HEADS
    pairs = features // 128
    chunk = features
    code_rows = relay_tx.shape[1]

    def rows_of(m):
        return pl.ds(pl.multiple_of(m * patches, patches), patches)

    def cols(j, width):
        return pl.ds(pl.multiple_of(j * width, width), width)

    def relay(m):
        return remote(
            relay_tx.at[m], relay_rx.at[m], r["relay_s"].at[m], r["relay_r"].at[m], at.other
        )

    def result(m):
        return pltpu.make_async_copy(h_buf.at[m], seg_out.at[rows_of(m)], r["out_sem"].at[m])

    def energy(slot, tensor, rs):
        square = row_sum(tensor * tensor * jnp.concatenate([mask_ref[rs, :]] * pairs, axis=1))
        total = square[:, :128]
        for j in range(1, pairs):
            total = total + square[:, j * 128 : (j + 1) * 128]
        stats[slot : slot + 1, :] += total

    def code_mask(array):
        return jnp.where(
            lax.broadcasted_iota(jnp.int32, array.shape, 0) < CODE_BITS, array, 0.0
        )

    def normalize(values, which, rs):
        gain, bias = norms[2 * which : 2 * which + 1, :], norms[2 * which + 1 : 2 * which + 2, :]
        centered = values - row_mean(values)
        scale = lax.rsqrt(row_mean(centered * centered) + norm_eps)
        hat = centered * scale
        xhats[which][rs, :] = low(hat)
        rstds[which][rs, :] = scale
        return low(hat * gain + bias)

    def norm_back(grad, which, rs):
        gain, slot = norms[2 * which : 2 * which + 1, :], code_rows + 2 * which
        hat = wide(xhats[which][rs, :])
        small_acc[slot : slot + 1, :] += row_sum(grad * hat)
        small_acc[slot + 1 : slot + 2, :] += row_sum(grad)
        scaled = grad * gain
        back = scaled - row_mean(scaled) - hat * row_mean(scaled * hat)
        return rstds[which][rs, :] * back

    lane = lax.broadcasted_iota(jnp.int32, (1, 128), 1)
    halves = [low(wide(lane < head_dim)), low(wide(lane >= head_dim))]
    one_lane = low(wide(jnp.broadcast_to(lane == 48, (patches, 128))))

    def head_lanes(head):
        return jnp.logical_and(lane < 48, lax.rem(lane, 16) == head)

    def three_terms(values):
        first = wide(low(values))
        rest = values - first
        second = wide(low(rest))
        third = wide(low(rest - second))
        return jnp.where(lane < 16, first, jnp.where(lane < 32, second, third))

    def attention(m, hooks=()):
        rs = rows_of(m)
        bias_pack[rs, :] = low(jnp.where(lane == 48, (1.0 - mask_ref[rs, :]) * -1e30, 0.0))
        a_s[rs, :] = normalize(h_buf[m], 0, rs)
        for j in range(3):
            part = dot_nn(a_s[rs, :], w_attn[:, j * features : (j + 1) * features])
            if j == 0:
                part = part * (LOG2E / math.sqrt(head_dim))
            qkv_s[rs, j * features : (j + 1) * features] = low(part)

        ones = [jnp.broadcast_to(half, (patches, 128)) for half in halves]

        def heads(j, carry):
            tops, counts = carry
            query = qkv_s[rs, cols(j, 128)]
            key = qkv_s[rs, cols(j + pairs, 128)]
            value = qkv_s[rs, cols(j + 2 * pairs, 128)]
            bias = bias_pack[rs, :]
            keys = beneath([beside([key * half, bias]) for half in halves])
            values = beneath([beside([value * half, one]) for half, one in zip(halves, ones)])
            scores = dot_nt(beside([query, one_lane]), keys)
            parts = [scores[:, :patches], scores[:, patches:]]
            top = [jnp.max(part, -1, keepdims=True) for part in parts]
            weight = beside([low(jnp.exp2(part - peak)) for part, peak in zip(parts, top)])
            found = dot_nn(weight, values)
            count = found[:, 128:]
            mixed_s[rs, cols(j, 128)] = low(found[:, :128] * (1.0 / count))
            first, second = head_lanes(2 * j), head_lanes(2 * j + 1)
            tops = jnp.where(first, top[0], jnp.where(second, top[1], tops))
            turned = pltpu.roll(count, head_dim, 1)
            counts = jnp.where(first, count, jnp.where(second, turned, counts))
            return tops, counts

        carry = (
            jnp.zeros((patches, 128), jnp.float32),
            jnp.ones((patches, 128), jnp.float32),
        )
        if hooks:
            for part in range(3):
                span = (part * pairs // 3, (part + 1) * pairs // 3)
                carry = lax.fori_loop(*span, heads, carry)
                hooks[part]()
        else:
            for j in range(pairs):
                carry = heads(j, carry)
        lse = carry[0] + jnp.log2(carry[1])
        lse_pack[rs, :] = low(
            jnp.where(lane < 48, three_terms(-lse), jnp.where(lane == 48, 1.0, 0.0))
        )
        attn_out = dot_nn(mixed_s[rs, :], w_attn[:, 3 * features : 4 * features])
        energy(1, attn_out, rs)
        h_buf[m] += attn_out
        c_s[rs, :] = normalize(h_buf[m], 1, rs)

    def widen(m):
        rs = rows_of(m)

        def up(j, _):
            pre = dot_nn(c_s[rs, :], w_up[:, cols(j, chunk)])
            phi = 0.5 + 0.5 * lax.erf(pre * math.sqrt(0.5))
            act_s[rs, cols(j, chunk)] = low(pre * phi)
            slope_s[rs, cols(j, chunk)] = low(
                phi + pre * (jnp.exp(-0.5 * pre * pre) * (1.0 / math.sqrt(2.0 * math.pi)))
            )
            return 0

        lax.fori_loop(0, hidden // chunk, up, 0, unroll=True)

    def forward(m, _):
        rs = rows_of(m)

        @pl.when(is_dec)
        def _():
            relay(m).wait_recv()
            h_buf[m] = dot_tn(relay_rx[m], maps[...])
            attention(m)
            widen(m)

        mlp_out = dot_nn(act_s[rs, :hidden], w_down[...])
        block_out = h_buf[m] + mlp_out
        h_buf[m] = block_out

        @pl.when(is_enc)
        def _():
            enc_s[rs, :] = low(h_buf[m])
            code_pre = code_mask(dot_nt(maps[...], enc_s[rs, :]))
            u_s[m] = code_pre
            scale = lax.rsqrt(row_sum(code_pre * code_pre) + 1.0)
            relay_tx[m] = low(jnp.tanh(2.0 * math.sqrt(CODE_BITS) * (code_pre * scale)))
            relay(m).start()

        pl.when(is_dec)(lambda: result(m).start())
        energy(2, mlp_out, rs)
        energy(0, block_out, rs)
        stats[3:4, :] += row_sum(mask_ref[rs, :])
        return 0

    def open_back(m):
        rs = rows_of(m)

        @pl.when(is_enc)
        def _():
            relay(m).wait_recv()
            code_pre = u_s[m]
            scale = lax.rsqrt(row_sum(code_pre * code_pre) + 1.0)
            unit = code_pre * scale
            factor = 2.0 * math.sqrt(CODE_BITS)
            bent = jnp.tanh(factor * unit)
            g_unit = wide(relay_rx[m]) * (factor * (1.0 - bent * bent))
            g_u = low((g_unit - unit * row_sum(g_unit * unit)) * scale)
            small_acc[0:code_rows, :] += dot_nn(g_u, enc_s[rs, :])
            h_buf[m] = dot_tn(g_u, maps[...])

        @pl.when(is_dec)
        def _():
            result(m).wait()
            h_buf[m] = wide(x_ref[rs, :])

    def mlp_back(m):
        rs = rows_of(m)
        gm_s[rs, :] = low(h_buf[m])

        def down(j, _):
            g_act = dot_nt(gm_s[rs, :], w_down[cols(j, chunk), :])
            slope_s[rs, cols(j, chunk)] = low(g_act * wide(slope_s[rs, cols(j, chunk)]))
            return 0

        lax.fori_loop(0, hidden // chunk, down, 0, unroll=True)
        g_c = dot_nt(slope_s[rs, :hidden], w_up[...])
        h_buf[m] += norm_back(g_c, 1, rs)
        go_s[rs, :] = low(h_buf[m])

    def attn_back_open(m):
        rs = rows_of(m)
        gmix_s[...] = low(dot_nt(go_s[rs, :], w_attn[:, 3 * features : 4 * features]))
        product = wide(gmix_s[...]) * wide(mixed_s[rs, :])
        high = low(product)
        head_of = lax.broadcasted_iota(jnp.int32, (features, 128), 0) // head_dim
        lane_of = lax.broadcasted_iota(jnp.int32, (features, 128), 1)
        pick = low(wide(jnp.logical_and(lane_of < 48, lax.rem(lane_of, 16) == head_of)))
        inner = dot_nn(high, pick) + dot_nn(low(product - wide(high)), pick)
        inner_pack[...] = low(three_terms(-inner))

    def attn_back_heads(m, first, last):
        rs = rows_of(m)

        def split(both):
            return beneath([both[:, :patches], both[:, patches:]])

        def front(j):
            query, key, value = [qkv_s[rs, cols(j + i * pairs, 128)] for i in range(3)]
            extra = [bias_pack[rs, :] + low(wide(head_lanes(2 * j + i))) for i in range(2)]
            keys = beneath([beside([key * halves[i], extra[i]]) for i in range(2)])
            values = beneath([beside([value * halves[i], extra[i]]) for i in range(2)])
            probs = jnp.exp2(dot_nt(beside([query, lse_pack[rs, :]]), keys))
            g_probs = dot_nt(beside([gmix_s[:, cols(j, 128)], inner_pack[...]]), values)
            return low(probs * g_probs), low(probs)

        def back(j, g_scores, probs):
            places = [cols(j + i * pairs, 128) for i in range(3)]
            query, key = qkv_s[rs, places[0]], qkv_s[rs, places[1]]
            g_mixed = gmix_s[:, cols(j, 128)]
            g_query = dot_nn(g_scores, beneath([key * half for half in halves]))
            g_key = dot_tn(split(g_scores), beneath([query * half for half in halves]))
            g_value = dot_tn(split(probs), beneath([g_mixed * half for half in halves]))
            qkv_s[rs, places[0]] = low(g_query * (1.0 / math.sqrt(head_dim)))
            qkv_s[rs, places[1]] = low(g_key * (1.0 / LOG2E))
            qkv_s[rs, places[2]] = low(g_value)

        ready = front(first)
        for j in range(first, last):
            after = front(j + 1) if j + 1 < last else None
            back(j, *ready)
            ready = after

    def attn_back_close(m):
        rs = rows_of(m)
        g_a = dot_nt(qkv_s[rs, :], w_attn[:, : 3 * features])
        h_buf[m] += norm_back(g_a, 0, rs)

    def close_back(m):
        rs = rows_of(m)

        @pl.when(is_enc)
        def _():
            result(m).start()

        @pl.when(is_dec)
        def _():
            g_z = low(h_buf[m])
            relay_tx[m] = low(code_mask(dot_nt(maps[...], g_z)))
            relay(m).start()
            small_acc[0:code_rows, :] += dot_nn(relay_rx[m], g_z)

    def attn_back(m):
        attn_back_open(m)
        attn_back_heads(m, 0, pairs)
        attn_back_close(m)

    def fill_mask():
        patch = lax.broadcasted_iota(jnp.int32, (patches, 128), 0).astype(jnp.float32)
        for m in range(images):
            wide_grid = extent[m, 0] == 0
            length = jnp.where(wide_grid, float(GW), float(GH))
            line = jnp.floor((patch + 0.5) * jnp.where(wide_grid, 1.0 / GW, 1.0 / GH))
            inside = jnp.logical_and(
                line < extent[m, 1].astype(jnp.float32),
                patch - line * length < extent[m, 2].astype(jnp.float32),
            )
            mask_ref[m * patches : (m + 1) * patches, :] = wide(inside)

    def pack_small():
        maps_in = r["maps_in"][...]
        vectors = beneath([r["norm%d_in" % i][...] for i in range(4)])

        def lanes(count, start):
            row_no = lax.broadcasted_iota(jnp.int32, (count, 128), 0)
            return low(wide(lax.broadcasted_iota(jnp.int32, (count, 128), 1) == row_no + start))

        return low(
            dot_tn(maps_in, lanes(CODE_BITS, 0)) + dot_tn(vectors, lanes(4, CODE_BITS))
        )

    def take_small():
        small = wide(w_attn[:, 4 * features :]).T
        maps[...] = low(code_mask(small[:code_rows]))
        norms[0:4, :] = small[CODE_BITS : CODE_BITS + 4]

    def start_image(m):
        h_buf[m] = wide(x_ref[rows_of(m), :])

    def up_grads():
        for j in range(hidden // chunk):
            place = slice(j * chunk, (j + 1) * chunk)
            w_up[:, place] = low(dot_tn(c_s[...], slope_s[:, place]))

    def attn_grads():
        for j in range(3):
            place = slice(j * features, (j + 1) * features)
            w_attn[:, place] = low(dot_tn(a_s[...], qkv_s[:, place]))
        w_attn[:, 3 * features : 4 * features] = low(dot_tn(mixed_s[...], go_s[...]))
        small_grad = jnp.concatenate(
            [
                small_acc[0:CODE_BITS, :],
                small_acc[code_rows : code_rows + 4, :],
                jnp.zeros((128 - CODE_BITS - 4, features), jnp.float32),
            ],
            axis=0,
        )
        w_attn[:, 4 * features :] = low(small_grad.T)

    def fresh():
        fill_mask()
        stats[...] = jnp.zeros_like(stats)
        small_acc[...] = jnp.zeros_like(small_acc)

    def before_relay():
        @pl.when(is_dec)
        def _():
            stats[...] = jnp.zeros_like(stats)

    if not fused:
        copies = [
            pltpu.make_async_copy(r[name], weights[arr], r["own_sem"].at[arr])
            for arr, name in enumerate(("attn_all", "up_all", "down_all"))
        ]
        for copy in copies:
            copy.start()
        fresh()
        at.meet(False)
        for copy in copies:
            copy.wait()
        take_small()
        for m in range(images):
            start_image(m)
            attention(m)
            widen(m)
        before_relay()
        lax.fori_loop(0, images, forward, 0)
        for m in reversed(range(images)):
            open_back(m)
            mlp_back(m)
            attn_back(m)
            close_back(m)
        w_down[...] = low(dot_tn(act_s[:, :hidden], gm_s[...]))
        up_grads()
        attn_grads()
        for arr, name in enumerate(("g_attn", "g_up", "g_down")):
            copy = pltpu.make_async_copy(weights[arr], r[name], r["own_sem"].at[arr])
            copy.start()
            copy.wait()
        for m in range(images):
            pl.when(is_enc)(lambda: result(m).wait())
            relay(m).wait_send()
        return

    heights = (r["qkv_in"].shape[0], r["up_in"].shape[0], r["down_in"].shape[0])
    own_rows = [
        pl.ds(pl.multiple_of(at.here * height, height), height) for height in heights
    ]
    own_copies = [
        pltpu.make_async_copy(src, dst, r["own_sem"].at[i])
        for i, (src, dst) in enumerate(
            (
                (r["qkv_in"], w_attn.at[own_rows[ATTN], pl.ds(0, 3 * features)]),
                (r["out_in"], w_attn.at[own_rows[ATTN], pl.ds(3 * features, features)]),
                (r["up_in"], w_up.at[own_rows[UP]]),
                (r["down_in"], w_down.at[own_rows[DOWN]]),
            )
        )
    ]
    half = heights[DOWN] // 2
    arrays = [
        Blocks(w_attn, heights[ATTN], 0, heights[ATTN], False),
        Blocks(w_up, heights[UP], 0, heights[UP], False),
        Blocks(w_down, 2 * half, 0, half, False),
        Blocks(w_down, 2 * half, half, half, True),
    ]
    gather = Gather(at, arrays, r["g_send"], r["g_recv"])
    scatter = Scatter(
        at,
        arrays,
        (act_s, r["sib_u"], r["sib_d"], r["sib_r"]),
        (act_s, r["x_u"], r["x_d"], r["x_r"]),
        (slope_s, r["z_u"], r["z_d"], r["z_r"]),
        [r[name] for name in ("sib_ssem", "sib_rsem", "x_ssem", "x_rsem", "z_ssem", "z_rsem")],
    )
    total = Total(
        at,
        r["t_pair"],
        r["t_sib"],
        r["t_cross"],
        r["t_lines"],
        [r[name] for name in ("t_near_s", "t_near_r", "t_z_s", "t_z_r")],
    )
    for copy in own_copies:
        copy.start()
    at.meet(True)
    w_attn[own_rows[ATTN], 4 * features :] = pack_small()
    for copy in own_copies[:2]:
        copy.wait()
    gather.own(ATTN)
    fresh()
    for arr in (UP, DOWN, REST):
        scatter.clear(arr)
    for m in range(images):
        start_image(m)
    for copy in own_copies[2:]:
        copy.wait()
    gather.own(REST)
    gather.own_across(REST)
    gather.away(ATTN, 1)
    gather.own(UP)
    gather.away(ATTN, 2)
    gather.away(ATTN, 3)
    gather.away(UP, 1)
    gather.away(UP, 2)
    gather.crossed(ATTN)
    gather.turn(REST)
    gather.paired(ATTN)
    take_small()

    def third_up():
        gather.away(UP, 3)
        gather.own(DOWN)

    attention(0, [third_up, lambda: None, lambda: gather.away(REST, 1)])
    attention(1, [lambda: gather.away(DOWN, 1), lambda: None, lambda: gather.crossed(UP)])
    gather.away(DOWN, 2)
    gather.away(REST, 2)
    gather.paired(UP)
    widen(0)
    gather.away(DOWN, 3)
    widen(1)
    gather.away(REST, 3)
    gather.crossed(DOWN)
    gather.paired(REST)
    gather.paired(DOWN)
    before_relay()
    lax.fori_loop(0, images, forward, 0)
    total.sib_copy(stats).start()

    def backward(step, _):
        m = images - 1 - step
        open_back(m)
        mlp_back(m)

        @pl.when(jnp.logical_or(is_dec, m > 0))
        def _():
            attn_back(m)
            close_back(m)

        return 0

    lax.fori_loop(0, images, backward, 0)
    for arr in range(4):
        gather.sent(arr)
    total.cross_over(stats)

    def down_block(pair):
        span = 4 * half
        place = pl.ds(pl.multiple_of(pair * span, span), span)
        w_down[place, :] = low(dot_tn(act_s[:, place], gm_s[...]))
        scatter.sib_copy(DOWN, pair).start()
        scatter.sib_copy(REST, pair).start()

    def last_heads(part):
        pl.when(is_enc)(
            lambda: attn_back_heads(0, part * pairs // 3, (part + 1) * pairs // 3)
        )

    scatter.each_far(lambda way, dst_row: down_block(2 * dst_row + 1 - at.col))
    down_block(2 * at.row + 1 - at.col)
    scatter.x_stage(DOWN)
    scatter.each_far(lambda way, dst_row: down_block(2 * dst_row + at.col))
    down_block(2 * at.row + at.col)
    scatter.z_stage(REST, [3])
    pl.when(is_enc)(lambda: attn_back_open(0))
    total.along()
    up_grads()
    scatter.start_pairs(UP)
    scatter.z_stage(REST, [2])
    total.away(1)
    last_heads(0)
    scatter.z_stage(DOWN, [3])
    scatter.x_stage(UP)
    last_heads(1)
    last_heads(2)
    scatter.z_stage(UP, [3])

    @pl.when(is_enc)
    def _():
        attn_back_close(0)
        close_back(0)

    attn_grads()
    total.away(2)
    scatter.z_stage(UP, [2])
    scatter.start_pairs(ATTN)
    scatter.z_stage(REST, [1])
    scatter.clear(ATTN)
    scatter.x_stage(ATTN)
    total.away(3)
    scatter.z_stage(UP, [1])
    r["up_out"][...] = scatter.final(UP)
    scatter.z_stage(ATTN, [3])
    scatter.z_stage(DOWN, [2])
    scatter.z_stage(ATTN, [2])
    scatter.turn(REST)
    scatter.z_stage(DOWN, [1])
    scatter.z_stage(ATTN, [1])
    sums = total.lines[0]
    for i in range(1, rows):
        sums = sums + total.lines[i]
    sums = jnp.sum(sums, -1, keepdims=True)
    scale = 128.0 / (sums[3:4] * features)
    found = jnp.sqrt(sums * scale)
    row_no = lax.broadcasted_iota(jnp.int32, (8, 128), 0)
    lane_no = lax.broadcasted_iota(jnp.int32, (8, 128), 1)
    r["rms"][...] = row_sum(jnp.where(row_no == lane_no, found, 0.0))[:, :3]
    r["down_out"][:half, :] = scatter.final(DOWN)
    r["down_out"][half:, :] = scatter.final(REST)
    last = scatter.final(ATTN)
    r["qkv_out"][...] = last[:, : 3 * features]
    r["out_out"][...] = last[:, 3 * features : 4 * features]
    small = last[:, 4 * features :]
    small = jnp.concatenate(
        [small, jnp.zeros((128 - small.shape[0], 128), jnp.float32)], axis=0
    ).T
    for i in range(CODE_BITS):
        r["maps_out"][i] = small[i : i + 1, : heights[ATTN]]
    for i in range(4):
        r["norm%d_out" % i][...] = small[CODE_BITS + i : CODE_BITS + i + 1, : heights[ATTN]]
    for m in range(images):
        pl.when(is_enc)(lambda: result(m).wait())
        relay(m).wait_send()
    for arr in range(4):
        scatter.sent(arr)
    total.sent(stats)


def run_blocks(fused, operands, x, extent, rows):
    images, patches, features = x.shape
    total = images * patches
    hidden = 4 * features
    attn_width = 4 * features + 128
    code_rows = -(-CODE_BITS // 16) * 16
    bf16, f32 = jnp.bfloat16, jnp.float32
    any_spec = pl.BlockSpec(memory_space=pl.ANY)
    vmem_spec = pl.BlockSpec(memory_space=pltpu.VMEM)
    dma = pltpu.SemaphoreType.DMA
    ins = dict(operands, x=x.reshape(total, features), extent=extent)
    outs = {"seg_out": ((total, features), f32)}
    full = {"a": (features, attn_width), "u": (features, hidden), "d": (hidden, features)}
    buffers = {
        "w_attn": (full["a"], bf16), "w_up": (full["u"], bf16), "w_down": (full["d"], bf16),
        "mask": ((total, 128), f32),
        "norms": ((8, features), f32), "maps": ((code_rows, features), bf16),
        "h": ((images, patches, features), f32),
        "xhat1": ((total, features), bf16), "rstd1": ((total, 1), f32),
        "xhat2": ((total, features), bf16), "rstd2": ((total, 1), f32),
        "a": ((total, features), bf16), "qkv": ((total, 3 * features), bf16),
        "mixed": ((total, features), bf16), "c": ((total, features), bf16),
        "act": ((total, attn_width), bf16), "slope": ((total, attn_width), bf16),
        "lse_pack": ((total, 128), bf16), "bias_pack": ((total, 128), bf16),
        "inner_pack": ((patches, 128), bf16),
        "gm": ((total, features), bf16), "go": ((total, features), bf16),
        "gmix": ((patches, features), bf16),
        "u": ((images, code_rows, patches), f32), "small_acc": ((code_rows + 8, features), f32),
        "relay_tx": ((images, code_rows, patches), bf16),
        "relay_rx": ((images, code_rows, patches), bf16),
    }
    sems = {"relay_s": (images,), "relay_r": (images,), "out_sem": (images,)}
    in_vmem = ["x", "maps_in", *("norm%d_in" % i for i in range(4))]
    smem_spec = pl.BlockSpec(memory_space=pltpu.SMEM)
    if fused:
        outs["rms"] = ((1, 3), f32)
        shards = {
            "a": (operands["qkv_in"].shape[0], attn_width),
            "u": operands["up_in"].shape,
            "d": operands["down_in"].shape,
        }
        outs["qkv_out"] = (operands["qkv_in"].shape, f32)
        outs["out_out"] = (operands["out_in"].shape, f32)
        outs["up_out"] = (shards["u"], f32)
        outs["down_out"] = (shards["d"], f32)
        outs["maps_out"] = ((CODE_BITS, 1, shards["a"][0]), f32)
        for i in range(4):
            outs["norm%d_out" % i] = ((1, shards["a"][0]), f32)
        buffers["stats"] = ((8, 128), f32)
        half = (shards["d"][0] // 2, features)
        for name, shape, split in (("u", shards["u"], 0), ("d", half, 0), ("r", half, 1)):
            buffers["sib_" + name] = ((2 * rows,) + shape, bf16)
            buffers["x_" + name] = ((1 if split else rows,) + shape, bf16)
            buffers["z_" + name] = (((1 + split) * (rows + 1),) + shape, bf16)
        for name in ("t_pair", "t_sib", "t_cross"):
            buffers[name] = ((8, 128), f32)
        buffers["t_lines"] = ((rows, 8, 128), f32)
        sems.update(
            own_sem=(4,), g_send=(4, 8 * rows), g_recv=(4, 4 * rows),
            sib_ssem=(4, 2 * rows), sib_rsem=(4, 2 * rows), x_ssem=(4, rows), x_rsem=(4, rows),
            z_ssem=(4, 2 * rows), z_rsem=(4, 2 * rows + 2),
            t_near_s=(2,), t_near_r=(2,), t_z_s=(2, rows), t_z_r=(rows,),
        )
    else:
        outs["g_attn"] = (full["a"], bf16)
        outs["g_up"] = (full["u"], bf16)
        outs["g_down"] = (full["d"], bf16)
        outs["stats"] = ((8, 128), f32)
        sems["own_sem"] = (3,)
    names = [*ins, *outs, *buffers, *sems]
    out_any = ("seg_out", "g_attn", "g_up", "g_down")
    found = pl.pallas_call(
        partial(blocks_body, fused, rows, names),
        out_shape=tuple(jax.ShapeDtypeStruct(s, t) for s, t in outs.values()),
        in_specs=[
            vmem_spec if n in in_vmem else smem_spec if n == "extent" else any_spec for n in ins
        ],
        out_specs=tuple(any_spec if n in out_any else vmem_spec for n in outs),
        scratch_shapes=[pltpu.VMEM(s, t) for s, t in buffers.values()]
        + [dma(s) for s in sems.values()],
        compiler_params=pltpu.CompilerParams(
            collective_id=1, has_side_effects=True, vmem_limit_bytes=VMEM_BYTES
        ),
        name="both_blocks",
    )(*ins.values())
    return dict(zip(outs, found))


def hand_over_body(count, *refs):
    steps = [refs[i * count : (i + 1) * count] for i in range(3)]
    sems = refs[3 * count :]
    parts = []
    for i in range(count):
        height = steps[0][i].shape[0]
        cuts = 4 if height % 32 == 0 else 1
        for j in range(cuts):
            parts.append([step[i].at[pl.ds(j * height // cuts, height // cuts)] for step in steps])
    copies = [
        (
            pltpu.make_async_copy(src, middle, sems[0].at[i]),
            pltpu.make_async_copy(middle, dst, sems[1].at[i]),
        )
        for i, (src, dst, middle) in enumerate(parts)
    ]
    for first, _ in copies:
        first.start()
    for first, second in copies:
        first.wait()
        second.start()
    for _, second in copies:
        second.wait()


def hand_over(arrays):
    any_spec = pl.BlockSpec(memory_space=pl.ANY)
    return pl.pallas_call(
        partial(hand_over_body, len(arrays)),
        out_shape=tuple(jax.ShapeDtypeStruct(v.shape, v.dtype) for v in arrays),
        in_specs=[any_spec] * len(arrays),
        out_specs=(any_spec,) * len(arrays),
        scratch_shapes=[pltpu.VMEM(v.shape, v.dtype) for v in arrays]
        + [pltpu.SemaphoreType.DMA((4 * len(arrays),))] * 2,
        name="hand_over",
    )(*arrays)


def on_device(
    segment_input,
    image_extent,
    norm1_gain,
    norm1_bias,
    norm2_gain,
    norm2_bias,
    qkv_weight,
    out_weight,
    up_weight,
    down_weight,
    code_maps,
):
    _, images, patches, features = segment_input.shape
    qkv_width = qkv_weight.shape[2]
    count = lax.axis_size("dp")
    x = segment_input[0]
    if qkv_weight.shape[1] % 16 == 0 and count % 4 == 0:
        operands = {
            "qkv_in": qkv_weight[0],
            "out_in": out_weight[0],
            "maps_in": code_maps[0].T,
            "norm0_in": norm1_gain,
            "norm1_in": norm1_bias,
            "norm2_in": norm2_gain,
            "norm3_in": norm2_bias,
            "up_in": up_weight[0],
            "down_in": down_weight[0],
        }
        found = run_blocks(True, operands, x, image_extent, count // 4)
        names = ["seg_out", "rms", *("norm%d_out" % i for i in range(4))]
        names += ["qkv_out", "out_out", "up_out", "down_out", "maps_out"]
        results = list(hand_over([found[name] for name in names]))
        results[-1] = jnp.transpose(results[-1][:, 0])
    else:
        small = jnp.concatenate(
            [code_maps[0]]
            + [v[0][:, None] for v in (norm1_gain, norm1_bias, norm2_gain, norm2_bias)],
            axis=1,
        )
        small = jnp.pad(small, ((0, 0), (0, 128 - small.shape[1])))
        attn = jnp.concatenate([qkv_weight[0], out_weight[0], small], axis=1)
        operands = {
            name: lax.all_gather(shard, "dp", axis=0, tiled=True)
            for name, shard in (
                ("attn_all", attn),
                ("up_all", up_weight[0]),
                ("down_all", down_weight[0]),
            )
        }
        found = run_blocks(False, operands, x, image_extent, 1)
        attn_shard, up_shard, down_shard = [
            lax.psum_scatter(
                found[name].astype(jnp.float32), "dp", scatter_dimension=0, tiled=True
            )
            for name in ("g_attn", "g_up", "g_down")
        ]
        stats = lax.psum(found["stats"], "dp")
        rms_stats = jnp.sqrt(jnp.sum(stats[:3], 1) / (stats[3, 0] * features))[None]
        small_shard = attn_shard[:, qkv_width + features :]
        results = [
            found["seg_out"],
            rms_stats,
            *(small_shard[:, CODE_BITS + i][None] for i in range(4)),
            attn_shard[:, :qkv_width],
            attn_shard[:, qkv_width : qkv_width + features],
            up_shard,
            down_shard,
            small_shard[:, :CODE_BITS],
        ]
    return (
        results[0].reshape(segment_input.shape),
        *results[1:6],
        *(v[None] for v in results[6:]),
    )


def solution(mesh):
    return jax.shard_map(
        on_device,
        mesh=mesh,
        in_specs=(
            P("segment", "dp", None, None),
            P("dp", None),
            P("segment", "dp"),
            P("segment", "dp"),
            P("segment", "dp"),
            P("segment", "dp"),
            P("segment", "dp", None),
            P("segment", "dp", None),
            P("segment", "dp", None),
            P("segment", "dp", None),
            P("segment", "dp", None),
        ),
        out_specs=(
            P("segment", "dp", None, None),
            P("segment", None),
            P("segment", "dp"),
            P("segment", "dp"),
            P("segment", "dp"),
            P("segment", "dp"),
            P("segment", "dp", None),
            P("segment", "dp", None),
            P("segment", "dp", None),
            P("segment", "dp", None),
            P("segment", "dp", None),
        ),
        check_vma=False,
    )
```
